32 devices in a mesh: fsdp: 8 (over z, core), dp: 4 (over y, x).
Axes of the slice: x: 2, y: 2, z: 4, core: 2. Of those that a mesh axis runs over, the one named last changes fastest.
Arguments:
- latents: bfloat16 [8, 60, 256, 320], P('fsdp', 'dp'), may hold values from -6 to 6
- target_noise: bfloat16 [8, 60, 256, 320], P('fsdp', 'dp'), may hold values from -6 to 6
- counts: int32 [8, 4], P('fsdp'), may hold values from 1 to 15, 32 in all within a row
- timesteps: int32 [8, 60], P('fsdp', 'dp'), may hold values from 0 to 999
- conv_master: float32 [2880, 320], P('fsdp'), may hold values from -0.109375 to 0.109375
- temb_master: float32 [1280, 320], P('fsdp'), may hold values from -0.15625 to 0.15625
Outputs:
- prediction: bfloat16 [8, 60, 256, 320], P('fsdp', 'dp')
- conv_grad: float32 [2880, 320], P('fsdp')
- temb_grad: float32 [1280, 320], P('fsdp')
The draws below stay inside these ranges and needn't reach their ends.
Inputs may be any that keep to these rules, and one draw needn't show every extreme that they name: In each row (one slide group) the 4 owners' live counts sum to exactly 32; 15 is reached in every row; an owner's live tiles are its first slots.
All inputs are finite; a program needn't handle non-finite values.
Results may differ from the reference program's by a relative error of at most 0.0085.
Values may be sent and summed in bfloat16 or wider, within the bound.
No kernel may reach another device: no remote copies, remote signals or barrier semaphores. Data moves between devices by JAX's collectives and lax.ppermute only.
A program may use at most 128 MiB of HBM per device.

```python
import math
import jax
import jax.numpy as jnp
import numpy as np
from jax import lax

C = 320
EMB = 1280
GROUPS = 32
SIDE = 16
BAL = 8
PIX = 256
OWN = 15
N_FSDP = 8
N_DP = 4


def set_ends(result, rng, smallest, top_value):
    longest = result.shape.index(max(result.shape))
    spots = []
    for shift in (0, 1):
        where = [jax.random.randint(jax.random.fold_in(rng, axis), (), 0, length) for axis, length in enumerate(result.shape)]
        where[longest] = (where[longest] + shift) % result.shape[longest]
        spots.append(tuple(where))
    return result.at[spots[0]].set(smallest).at[spots[1]].set(top_value)


def block_scale(rng, extent, shards, smallest, top_value):
    def one(axis_at, shards_of):
        draws = jax.random.uniform(jax.random.fold_in(jax.random.fold_in(rng, 6), axis_at), (shards_of,), jnp.float32, smallest / len(shards), top_value / len(shards))
        return jnp.repeat(jnp.exp(draws), extent[axis_at] // shards_of).reshape((-1,) + (1,) * (len(extent) - axis_at - 1))

    level = one(*shards[0])
    for cut in shards[1:]:
        level = level * one(*cut)
    return level


def profile(count, total, most, skew):
    weights = [(1 << 20) // math.isqrt(grade ** skew) + 1 for grade in range(2, count + 1)]
    rest, given = total - most - (count - 1), [1] * (count - 1)
    while rest > 0:
        candidates = [i for i in range(count - 1) if given[i] < most]
        pool, left = sum([weights[i] for i in candidates]), rest
        for i in candidates:
            addition = min(most - given[i], max(1, left * weights[i] // pool), rest)
            given[i] = given[i] + addition
            rest = rest - addition
    return np.array([most] + given)


def ragged(key, amount, total, most, skew):
    if amount == 2:
        one = jax.random.randint(key, (), max(1, total - most), min(most, total - 1) + 1)
        return jnp.stack([one, total - one])
    lengths = jnp.asarray(profile(amount, total, most, skew), jnp.int32)
    couples = (amount - 1) // 2
    giver, taker = lengths[1:1 + 2 * couples:2], lengths[2:2 + 2 * couples:2]
    margin = jnp.minimum(giver - 1, most - taker)
    moved = jax.random.randint(jax.random.fold_in(key, 1), (couples,), 0, 1 << 20) % (margin + 1)
    lengths = lengths.at[1:1 + 2 * couples:2].set(giver - moved).at[2:2 + 2 * couples:2].set(taker + moved)
    return lengths[jax.random.permutation(jax.random.fold_in(key, 2), amount)]


def bell_draw(stream_key, shape, width, most, split=(), held_as=jnp.bfloat16):
    drawn = width * jax.random.normal(stream_key, shape, jnp.float32)
    if split:
        drawn = drawn * block_scale(stream_key, shape, split, -0.22, 0.18)
    return jnp.clip(drawn, -most, most).astype(held_as)


def setup_inputs(seed: int = 0) -> dict:
    seeds = jax.random.split(jax.random.key(seed), 7)
    latents = bell_draw(seeds[0], (N_FSDP, N_DP * OWN, PIX, C), 1.0, 6.0, ((0, 8), (1, 4)))
    target_noise = bell_draw(seeds[1], (N_FSDP, N_DP * OWN, PIX, C), 1.0, 6.0, ((0, 8), (1, 4)))
    counts = jax.vmap(lambda own: ragged(own, N_DP, N_DP * BAL, OWN, 2))(jax.random.split(seeds[2], N_FSDP)).reshape((N_FSDP, N_DP)).astype(jnp.int32)
    timesteps = set_ends(jax.random.randint(seeds[3], (N_FSDP, N_DP * OWN), 0, 1000), jax.random.fold_in(seeds[3], 1), 0, 999).astype(jnp.int32)
    conv_master = bell_draw(seeds[4], (9 * C, C), (9 * C) ** -0.5, 0.109375, ((0, 8),), jnp.float32)
    temb_master = bell_draw(seeds[5], (EMB, C), EMB ** -0.5, 0.15625, ((0, 8),), jnp.float32)
    return {"latents": latents, "target_noise": target_noise, "counts": counts, "timesteps": timesteps, "conv_master": conv_master, "temb_master": temb_master}


def time_features(timestep):
    half_width = EMB // 2
    frequency = jnp.exp(-math.log(10000.0) * jnp.arange(half_width, dtype=jnp.float32) / half_width)
    angles = timestep.astype(jnp.float32) * frequency
    return jax.nn.silu(jnp.concatenate([jnp.cos(angles), jnp.sin(angles)])).astype(jnp.bfloat16)

def normed(latent_tile):
    grouped = latent_tile.astype(jnp.float32).reshape(PIX, GROUPS, C // GROUPS)
    group_mean = lax.optimization_barrier(jnp.mean(grouped, axis=(0, 2), keepdims=True))
    centred = grouped - group_mean
    variance = lax.optimization_barrier(jnp.mean(centred * centred, axis=(0, 2), keepdims=True))
    return jax.nn.silu(centred / jnp.sqrt(variance + 1e-05)).reshape(PIX, C).astype(jnp.bfloat16)

def unfold(values):
    spatial = values.reshape(SIDE, SIDE, C)
    padded = jnp.pad(spatial, ((1, 1), (1, 1), (0, 0)))
    shifted = [padded[a:a + SIDE, b:b + SIDE] for a in range(3) for b in range(3)]
    return jnp.concatenate(shifted, axis=-1).reshape(PIX, 9 * C)

def reference(latents, target_noise, counts, timesteps, conv_master, temb_master):
    conv_weight = conv_master.astype(jnp.bfloat16)
    time_weight = temb_master.astype(jnp.bfloat16)
    flat_counts = counts.reshape(-1).astype(jnp.int32)
    count_ends = jnp.cumsum(flat_counts).astype(jnp.int32)
    count_starts = count_ends - flat_counts
    live_total = N_FSDP * N_DP * BAL
    wanted = jnp.arange(live_total, dtype=jnp.int32)
    owner_index = lax.optimization_barrier(jnp.sum((count_ends[None, :] <= wanted[:, None]).astype(jnp.int32), axis=1))
    owners_all = jnp.arange(flat_counts.shape[0], dtype=jnp.int32)
    owner_start = lax.optimization_barrier(jnp.sum(jnp.where(owner_index[:, None] == owners_all[None, :], count_starts[None, :], 0), axis=1))
    group_index = (owner_index // N_DP).astype(jnp.int32)
    slot_index = (owner_index % N_DP * OWN + wanted - owner_start).astype(jnp.int32)
    zero_index = jnp.zeros((), jnp.int32)

    def visit(state_now, indices):
        predictions, conv_grad, temb_grad = state_now
        group_at, slot_at = indices
        latent_tile = lax.dynamic_slice(latents, (group_at, slot_at, zero_index, zero_index), (1, 1, PIX, C)).reshape(PIX, C)
        target_tile = lax.dynamic_slice(target_noise, (group_at, slot_at, zero_index, zero_index), (1, 1, PIX, C)).reshape(PIX, C)
        timestep = lax.dynamic_slice(timesteps, (group_at, slot_at), (1, 1)).reshape(())
        time_act = time_features(timestep)
        columns = unfold(normed(latent_tile))
        time_bias = jnp.dot(time_act[None, :], time_weight, preferred_element_type=jnp.float32)[0]
        pred32 = latent_tile.astype(jnp.float32) + jnp.dot(columns, conv_weight, preferred_element_type=jnp.float32) + time_bias[None, :]
        error_grad = ((pred32 - target_tile.astype(jnp.float32)) / PIX).astype(jnp.bfloat16)
        conv_grad = conv_grad + lax.dot_general(columns, error_grad, (((0,), (0,)), ((), ())), preferred_element_type=jnp.float32)
        temb_grad = temb_grad + jnp.outer(time_act.astype(jnp.float32), lax.optimization_barrier(jnp.sum(error_grad.astype(jnp.float32), axis=0)))
        predictions = lax.dynamic_update_slice(predictions, pred32.astype(jnp.bfloat16).reshape(1, 1, PIX, C), (group_at, slot_at, zero_index, zero_index))
        return ((predictions, conv_grad, temb_grad), None)
    start_state = (jnp.zeros(latents.shape, jnp.bfloat16), jnp.zeros((9 * C, C), jnp.float32), jnp.zeros((EMB, C), jnp.float32))
    final_state, unused = lax.scan(visit, start_state, (group_index, slot_index))
    return (final_state[0], final_state[1], final_state[2])
```

```python
import functools
import math

import jax
import jax.numpy as jnp
from jax import lax
from jax.experimental import pallas as pl
from jax.experimental.pallas import tpu as pltpu
from jax.sharding import PartitionSpec as P

GROUPS = 32
SIDE = 16
LANES = 128

bf16 = jnp.bfloat16
f32 = jnp.float32


def tiles_per_step(number):
    return max(size for size in range(1, 6) if number % size == 0)


def norm_kernel(group_width, same_ref, tiles_ref, out_ref):
    same_group = same_ref[...]
    number, channels, pixels = tiles_ref.shape
    scale = 1.0 / (group_width * pixels)
    lane = lax.broadcasted_iota(jnp.int32, (channels, LANES), 1)

    def group_mean(row_sums):
        high = row_sums.astype(bf16).astype(f32)
        middle = (row_sums - high).astype(bf16).astype(f32)
        low = row_sums - high - middle
        terms = jnp.where(
            lane == 0, high, jnp.where(lane == 1, middle, jnp.where(lane == 2, low, 0.0))
        ).astype(bf16)
        summed = jnp.dot(same_group, terms, preferred_element_type=f32)
        return jnp.sum(summed, axis=1, keepdims=True) * scale

    for at in range(number):
        values = tiles_ref[at].astype(f32)
        centred = values - group_mean(jnp.sum(values, axis=1, keepdims=True))
        variance = group_mean(jnp.sum(centred * centred, axis=1, keepdims=True))
        scaled = centred * lax.rsqrt(variance + 1e-05)
        out_ref[at] = (scaled / (1.0 + jnp.exp(-scaled))).astype(bf16)


def group_norm(tiles):
    number, channels, pixels = tiles.shape
    step = tiles_per_step(number)
    group_width = channels // GROUPS
    group = jnp.arange(channels, dtype=jnp.int32) // group_width
    same_group = (group[:, None] == group[None, :]).astype(bf16)
    block = pl.BlockSpec((step, channels, pixels), lambda i: (i, 0, 0))
    return pl.pallas_call(
        functools.partial(norm_kernel, group_width),
        grid=(number // step,),
        in_specs=[pl.BlockSpec((channels, channels), lambda i: (0, 0)), block],
        out_specs=block,
        out_shape=jax.ShapeDtypeStruct(tiles.shape, bf16),
        compiler_params=pltpu.CompilerParams(vmem_limit_bytes=32 * 2**20),
        cost_estimate=pl.CostEstimate(
            flops=20 * tiles.size, bytes_accessed=4 * tiles.size, transcendentals=tiles.size
        ),
        name="group_norm",
    )(same_group, tiles)


def write_columns(values, columns_ref, at):
    channels, pixels = values.shape
    cell = lax.broadcasted_iota(jnp.int32, (channels, pixels), 1)
    column = cell % SIDE
    wide = values.astype(f32)
    for b in range(3):
        if b == 1:
            moved = wide
        else:
            moved = pltpu.roll(wide, (1 - b) % pixels, 1)
            moved = jnp.where(column == (0 if b == 0 else SIDE - 1), 0.0, moved)
        for a in range(3):
            if a == 1:
                shifted = moved
            else:
                shifted = pltpu.roll(moved, ((1 - a) * SIDE) % pixels, 1)
                outside = (cell < SIDE) if a == 0 else (cell >= pixels - SIDE)
                shifted = jnp.where(outside, 0.0, shifted)
            tap = 3 * a + b
            columns_ref[
                tap * channels : (tap + 1) * channels, at * pixels : (at + 1) * pixels
            ] = shifted.astype(values.dtype)


def conv_kernel(
    steps,
    count_ref,
    weight_ref,
    normed_ref,
    tiles_ref,
    target_ref,
    bias_ref,
    predicted_ref,
    sums_ref,
    grad_ref,
    weight,
    columns,
    total,
):
    i = pl.program_id(0)
    shards, outs, rows = weight_ref.shape
    step, channels, pixels = normed_ref.shape
    count = count_ref[0]

    @pl.when(i == 0)
    def _():
        for f in range(shards):
            weight[:, f * rows : (f + 1) * rows] = weight_ref[f]
        total[...] = jnp.zeros_like(total)
        sums_ref[...] = jnp.zeros_like(sums_ref)

    @pl.when(i * step < count)
    def _():
        for t in range(step):
            write_columns(normed_ref[t], columns, t)
        conv = jnp.dot(weight[...], columns[...], preferred_element_type=f32)
        lane = lax.broadcasted_iota(jnp.int32, (outs, LANES), 1)
        errors = []
        sums = sums_ref[...]
        for t in range(step):
            slot = i * step + t
            live = slot < count
            bias = jnp.sum(jnp.where(lane == slot, bias_ref[...], 0.0), axis=1, keepdims=True)
            pred32 = tiles_ref[t].astype(f32) + conv[:, t * pixels : (t + 1) * pixels] + bias
            predicted_ref[t] = jnp.where(live, pred32, 0.0).astype(bf16)
            error = jnp.where(
                live, (pred32 - target_ref[t].astype(f32)) * (1.0 / pixels), 0.0
            ).astype(bf16)
            error_sum = jnp.sum(error.astype(f32), axis=1, keepdims=True)
            sums = jnp.where(lane == slot, error_sum, sums)
            errors.append(error)
        sums_ref[...] = sums
        total[...] += lax.dot_general(
            jnp.concatenate(errors, axis=1),
            columns[...],
            (((1,), (1,)), ((), ())),
            preferred_element_type=f32,
        )

    @pl.when(i * step >= count)
    def _():
        predicted_ref[...] = jnp.zeros_like(predicted_ref)

    @pl.when(i == steps - 1)
    def _():
        for f in range(shards):
            grad_ref[f] = total[:, f * rows : (f + 1) * rows].astype(bf16)


def conv_both(count, weight, normed, tiles, targets, bias):
    number, channels, pixels = normed.shape
    shards, outs, rows = weight.shape
    depth = shards * rows
    step = tiles_per_step(number)
    steps = number // step

    def whole(shape):
        return pl.BlockSpec(shape, lambda i, c: (0,) * len(shape))

    block = pl.BlockSpec((step, channels, pixels), lambda i, c: (i, 0, 0))
    return pl.pallas_call(
        functools.partial(conv_kernel, steps),
        grid_spec=pltpu.PrefetchScalarGridSpec(
            num_scalar_prefetch=1,
            grid=(steps,),
            in_specs=[whole(weight.shape), block, block, block, whole(bias.shape)],
            out_specs=[block, whole((outs, LANES)), whole(weight.shape)],
            scratch_shapes=[
                pltpu.VMEM((outs, depth), bf16),
                pltpu.VMEM((depth, step * pixels), bf16),
                pltpu.VMEM((outs, depth), f32),
            ],
        ),
        out_shape=[
            jax.ShapeDtypeStruct(tiles.shape, bf16),
            jax.ShapeDtypeStruct((outs, LANES), f32),
            jax.ShapeDtypeStruct(weight.shape, bf16),
        ],
        compiler_params=pltpu.CompilerParams(vmem_limit_bytes=56 * 2**20),
        cost_estimate=pl.CostEstimate(
            flops=4 * number * pixels * depth * outs, bytes_accessed=8 * tiles.size, transcendentals=0
        ),
        name="conv_both",
    )(count, weight, normed, tiles, targets, bias)


def swap(values, axis, mask):
    pairs = [(i, i ^ mask) for i in range(lax.axis_size(axis))]
    return lax.ppermute(values, axis, pairs)


def bit_groups(low, high, width=2):
    return [(at, min(width, high - at)) for at in range(low, high, width)]


def block_at(values, index):
    return lax.dynamic_index_in_dim(values, index, 0, keepdims=False)


def scatter_bits(values, axis, low, width):
    mine = (lax.axis_index(axis) >> low) & ((1 << width) - 1)
    got = [
        swap(block_at(values, mine ^ other), axis, other << low) for other in range(1, 1 << width)
    ]
    total = block_at(values, mine).astype(f32)
    for part in got:
        total = total + part.astype(f32)
    return total.astype(values.dtype)


def gather_bits(values, axis, low, width):
    mine = (lax.axis_index(axis) >> low) & ((1 << width) - 1)
    got = [values] + [swap(values, axis, other << low) for other in range(1, 1 << width)]
    if width == 1:
        first = mine == 0
        return jnp.stack([jnp.where(first, got[0], got[1]), jnp.where(first, got[1], got[0])])
    stacked = jnp.stack(got)
    return jnp.stack([block_at(stacked, mine ^ s) for s in range(1 << width)])


def bits_of(axis):
    return (lax.axis_size(axis) - 1).bit_length()


def gather_axis(values, axis):
    shape = values.shape
    values = values[None]
    for low in range(bits_of(axis)):
        values = gather_bits(values, axis, low, 1)
        values = values.reshape((-1,) + shape)
    return values


def time_rows(timesteps, emb, first, rows):
    half_width = emb // 2
    index = first + jnp.arange(rows, dtype=jnp.int32)
    place = (index % half_width).astype(f32)
    frequency = jnp.exp(-math.log(10000.0) * place / half_width)
    angles = timesteps.astype(f32)[:, None] * frequency[None, :]
    waves = jnp.where(index[None, :] < half_width, jnp.cos(angles), jnp.sin(angles))
    return jax.nn.silu(waves).astype(bf16)


def per_device(latents, target_noise, counts, timesteps, conv_master, temb_master):
    tiles = jnp.swapaxes(latents[0], 1, 2)
    targets = jnp.swapaxes(target_noise[0], 1, 2)
    number, channels, pixels = tiles.shape
    shards, peers = lax.axis_size("fsdp"), lax.axis_size("dp")
    shard_bits, peer_bits = bits_of("fsdp"), bits_of("dp")
    my_shard, my_peer = lax.axis_index("fsdp"), lax.axis_index("dp")
    rows, outs = conv_master.shape
    time_depth = temb_master.shape[0]
    emb = time_depth * shards
    count = lax.dynamic_slice(counts[0], (my_peer,), (1,))

    weight = lax.all_gather(conv_master.T.astype(bf16), "fsdp", axis=0, tiled=False)
    normed = group_norm(tiles)

    column_times = gather_axis(timesteps[0], "fsdp")
    column_rows = time_rows(column_times.reshape(-1), emb, my_shard * time_depth, time_depth)
    bias = jnp.dot(column_rows, temb_master.astype(bf16), preferred_element_type=f32)
    bias = bias.reshape((shards, number, outs))
    for low in range(shard_bits):
        bias = bias.reshape((-1, 2, number, outs)).swapaxes(0, 1)
        bias = scatter_bits(bias, "fsdp", low, 1)
    bias = jnp.pad(bias.reshape(number, outs).T, ((0, 0), (0, LANES - number)))

    predicted, error_sums, grad = conv_both(count, weight, normed, tiles, targets, bias)

    all_times = gather_axis(column_times, "dp")
    sums = error_sums[:, :number].T.astype(bf16)
    all_sums = gather_axis(gather_axis(sums, "dp"), "fsdp")
    all_times = all_times.swapaxes(0, 1)
    all_rows = time_rows(all_times.reshape(-1), emb, my_shard * time_depth, time_depth)
    temb_grad = lax.dot_general(
        all_rows,
        all_sums.reshape(-1, outs),
        (((0,), (0,)), ((), ())),
        preferred_element_type=f32,
    )

    grad = scatter_bits(grad.reshape((shards // 2, 2, outs, rows)).swapaxes(0, 1), "fsdp", 0, 1)
    grad = grad.reshape((shards // 2, peers, outs // peers, rows)).swapaxes(0, 1)
    for low, width in bit_groups(0, peer_bits):
        if width < peer_bits:
            grad = grad.reshape((-1, 1 << width) + grad.shape[1:]).swapaxes(0, 1)
        grad = scatter_bits(grad, "dp", low, width)
    grad = grad.reshape((shards // 2, outs // peers, rows))
    for low, width in bit_groups(1, shard_bits):
        grad = grad.reshape((-1, 1 << width, outs // peers, rows)).swapaxes(0, 1)
        grad = scatter_bits(grad, "fsdp", low, width)
    grad = grad.reshape((1, outs // peers, rows))
    for low, width in bit_groups(0, peer_bits):
        grad = gather_bits(grad, "dp", low, width)
        grad = grad.reshape((-1, outs // peers, rows))
    conv_grad = grad.reshape(outs, rows).T.astype(f32)

    return (jnp.swapaxes(predicted, 1, 2)[None], conv_grad, temb_grad)


def solution(mesh):
    placed = (
        P("fsdp", "dp", None, None),
        P("fsdp", "dp", None, None),
        P("fsdp", None),
        P("fsdp", "dp"),
        P("fsdp", None),
        P("fsdp", None),
    )
    return jax.shard_map(
        per_device,
        mesh=mesh,
        in_specs=placed,
        out_specs=(P("fsdp", "dp", None, None), P("fsdp", None), P("fsdp", None)),
        check_vma=False,
    )
```

```python
import functools
import math

import jax
import jax.numpy as jnp
from jax import lax
from jax.experimental import pallas as pl
from jax.experimental.pallas import tpu as pltpu
from jax.sharding import PartitionSpec as P

GROUPS = 32
SIDE = 16
LANES = 128

bf16 = jnp.bfloat16
f32 = jnp.float32


def tiles_per_step(number):
    return max(size for size in range(1, 6) if number % size == 0)


def norm_kernel(group_width, same_ref, tiles_ref, out_ref):
    same_group = same_ref[...]
    number, channels, pixels = tiles_ref.shape
    scale = 1.0 / (group_width * pixels)
    lane = lax.broadcasted_iota(jnp.int32, (channels, LANES), 1)

    def group_mean(row_sums):
        high = row_sums.astype(bf16).astype(f32)
        middle = (row_sums - high).astype(bf16).astype(f32)
        low = row_sums - high - middle
        terms = jnp.where(
            lane == 0, high, jnp.where(lane == 1, middle, jnp.where(lane == 2, low, 0.0))
        ).astype(bf16)
        summed = jnp.dot(same_group, terms, preferred_element_type=f32)
        return jnp.sum(summed, axis=1, keepdims=True) * scale

    for at in range(number):
        values = tiles_ref[at].astype(f32)
        centred = values - group_mean(jnp.sum(values, axis=1, keepdims=True))
        variance = group_mean(jnp.sum(centred * centred, axis=1, keepdims=True))
        scaled = centred * lax.rsqrt(variance + 1e-05)
        out_ref[at] = (scaled / (1.0 + jnp.exp(-scaled))).astype(bf16)


def group_norm(tiles):
    number, channels, pixels = tiles.shape
    step = tiles_per_step(number)
    group_width = channels // GROUPS
    group = jnp.arange(channels, dtype=jnp.int32) // group_width
    same_group = (group[:, None] == group[None, :]).astype(bf16)
    block = pl.BlockSpec((step, channels, pixels), lambda i: (i, 0, 0))
    return pl.pallas_call(
        functools.partial(norm_kernel, group_width),
        grid=(number // step,),
        in_specs=[pl.BlockSpec((channels, channels), lambda i: (0, 0)), block],
        out_specs=block,
        out_shape=jax.ShapeDtypeStruct(tiles.shape, bf16),
        compiler_params=pltpu.CompilerParams(vmem_limit_bytes=32 * 2**20),
        cost_estimate=pl.CostEstimate(
            flops=20 * tiles.size, bytes_accessed=4 * tiles.size, transcendentals=tiles.size
        ),
        name="group_norm",
    )(same_group, tiles)


def write_columns(values, columns_ref, at):
    channels, pixels = values.shape
    cell = lax.broadcasted_iota(jnp.int32, (channels, pixels), 1)
    column = cell % SIDE
    wide = values.astype(f32)
    for b in range(3):
        if b == 1:
            moved = wide
        else:
            moved = pltpu.roll(wide, (1 - b) % pixels, 1)
            moved = jnp.where(column == (0 if b == 0 else SIDE - 1), 0.0, moved)
        for a in range(3):
            if a == 1:
                shifted = moved
            else:
                shifted = pltpu.roll(moved, ((1 - a) * SIDE) % pixels, 1)
                outside = (cell < SIDE) if a == 0 else (cell >= pixels - SIDE)
                shifted = jnp.where(outside, 0.0, shifted)
            tap = 3 * a + b
            columns_ref[
                tap * channels : (tap + 1) * channels, at * pixels : (at + 1) * pixels
            ] = shifted.astype(values.dtype)


def conv_kernel(
    steps,
    where_ref,
    own_ref,
    other_ref,
    features_ref,
    normed_ref,
    tiles_ref,
    target_ref,
    predicted_ref,
    keep_ref,
    send_ref,
    weight,
    time_weight,
    bias,
    sums,
    columns,
    total,
):
    i = pl.program_id(0)
    parts, planes, part_rows, width = own_ref.shape
    step, channels, pixels = normed_ref.shape
    shards = 2 * planes
    rows = weight.shape[1] // shards
    time_rows = width - rows
    count, core, plane, part = (where_ref[n] for n in range(4))
    outs = parts * part_rows
    lane = lax.broadcasted_iota(jnp.int32, (outs, LANES), 1)

    @pl.when(i == 0)
    def _():
        for f in range(shards):
            for q in range(parts):
                at = (q ^ part, (f // 2) ^ plane)
                block = jnp.where(core == f % 2, own_ref[at], other_ref[at])
                into = slice(q * part_rows, (q + 1) * part_rows)
                weight[into, f * rows : (f + 1) * rows] = block[:, :rows]
                time_weight[into, f * time_rows : (f + 1) * time_rows] = block[:, rows:]
        bias[...] = jnp.dot(time_weight[...], features_ref[...], preferred_element_type=f32)
        total[...] = jnp.zeros_like(total)
        sums[...] = jnp.zeros_like(sums)

    @pl.when(i * step < count)
    def _():
        for t in range(step):
            write_columns(normed_ref[t], columns, t)
        conv = jnp.dot(weight[...], columns[...], preferred_element_type=f32)
        errors = []
        error_sums = sums[...]
        for t in range(step):
            slot = i * step + t
            live = slot < count
            tile_bias = jnp.sum(jnp.where(lane == slot, bias[...], 0.0), axis=1, keepdims=True)
            pred32 = tiles_ref[t].astype(f32) + conv[:, t * pixels : (t + 1) * pixels] + tile_bias
            predicted_ref[t] = jnp.where(live, pred32, 0.0).astype(bf16)
            error = jnp.where(
                live, (pred32 - target_ref[t].astype(f32)) * (1.0 / pixels), 0.0
            ).astype(bf16)
            error_sum = jnp.sum(error.astype(f32), axis=1, keepdims=True)
            error_sums = jnp.where(lane == slot, error_sum, error_sums)
            errors.append(error)
        sums[...] = error_sums
        total[...] += lax.dot_general(
            jnp.concatenate(errors, axis=1),
            columns[...],
            (((1,), (1,)), ((), ())),
            preferred_element_type=f32,
        )

    @pl.when(i * step >= count)
    def _():
        predicted_ref[...] = jnp.zeros_like(predicted_ref)

    @pl.when(i == steps - 1)
    def _():
        high = sums[...].astype(bf16)
        low = (sums[...] - high.astype(f32)).astype(bf16)
        time_total = sum(
            lax.dot_general(
                term, features_ref[...], (((1,), (1,)), ((), ())), preferred_element_type=f32
            )
            for term in (high, low)
        )
        for c in range(2):
            for f in range(shards):
                into = keep_ref if f % 2 == c else send_ref

                @pl.when(core == c)
                def _():
                    for q in range(parts):
                        at = (q ^ part, (f // 2) ^ plane)
                        here = slice(q * part_rows, (q + 1) * part_rows)
                        into[at] = jnp.concatenate(
                            [
                                total[here, f * rows : (f + 1) * rows],
                                time_total[here, f * time_rows : (f + 1) * time_rows],
                            ],
                            axis=1,
                        ).astype(bf16)


def conv_both(where, own, other, features, normed, tiles, targets, rows):
    number, channels, pixels = normed.shape
    parts, planes, part_rows, width = own.shape
    shards, outs = 2 * planes, parts * part_rows
    depth, emb = shards * rows, shards * (width - rows)
    step = tiles_per_step(number)
    steps = number // step

    def whole(shape):
        return pl.BlockSpec(shape, lambda i, c: (0,) * len(shape))

    block = pl.BlockSpec((step, channels, pixels), lambda i, c: (i, 0, 0))
    return pl.pallas_call(
        functools.partial(conv_kernel, steps),
        grid_spec=pltpu.PrefetchScalarGridSpec(
            num_scalar_prefetch=1,
            grid=(steps,),
            in_specs=[whole(own.shape), whole(own.shape), whole(features.shape)] + [block] * 3,
            out_specs=[block, whole(own.shape), whole(own.shape)],
            scratch_shapes=[
                pltpu.VMEM((outs, depth), bf16),
                pltpu.VMEM((outs, emb), bf16),
                pltpu.VMEM((outs, LANES), f32),
                pltpu.VMEM((outs, LANES), f32),
                pltpu.VMEM((depth, step * pixels), bf16),
                pltpu.VMEM((outs, depth), f32),
            ],
        ),
        out_shape=[
            jax.ShapeDtypeStruct(tiles.shape, bf16),
            jax.ShapeDtypeStruct(own.shape, bf16),
            jax.ShapeDtypeStruct(own.shape, bf16),
        ],
        compiler_params=pltpu.CompilerParams(vmem_limit_bytes=56 * 2**20),
        cost_estimate=pl.CostEstimate(
            flops=4 * number * pixels * depth * outs, bytes_accessed=8 * tiles.size, transcendentals=0
        ),
        name="conv_both",
    )(where, own, other, features, normed, tiles, targets)


def swap(values, axis, mask):
    pairs = [(i, i ^ mask) for i in range(lax.axis_size(axis))]
    return lax.ppermute(values, axis, pairs)


def bits_of(axis):
    return (lax.axis_size(axis) - 1).bit_length()


def bit_groups(bits):
    return [(at, min(2, bits - at)) for at in range(0, bits, 2)]


def gather_partners(values, axis, low, bits):
    shape = values.shape
    values = values[None]
    for at, width in bit_groups(bits):
        parts = [values] + [swap(values, axis, m << (low + at)) for m in range(1, 1 << width)]
        values = jnp.concatenate(parts)
    return values.reshape((1 << bits,) + shape)


def add_up(parts):
    total = parts[0].astype(f32)
    for part in parts[1:]:
        total = total + part.astype(f32)
    return total.astype(parts[0].dtype)


def scatter_partners(values, axis, low, bits):
    shape = values.shape[1:]
    for at, width in bit_groups(bits):
        values = values.reshape((-1, 1 << width) + shape)
        parts = [values[:, 0]]
        parts += [swap(values[:, m], axis, m << (low + at)) for m in range(1, 1 << width)]
        values = add_up(parts)
    return values.reshape(shape)


def time_features(timesteps, emb):
    half_width = emb // 2
    frequency = jnp.exp(-math.log(10000.0) * jnp.arange(half_width, dtype=f32) / half_width)
    angles = frequency[:, None] * timesteps.astype(f32)[None, :]
    return jax.nn.silu(jnp.concatenate([jnp.cos(angles), jnp.sin(angles)])).astype(bf16)


def per_device(latents, target_noise, counts, timesteps, conv_master, temb_master):
    tiles = jnp.swapaxes(latents[0], 1, 2)
    targets = jnp.swapaxes(target_noise[0], 1, 2)
    number = tiles.shape[0]
    shards = lax.axis_size("fsdp")
    shard_bits, peer_bits = bits_of("fsdp"), bits_of("dp")
    my_shard, my_peer = lax.axis_index("fsdp"), lax.axis_index("dp")
    rows, outs = conv_master.shape
    time_rows = temb_master.shape[0]
    part_bits = max(n for n in range(peer_bits + 1) if outs % (16 << n) == 0)
    parts = 1 << part_bits
    part = my_peer & (parts - 1)
    plane_bits = shard_bits - 1
    core, plane = my_shard & 1, my_shard >> 1
    where = jnp.stack([counts[0][my_peer], core, plane, part]).astype(jnp.int32)

    master = jnp.concatenate([conv_master.T, temb_master.T], axis=1).astype(bf16)
    master = master.reshape(parts, outs // parts, rows + time_rows)
    mine = [lax.dynamic_index_in_dim(master, part ^ m, 0, keepdims=False) for m in range(parts)]
    over_planes = gather_partners(mine[0], "fsdp", 1, plane_bits)
    tiles_then, over_planes = lax.optimization_barrier((tiles, over_planes))
    normed = group_norm(tiles_then)
    features = time_features(jnp.pad(timesteps[0], (0, LANES - number)), time_rows * shards)
    far = gather_partners(over_planes[1:], "dp", 0, part_bits)
    own = jnp.concatenate([jnp.stack(mine)[:, None], far], axis=1)
    other = swap(own, "fsdp", 1)

    predicted, keep, send = conv_both(where, own, other, features, normed, tiles, targets, rows)

    grad = add_up([keep, swap(send, "fsdp", 1)])
    grad = scatter_partners(grad, "dp", 0, part_bits)
    for bit in range(part_bits, peer_bits):
        grad = add_up([grad, swap(grad, "dp", 1 << bit)])
    grad = scatter_partners(grad, "fsdp", 1, plane_bits)
    grad = gather_partners(grad, "dp", 0, part_bits)
    grad = jnp.concatenate(
        [lax.dynamic_index_in_dim(grad, part ^ q, 0, keepdims=False) for q in range(parts)]
    ).astype(f32)
    return (jnp.swapaxes(predicted, 1, 2)[None], grad[:, :rows].T, grad[:, rows:].T)


def solution(mesh):
    placed = (
        P("fsdp", "dp", None, None),
        P("fsdp", "dp", None, None),
        P("fsdp", None),
        P("fsdp", "dp"),
        P("fsdp", None),
        P("fsdp", None),
    )
    return jax.shard_map(
        per_device,
        mesh=mesh,
        in_specs=placed,
        out_specs=(P("fsdp", "dp", None, None), P("fsdp", None), P("fsdp", None)),
        check_vma=False,
    )
```

```python
import functools
import math

import jax
import jax.numpy as jnp
from jax import lax
from jax.experimental import pallas as pl
from jax.experimental.pallas import tpu as pltpu
from jax.sharding import PartitionSpec as P

GROUPS = 32
SIDE = 16
LANES = 128

bf16 = jnp.bfloat16
f32 = jnp.float32


def tiles_per_step(number):
    return max(size for size in range(1, 6) if number % size == 0)


def norm_kernel(group_width, same_ref, tiles_ref, out_ref):
    same_group = same_ref[...]
    number, channels, pixels = tiles_ref.shape
    scale = 1.0 / (group_width * pixels)
    lane = lax.broadcasted_iota(jnp.int32, (channels, LANES), 1)

    def group_mean(row_sums):
        high = row_sums.astype(bf16).astype(f32)
        middle = (row_sums - high).astype(bf16).astype(f32)
        low = row_sums - high - middle
        terms = jnp.where(
            lane == 0, high, jnp.where(lane == 1, middle, jnp.where(lane == 2, low, 0.0))
        ).astype(bf16)
        summed = jnp.dot(same_group, terms, preferred_element_type=f32)
        return jnp.sum(summed, axis=1, keepdims=True) * scale

    for at in range(number):
        values = tiles_ref[at].astype(f32)
        centred = values - group_mean(jnp.sum(values, axis=1, keepdims=True))
        variance = group_mean(jnp.sum(centred * centred, axis=1, keepdims=True))
        scaled = centred * lax.rsqrt(variance + 1e-05)
        out_ref[at] = (scaled / (1.0 + jnp.exp(-scaled))).astype(bf16)


def group_norm(tiles):
    number, channels, pixels = tiles.shape
    step = tiles_per_step(number)
    group_width = channels // GROUPS
    group = jnp.arange(channels, dtype=jnp.int32) // group_width
    same_group = (group[:, None] == group[None, :]).astype(bf16)
    block = pl.BlockSpec((step, channels, pixels), lambda i: (i, 0, 0))
    return pl.pallas_call(
        functools.partial(norm_kernel, group_width),
        grid=(number // step,),
        in_specs=[pl.BlockSpec((channels, channels), lambda i: (0, 0)), block],
        out_specs=block,
        out_shape=jax.ShapeDtypeStruct(tiles.shape, bf16),
        compiler_params=pltpu.CompilerParams(vmem_limit_bytes=32 * 2**20),
        cost_estimate=pl.CostEstimate(
            flops=20 * tiles.size, bytes_accessed=4 * tiles.size, transcendentals=tiles.size
        ),
        name="group_norm",
    )(same_group, tiles)


def write_columns(values, columns_ref, at):
    channels, pixels = values.shape
    cell = lax.broadcasted_iota(jnp.int32, (channels, pixels), 1)
    column = cell % SIDE
    wide = values.astype(f32)
    for b in range(3):
        if b == 1:
            moved = wide
        else:
            moved = pltpu.roll(wide, (1 - b) % pixels, 1)
            moved = jnp.where(column == (0 if b == 0 else SIDE - 1), 0.0, moved)
        for a in range(3):
            if a == 1:
                shifted = moved
            else:
                shifted = pltpu.roll(moved, ((1 - a) * SIDE) % pixels, 1)
                outside = (cell < SIDE) if a == 0 else (cell >= pixels - SIDE)
                shifted = jnp.where(outside, 0.0, shifted)
            tap = 3 * a + b
            columns_ref[
                tap * channels : (tap + 1) * channels, at * pixels : (at + 1) * pixels
            ] = shifted.astype(values.dtype)


def conv_kernel(
    steps,
    where_ref,
    own_ref,
    other_ref,
    own_time_ref,
    other_time_ref,
    features_ref,
    normed_ref,
    tiles_ref,
    target_ref,
    predicted_ref,
    keep_ref,
    send_ref,
    keep_time_ref,
    send_time_ref,
    weight,
    time_weight,
    bias,
    sums,
    columns,
    total,
):
    i = pl.program_id(0)
    parts, planes, part_rows, rows = own_ref.shape
    step, channels, pixels = normed_ref.shape
    shards = 2 * planes
    time_rows = own_time_ref.shape[1]
    count, core, plane, part = (where_ref[n] for n in range(4))
    outs = parts * part_rows
    lane = lax.broadcasted_iota(jnp.int32, (outs, LANES), 1)

    @pl.when(i == 0)
    def _():
        for f in range(shards):
            for q in range(parts):
                at = (q ^ part, (f // 2) ^ plane)
                block = jnp.where(core == f % 2, own_ref[at], other_ref[at])
                into = slice(q * part_rows, (q + 1) * part_rows)
                weight[into, f * rows : (f + 1) * rows] = block
            block = jnp.where(
                core == f % 2, own_time_ref[(f // 2) ^ plane], other_time_ref[(f // 2) ^ plane]
            )
            time_weight[f * time_rows : (f + 1) * time_rows, :] = block.astype(f32)
        bias[...] = lax.dot_general(
            time_weight[...].astype(bf16),
            features_ref[...],
            (((0,), (0,)), ((), ())),
            preferred_element_type=f32,
        )
        total[...] = jnp.zeros_like(total)
        sums[...] = jnp.zeros_like(sums)

    @pl.when(i * step < count)
    def _():
        for t in range(step):
            write_columns(normed_ref[t], columns, t)
        conv = jnp.dot(weight[...], columns[...], preferred_element_type=f32)
        errors = []
        error_sums = sums[...]
        for t in range(step):
            slot = i * step + t
            live = slot < count
            tile_bias = jnp.sum(jnp.where(lane == slot, bias[...], 0.0), axis=1, keepdims=True)
            pred32 = tiles_ref[t].astype(f32) + conv[:, t * pixels : (t + 1) * pixels] + tile_bias
            predicted_ref[t] = jnp.where(live, pred32, 0.0).astype(bf16)
            error = jnp.where(
                live, (pred32 - target_ref[t].astype(f32)) * (1.0 / pixels), 0.0
            ).astype(bf16)
            error_sum = jnp.sum(error.astype(f32), axis=1, keepdims=True)
            error_sums = jnp.where(lane == slot, error_sum, error_sums)
            errors.append(error)
        sums[...] = error_sums
        total[...] += lax.dot_general(
            jnp.concatenate(errors, axis=1),
            columns[...],
            (((1,), (1,)), ((), ())),
            preferred_element_type=f32,
        )

    @pl.when(i * step >= count)
    def _():
        predicted_ref[...] = jnp.zeros_like(predicted_ref)

    @pl.when(i == steps - 1)
    def _():
        high = sums[...].astype(bf16)
        low = (sums[...] - high.astype(f32)).astype(bf16)
        time_total = sum(
            lax.dot_general(
                features_ref[...], term, (((1,), (1,)), ((), ())), preferred_element_type=f32
            )
            for term in (high, low)
        )
        for c in range(2):
            for f in range(shards):
                into = keep_ref if f % 2 == c else send_ref
                time_into = keep_time_ref if f % 2 == c else send_time_ref

                @pl.when(core == c)
                def _():
                    at = (f // 2) ^ plane
                    for q in range(parts):
                        here = slice(q * part_rows, (q + 1) * part_rows)
                        into[q ^ part, at] = total[here, f * rows : (f + 1) * rows].astype(bf16)
                    time_into[at] = time_total[f * time_rows : (f + 1) * time_rows].astype(bf16)


def conv_both(where, own, other, own_time, other_time, features, normed, tiles, targets):
    number, channels, pixels = normed.shape
    parts, planes, part_rows, rows = own.shape
    shards, outs = 2 * planes, parts * part_rows
    depth, emb = shards * rows, features.shape[0]
    step = tiles_per_step(number)
    steps = number // step

    def whole(shape):
        return pl.BlockSpec(shape, lambda i, c: (0,) * len(shape))

    block = pl.BlockSpec((step, channels, pixels), lambda i, c: (i, 0, 0))
    return pl.pallas_call(
        functools.partial(conv_kernel, steps),
        grid_spec=pltpu.PrefetchScalarGridSpec(
            num_scalar_prefetch=1,
            grid=(steps,),
            in_specs=[whole(own.shape)] * 2
            + [whole(own_time.shape)] * 2
            + [whole(features.shape)]
            + [block] * 3,
            out_specs=[block] + [whole(own.shape)] * 2 + [whole(own_time.shape)] * 2,
            scratch_shapes=[
                pltpu.VMEM((outs, depth), bf16),
                pltpu.VMEM((emb, outs), f32),
                pltpu.VMEM((outs, LANES), f32),
                pltpu.VMEM((outs, LANES), f32),
                pltpu.VMEM((depth, step * pixels), bf16),
                pltpu.VMEM((outs, depth), f32),
            ],
        ),
        out_shape=[
            jax.ShapeDtypeStruct(tiles.shape, bf16),
            jax.ShapeDtypeStruct(own.shape, bf16),
            jax.ShapeDtypeStruct(own.shape, bf16),
            jax.ShapeDtypeStruct(own_time.shape, bf16),
            jax.ShapeDtypeStruct(own_time.shape, bf16),
        ],
        compiler_params=pltpu.CompilerParams(vmem_limit_bytes=56 * 2**20),
        cost_estimate=pl.CostEstimate(
            flops=4 * number * pixels * depth * outs, bytes_accessed=8 * tiles.size, transcendentals=0
        ),
        name="conv_both",
    )(where, own, other, own_time, other_time, features, normed, tiles, targets)


def swap(values, axis, mask):
    pairs = [(i, i ^ mask) for i in range(lax.axis_size(axis))]
    return lax.ppermute(values, axis, pairs)


def bits_of(axis):
    return (lax.axis_size(axis) - 1).bit_length()


def bit_groups(bits):
    return [(at, min(2, bits - at)) for at in range(0, bits, 2)]


def gather_partners(values, axis, low, bits):
    shape = values.shape
    values = values[None]
    for at, width in bit_groups(bits):
        parts = [values] + [swap(values, axis, m << (low + at)) for m in range(1, 1 << width)]
        values = jnp.concatenate(parts)
    return values.reshape((1 << bits,) + shape)


def add_up(parts):
    kept_as = parts[0].dtype
    parts = [part.astype(f32) for part in parts]
    while len(parts) > 1:
        parts = [sum(parts[n : n + 2]) for n in range(0, len(parts), 2)]
    return parts[0].astype(kept_as)


def sum_partners(values, axis, low, bits):
    for at, width in bit_groups(bits):
        parts = [values] + [swap(values, axis, m << (low + at)) for m in range(1, 1 << width)]
        values = add_up(parts)
    return values


def scatter_partners(values, axis, low, bits):
    shape = values.shape[1:]
    for at, width in bit_groups(bits):
        values = values.reshape((-1, 1 << width) + shape)
        parts = [values[:, 0]]
        parts += [swap(values[:, m], axis, m << (low + at)) for m in range(1, 1 << width)]
        values = add_up(parts)
    return values.reshape(shape)


def time_features(timesteps, emb):
    half_width = emb // 2
    frequency = jnp.exp(-math.log(10000.0) * jnp.arange(half_width, dtype=f32) / half_width)
    angles = frequency[:, None] * timesteps.astype(f32)[None, :]
    return jax.nn.silu(jnp.concatenate([jnp.cos(angles), jnp.sin(angles)])).astype(bf16)


def per_device(latents, target_noise, counts, timesteps, conv_master, temb_master):
    tiles = jnp.swapaxes(latents[0], 1, 2)
    targets = jnp.swapaxes(target_noise[0], 1, 2)
    number = tiles.shape[0]
    shards = lax.axis_size("fsdp")
    shard_bits, peer_bits = bits_of("fsdp"), bits_of("dp")
    my_shard, my_peer = lax.axis_index("fsdp"), lax.axis_index("dp")
    rows, outs = conv_master.shape
    time_rows = temb_master.shape[0]
    part_bits = max(n for n in range(peer_bits + 1) if outs % (16 << n) == 0)
    parts = 1 << part_bits
    part = my_peer & (parts - 1)
    plane_bits = shard_bits - 1
    core, plane = my_shard & 1, my_shard >> 1
    where = jnp.stack([counts[0][my_peer], core, plane, part]).astype(jnp.int32)

    master = conv_master.T.astype(bf16).reshape(parts, outs // parts, rows)
    time_master = temb_master.astype(bf16)
    mine = [lax.dynamic_index_in_dim(master, part ^ m, 0, keepdims=False) for m in range(parts)]
    over_planes = gather_partners(mine[0], "fsdp", 1, plane_bits)
    features = time_features(jnp.pad(timesteps[0], (0, LANES - number)), time_rows * shards)
    over_planes, features, tiles_then, time_master, where = lax.optimization_barrier(
        (over_planes, features, tiles, time_master, where)
    )
    far = gather_partners(over_planes[1:], "dp", 0, part_bits)
    own_time = gather_partners(time_master, "fsdp", 1, plane_bits)
    normed = group_norm(tiles_then)
    own = jnp.concatenate([jnp.stack(mine)[:, None], far], axis=1)
    own, own_time, normed = lax.optimization_barrier((own, own_time, normed))
    other, other_time = swap(own, "fsdp", 1), swap(own_time, "fsdp", 1)

    predicted, keep, send, keep_time, send_time = conv_both(
        where, own, other, own_time, other_time, features, normed, tiles, targets
    )

    grad = add_up([keep, swap(send, "fsdp", 1)])
    time_grad = add_up([keep_time, swap(send_time, "fsdp", 1)])
    grad, time_grad = lax.optimization_barrier((grad, time_grad))
    grad = scatter_partners(grad, "dp", 0, part_bits)
    for bit in range(part_bits, peer_bits):
        grad = sum_partners(grad, "dp", bit, 1)
    time_grad = scatter_partners(time_grad, "fsdp", 1, plane_bits)
    grad = scatter_partners(grad, "fsdp", 1, plane_bits)
    time_grad = sum_partners(time_grad, "dp", 0, peer_bits)
    grad = gather_partners(grad, "dp", 0, part_bits)
    grad = jnp.concatenate(
        [lax.dynamic_index_in_dim(grad, part ^ q, 0, keepdims=False) for q in range(parts)]
    )
    return (
        jnp.swapaxes(predicted, 1, 2)[None],
        grad.T.astype(f32),
        time_grad.astype(f32),
    )


def solution(mesh):
    placed = (
        P("fsdp", "dp", None, None),
        P("fsdp", "dp", None, None),
        P("fsdp", None),
        P("fsdp", "dp"),
        P("fsdp", None),
        P("fsdp", None),
    )
    return jax.shard_map(
        per_device,
        mesh=mesh,
        in_specs=placed,
        out_specs=(P("fsdp", "dp", None, None), P("fsdp", None), P("fsdp", None)),
        check_vma=False,
    )
```

```python
import functools
import math

import jax
import jax.numpy as jnp
from jax import lax
from jax.experimental import pallas as pl
from jax.experimental.pallas import tpu as pltpu
from jax.sharding import PartitionSpec as P

GROUPS = 32
SIDE = 16
LANES = 128

bf16 = jnp.bfloat16
f32 = jnp.float32


def tiles_per_step(number):
    return max(size for size in range(1, 6) if number % size == 0)


def norm_kernel(group_width, same_ref, tiles_ref, out_ref):
    same_group = same_ref[...]
    number, channels, pixels = tiles_ref.shape
    scale = 1.0 / (group_width * pixels)
    lane = lax.broadcasted_iota(jnp.int32, (channels, LANES), 1)

    def group_mean(row_sums):
        high = row_sums.astype(bf16).astype(f32)
        middle = (row_sums - high).astype(bf16).astype(f32)
        low = row_sums - high - middle
        terms = jnp.where(
            lane == 0, high, jnp.where(lane == 1, middle, jnp.where(lane == 2, low, 0.0))
        ).astype(bf16)
        summed = jnp.dot(same_group, terms, preferred_element_type=f32)
        return jnp.sum(summed, axis=1, keepdims=True) * scale

    for at in range(number):
        values = tiles_ref[at].astype(f32)
        centred = values - group_mean(jnp.sum(values, axis=1, keepdims=True))
        variance = group_mean(jnp.sum(centred * centred, axis=1, keepdims=True))
        scaled = centred * lax.rsqrt(variance + 1e-05)
        half = 0.5 * scaled
        out_ref[at] = (half + half * jnp.tanh(half)).astype(bf16)


def group_norm(tiles):
    number, channels, pixels = tiles.shape
    step = tiles_per_step(number)
    group_width = channels // GROUPS
    group = jnp.arange(channels, dtype=jnp.int32) // group_width
    same_group = (group[:, None] == group[None, :]).astype(bf16)
    block = pl.BlockSpec((step, channels, pixels), lambda i: (i, 0, 0))
    return pl.pallas_call(
        functools.partial(norm_kernel, group_width),
        grid=(number // step,),
        in_specs=[pl.BlockSpec((channels, channels), lambda i: (0, 0)), block],
        out_specs=block,
        out_shape=jax.ShapeDtypeStruct(tiles.shape, bf16),
        compiler_params=pltpu.CompilerParams(vmem_limit_bytes=60 * 2**20),
        cost_estimate=pl.CostEstimate(
            flops=20 * tiles.size, bytes_accessed=4 * tiles.size, transcendentals=tiles.size
        ),
        name="group_norm",
    )(same_group, tiles)


def write_columns(values, columns_ref, at):
    channels, pixels = values.shape
    cell = lax.broadcasted_iota(jnp.int32, (channels, pixels), 1)
    column = cell % SIDE
    wide = values.astype(f32)
    for b in range(3):
        if b == 1:
            moved = wide
        else:
            moved = pltpu.roll(wide, (1 - b) % pixels, 1)
            moved = jnp.where(column == (0 if b == 0 else SIDE - 1), 0.0, moved)
        for a in range(3):
            if a == 1:
                shifted = moved
            else:
                shifted = pltpu.roll(moved, ((1 - a) * SIDE) % pixels, 1)
                outside = (cell < SIDE) if a == 0 else (cell >= pixels - SIDE)
                shifted = jnp.where(outside, 0.0, shifted)
            tap = 3 * a + b
            columns_ref[
                tap * channels : (tap + 1) * channels, at * pixels : (at + 1) * pixels
            ] = shifted.astype(values.dtype)


def conv_kernel(
    steps,
    counts_ref,
    own_ref,
    other_ref,
    own_time_ref,
    other_time_ref,
    features_ref,
    normed_ref,
    tiles_ref,
    target_ref,
    predicted_ref,
    keep_ref,
    send_ref,
    keep_time_ref,
    send_time_ref,
    weight,
    time_weight,
    bias,
    sums,
    columns,
    total,
):
    i = pl.program_id(0)
    parts, planes, part_rows, rows = own_ref.shape
    step, channels, pixels = normed_ref.shape
    shards = 2 * planes
    time_rows = own_time_ref.shape[1]
    my_shard, my_peer = lax.axis_index("fsdp"), lax.axis_index("dp")
    count = counts_ref[0, my_peer]
    core, plane, part = my_shard & 1, my_shard >> 1, my_peer & (parts - 1)
    outs = parts * part_rows
    lane = lax.broadcasted_iota(jnp.int32, (outs, LANES), 1)

    @pl.when(i == 0)
    def _():
        for f in range(shards):
            for q in range(parts):
                at = (q ^ part, (f // 2) ^ plane)
                block = jnp.where(core == f % 2, own_ref[at], other_ref[at])
                into = slice(q * part_rows, (q + 1) * part_rows)
                weight[into, f * rows : (f + 1) * rows] = block
            block = jnp.where(
                core == f % 2, own_time_ref[(f // 2) ^ plane], other_time_ref[(f // 2) ^ plane]
            )
            time_weight[f * time_rows : (f + 1) * time_rows, :] = block.astype(f32)
        bias[...] = lax.dot_general(
            time_weight[...].astype(bf16),
            features_ref[...],
            (((0,), (0,)), ((), ())),
            preferred_element_type=f32,
        )
        total[...] = jnp.zeros_like(total)
        sums[...] = jnp.zeros_like(sums)

    @pl.when(i * step < count)
    def _():
        for t in range(step):
            write_columns(normed_ref[t], columns, t)
        conv = jnp.dot(weight[...], columns[...], preferred_element_type=f32)
        errors = []
        error_sums = sums[...]
        for t in range(step):
            slot = i * step + t
            live = slot < count
            tile_bias = jnp.sum(jnp.where(lane == slot, bias[...], 0.0), axis=1, keepdims=True)
            pred32 = tiles_ref[t].astype(f32) + conv[:, t * pixels : (t + 1) * pixels] + tile_bias
            predicted_ref[t] = jnp.where(live, pred32, 0.0).astype(bf16)
            error = jnp.where(
                live, (pred32 - target_ref[t].astype(f32)) * (1.0 / pixels), 0.0
            ).astype(bf16)
            error_sum = jnp.sum(error.astype(f32), axis=1, keepdims=True)
            error_sums = jnp.where(lane == slot, error_sum, error_sums)
            errors.append(error)
        sums[...] = error_sums
        total[...] += lax.dot_general(
            jnp.concatenate(errors, axis=1),
            columns[...],
            (((1,), (1,)), ((), ())),
            preferred_element_type=f32,
        )

    @pl.when(i * step >= count)
    def _():
        predicted_ref[...] = jnp.zeros_like(predicted_ref)

    @pl.when(i == steps - 1)
    def _():
        high = sums[...].astype(bf16)
        low = (sums[...] - high.astype(f32)).astype(bf16)
        time_total = sum(
            lax.dot_general(
                features_ref[...], term, (((1,), (1,)), ((), ())), preferred_element_type=f32
            )
            for term in (high, low)
        )
        for c in range(2):
            for f in range(shards):
                into = keep_ref if f % 2 == c else send_ref
                time_into = keep_time_ref if f % 2 == c else send_time_ref

                @pl.when(core == c)
                def _():
                    at = (f // 2) ^ plane
                    for q in range(parts):
                        here = slice(q * part_rows, (q + 1) * part_rows)
                        into[q ^ part, at] = total[here, f * rows : (f + 1) * rows].astype(bf16)
                    time_into[at] = time_total[f * time_rows : (f + 1) * time_rows].astype(bf16)


def conv_both(counts, own, other, own_time, other_time, features, normed, tiles, targets):
    number, channels, pixels = normed.shape
    parts, planes, part_rows, rows = own.shape
    shards, outs = 2 * planes, parts * part_rows
    depth, emb = shards * rows, features.shape[0]
    step = tiles_per_step(number)
    steps = number // step

    def whole(shape):
        return pl.BlockSpec(shape, lambda i, c: (0,) * len(shape))

    block = pl.BlockSpec((step, channels, pixels), lambda i, c: (i, 0, 0))
    return pl.pallas_call(
        functools.partial(conv_kernel, steps),
        grid_spec=pltpu.PrefetchScalarGridSpec(
            num_scalar_prefetch=1,
            grid=(steps,),
            in_specs=[whole(own.shape)] * 2
            + [whole(own_time.shape)] * 2
            + [whole(features.shape)]
            + [block] * 3,
            out_specs=[block] + [whole(own.shape)] * 2 + [whole(own_time.shape)] * 2,
            scratch_shapes=[
                pltpu.VMEM((outs, depth), bf16),
                pltpu.VMEM((emb, outs), f32),
                pltpu.VMEM((outs, LANES), f32),
                pltpu.VMEM((outs, LANES), f32),
                pltpu.VMEM((depth, step * pixels), bf16),
                pltpu.VMEM((outs, depth), f32),
            ],
        ),
        out_shape=[
            jax.ShapeDtypeStruct(tiles.shape, bf16),
            jax.ShapeDtypeStruct(own.shape, bf16),
            jax.ShapeDtypeStruct(own.shape, bf16),
            jax.ShapeDtypeStruct(own_time.shape, bf16),
            jax.ShapeDtypeStruct(own_time.shape, bf16),
        ],
        compiler_params=pltpu.CompilerParams(vmem_limit_bytes=44 * 2**20),
        cost_estimate=pl.CostEstimate(
            flops=4 * number * pixels * depth * outs, bytes_accessed=8 * tiles.size, transcendentals=0
        ),
        name="conv_both",
    )(counts, own, other, own_time, other_time, features, normed, tiles, targets)


def swap(values, axis, mask):
    pairs = [(i, i ^ mask) for i in range(lax.axis_size(axis))]
    return lax.ppermute(values, axis, pairs)


def bits_of(axis):
    return (lax.axis_size(axis) - 1).bit_length()


def bit_groups(bits):
    return [(at, min(2, bits - at)) for at in range(0, bits, 2)]


def gather_partners(values, axis, low, bits):
    shape = values.shape
    values = values[None]
    for at, width in bit_groups(bits):
        parts = [values] + [swap(values, axis, m << (low + at)) for m in range(1, 1 << width)]
        values = jnp.concatenate(parts)
    return values.reshape((1 << bits,) + shape)


def add_up(parts):
    kept_as = parts[0].dtype
    parts = [part.astype(f32) for part in parts]
    while len(parts) > 1:
        parts = [sum(parts[n : n + 2]) for n in range(0, len(parts), 2)]
    return parts[0].astype(kept_as)


def sum_partners(values, axis, low, bits):
    for at, width in bit_groups(bits):
        parts = [values] + [swap(values, axis, m << (low + at)) for m in range(1, 1 << width)]
        values = add_up(parts)
    return values


def scatter_partners(values, axis, low, bits):
    shape = values.shape[1:]
    for at, width in bit_groups(bits):
        values = values.reshape((-1, 1 << width) + shape)
        parts = [values[:, 0]]
        parts += [swap(values[:, m], axis, m << (low + at)) for m in range(1, 1 << width)]
        values = add_up(parts)
    return values.reshape(shape)


def time_features(timesteps, emb):
    half_width = emb // 2
    frequency = jnp.exp(-math.log(10000.0) * jnp.arange(half_width, dtype=f32) / half_width)
    angles = frequency[:, None] * timesteps.astype(f32)[None, :]
    return jax.nn.silu(jnp.concatenate([jnp.cos(angles), jnp.sin(angles)])).astype(bf16)


def per_device(latents, target_noise, counts, timesteps, conv_master, temb_master):
    tiles = jnp.swapaxes(latents[0], 1, 2)
    targets = jnp.swapaxes(target_noise[0], 1, 2)
    number = tiles.shape[0]
    shards = lax.axis_size("fsdp")
    shard_bits, peer_bits = bits_of("fsdp"), bits_of("dp")
    rows, outs = conv_master.shape
    time_rows = temb_master.shape[0]
    part_bits = max(n for n in range(peer_bits + 1) if outs % (16 << n) == 0)
    parts = 1 << part_bits
    part = lax.axis_index("dp") & (parts - 1)
    plane_bits = shard_bits - 1

    master = conv_master.T.astype(bf16).reshape(parts, outs // parts, rows)
    time_master = temb_master.astype(bf16)
    mine = [lax.dynamic_index_in_dim(master, part ^ m, 0, keepdims=False) for m in range(parts)]
    over_planes = gather_partners(mine[0], "fsdp", 1, plane_bits)
    features = time_features(jnp.pad(timesteps[0], (0, LANES - number)), time_rows * shards)
    time_master, features = lax.optimization_barrier((time_master, features))
    own_time = gather_partners(time_master, "fsdp", 1, plane_bits)
    over_planes, tiles_then = lax.optimization_barrier((over_planes, tiles))
    far = gather_partners(over_planes[1:], "dp", 0, part_bits)
    normed = group_norm(tiles_then)
    own = jnp.concatenate([jnp.stack(mine)[:, None], far], axis=1)
    own, own_time, normed = lax.optimization_barrier((own, own_time, normed))
    other, other_time = swap(own, "fsdp", 1), swap(own_time, "fsdp", 1)

    predicted, keep, send, keep_time, send_time = conv_both(
        counts, own, other, own_time, other_time, features, normed, tiles, targets
    )

    grad = add_up([keep, swap(send, "fsdp", 1)])
    time_grad = add_up([keep_time, swap(send_time, "fsdp", 1)])
    grad, time_grad = lax.optimization_barrier((grad, time_grad))
    grad = scatter_partners(grad, "dp", 0, part_bits)
    for bit in range(part_bits, peer_bits):
        grad = sum_partners(grad, "dp", bit, 1)
    time_grad = scatter_partners(time_grad, "fsdp", 1, plane_bits)
    grad = scatter_partners(grad, "fsdp", 1, plane_bits)
    time_grad = sum_partners(time_grad, "dp", 0, peer_bits)
    grad = gather_partners(grad, "dp", 0, part_bits)
    grad = jnp.concatenate(
        [lax.dynamic_index_in_dim(grad, part ^ q, 0, keepdims=False) for q in range(parts)]
    )
    return (
        jnp.swapaxes(predicted, 1, 2)[None],
        grad.T.astype(f32),
        time_grad.astype(f32),
    )


def solution(mesh):
    placed = (
        P("fsdp", "dp", None, None),
        P("fsdp", "dp", None, None),
        P("fsdp", None),
        P("fsdp", "dp"),
        P("fsdp", None),
        P("fsdp", None),
    )
    return jax.shard_map(
        per_device,
        mesh=mesh,
        in_specs=placed,
        out_specs=(P("fsdp", "dp", None, None), P("fsdp", None), P("fsdp", None)),
        check_vma=False,
    )
```

```python
import functools
import math

import jax
import jax.numpy as jnp
import numpy as np
from jax import lax
from jax.experimental import pallas as pl
from jax.experimental.pallas import tpu as pltpu
from jax.sharding import PartitionSpec as P

GROUPS = 32
SIDE = 16
LANES = 128

bf16 = jnp.bfloat16
f32 = jnp.float32


def tiles_per_step(number):
    return max(size for size in range(1, 6) if number % size == 0)


def norm_kernel(group_width, same_ref, tiles_ref, out_ref):
    same_group = same_ref[...]
    number, channels, pixels = tiles_ref.shape
    scale = 1.0 / (group_width * pixels)
    lane = lax.broadcasted_iota(jnp.int32, (channels, LANES), 1)

    def group_means(values):
        row_sums = jnp.zeros((channels, LANES), f32)
        for t, value in enumerate(values):
            row_sums = jnp.where(lane == t, jnp.sum(value, axis=1, keepdims=True), row_sums)
        high = row_sums.astype(bf16)
        rest = row_sums - high.astype(f32)
        middle = rest.astype(bf16)
        low = (rest - middle.astype(f32)).astype(bf16)
        return scale * sum(
            jnp.dot(same_group, term, preferred_element_type=f32) for term in (high, middle, low)
        )

    mean = group_means([tiles_ref[t].astype(f32) for t in range(number)])
    centred = [tiles_ref[t].astype(f32) - mean[:, t : t + 1] for t in range(number)]
    spread = lax.rsqrt(group_means([value * value for value in centred]) + 1e-05)
    for t in range(number):
        half = (tiles_ref[t].astype(f32) - mean[:, t : t + 1]) * (0.5 * spread[:, t : t + 1])
        out_ref[t] = (half + half * jnp.tanh(half)).astype(bf16)


def group_norm(tiles):
    number, channels, pixels = tiles.shape
    step = tiles_per_step(number)
    group_width = channels // GROUPS
    group = np.arange(channels) // group_width
    same_group = jnp.asarray(group[:, None] == group[None, :], bf16)
    block = pl.BlockSpec((step, channels, pixels), lambda i: (i, 0, 0))
    return pl.pallas_call(
        functools.partial(norm_kernel, group_width),
        grid=(number // step,),
        in_specs=[pl.BlockSpec((channels, channels), lambda i: (0, 0)), block],
        out_specs=block,
        out_shape=jax.ShapeDtypeStruct(tiles.shape, bf16),
        compiler_params=pltpu.CompilerParams(vmem_limit_bytes=60 * 2**20),
        cost_estimate=pl.CostEstimate(
            flops=20 * tiles.size, bytes_accessed=4 * tiles.size, transcendentals=tiles.size
        ),
        name="group_norm",
    )(same_group, tiles)


def write_columns(values, columns_ref, at):
    channels, pixels = values.shape
    cell = lax.broadcasted_iota(jnp.int32, (channels, pixels), 1)
    column = cell % SIDE
    wide = values.astype(f32)
    for b in range(3):
        if b == 1:
            moved = wide
        else:
            moved = pltpu.roll(wide, (1 - b) % pixels, 1)
            moved = jnp.where(column == (0 if b == 0 else SIDE - 1), 0.0, moved)
        for a in range(3):
            if a == 1:
                shifted = moved
            else:
                shifted = pltpu.roll(moved, ((1 - a) * SIDE) % pixels, 1)
                outside = (cell < SIDE) if a == 0 else (cell >= pixels - SIDE)
                shifted = jnp.where(outside, 0.0, shifted)
            tap = 3 * a + b
            columns_ref[
                tap * channels : (tap + 1) * channels, at * pixels : (at + 1) * pixels
            ] = shifted.astype(values.dtype)


def conv_kernel(
    steps,
    counts_ref,
    own_ref,
    other_ref,
    own_time_ref,
    other_time_ref,
    features_ref,
    normed_ref,
    tiles_ref,
    target_ref,
    predicted_ref,
    keep_ref,
    send_ref,
    keep_time_ref,
    send_time_ref,
    weight,
    time_weight,
    bias,
    sums,
    columns,
    total,
):
    i = pl.program_id(0)
    parts, planes, part_rows, rows = own_ref.shape
    step, channels, pixels = normed_ref.shape
    shards = 2 * planes
    time_rows = own_time_ref.shape[1]
    my_shard, my_peer = lax.axis_index("fsdp"), lax.axis_index("dp")
    count = counts_ref[0, my_peer]
    core, plane, part = my_shard & 1, my_shard >> 1, my_peer & (parts - 1)
    outs = parts * part_rows
    lane = lax.broadcasted_iota(jnp.int32, (outs, LANES), 1)

    @pl.when(i == 0)
    def _():
        for f in range(shards):
            for q in range(parts):
                at = (q ^ part, (f // 2) ^ plane)
                block = jnp.where(core == f % 2, own_ref[at], other_ref[at])
                into = slice(q * part_rows, (q + 1) * part_rows)
                weight[into, f * rows : (f + 1) * rows] = block
            block = jnp.where(
                core == f % 2, own_time_ref[(f // 2) ^ plane], other_time_ref[(f // 2) ^ plane]
            )
            time_weight[f * time_rows : (f + 1) * time_rows, :] = block.astype(f32)
        bias[...] = lax.dot_general(
            time_weight[...].astype(bf16),
            features_ref[...],
            (((0,), (0,)), ((), ())),
            preferred_element_type=f32,
        )
        total[...] = jnp.zeros_like(total)
        sums[...] = jnp.zeros_like(sums)

    @pl.when(i * step < count)
    def _():
        for t in range(step):
            write_columns(normed_ref[t], columns, t)
        conv = jnp.dot(weight[...], columns[...], preferred_element_type=f32)
        errors = []
        error_sums = sums[...]
        for t in range(step):
            slot = i * step + t
            live = slot < count
            tile_bias = jnp.sum(jnp.where(lane == slot, bias[...], 0.0), axis=1, keepdims=True)
            pred32 = tiles_ref[t].astype(f32) + conv[:, t * pixels : (t + 1) * pixels] + tile_bias
            predicted_ref[t] = jnp.where(live, pred32, 0.0).astype(bf16)
            error = jnp.where(
                live, (pred32 - target_ref[t].astype(f32)) * (1.0 / pixels), 0.0
            ).astype(bf16)
            error_sum = jnp.sum(error.astype(f32), axis=1, keepdims=True)
            error_sums = jnp.where(lane == slot, error_sum, error_sums)
            errors.append(error)
        sums[...] = error_sums
        total[...] += lax.dot_general(
            jnp.concatenate(errors, axis=1),
            columns[...],
            (((1,), (1,)), ((), ())),
            preferred_element_type=f32,
        )

    @pl.when(i * step >= count)
    def _():
        predicted_ref[...] = jnp.zeros_like(predicted_ref)

    @pl.when(i == steps - 1)
    def _():
        high = sums[...].astype(bf16)
        low = (sums[...] - high.astype(f32)).astype(bf16)
        time_total = sum(
            lax.dot_general(
                features_ref[...], term, (((1,), (1,)), ((), ())), preferred_element_type=f32
            )
            for term in (high, low)
        )
        for c in range(2):
            for f in range(shards):
                into = keep_ref if f % 2 == c else send_ref
                time_into = keep_time_ref if f % 2 == c else send_time_ref

                @pl.when(core == c)
                def _():
                    at = (f // 2) ^ plane
                    for q in range(parts):
                        here = slice(q * part_rows, (q + 1) * part_rows)
                        into[q ^ part, at] = total[here, f * rows : (f + 1) * rows].astype(bf16)
                    time_into[at] = time_total[f * time_rows : (f + 1) * time_rows].astype(bf16)


def conv_both(counts, own, other, own_time, other_time, features, normed, tiles, targets):
    number, channels, pixels = normed.shape
    parts, planes, part_rows, rows = own.shape
    shards, outs = 2 * planes, parts * part_rows
    depth, emb = shards * rows, features.shape[0]
    step = tiles_per_step(number)
    steps = number // step

    def whole(shape):
        return pl.BlockSpec(shape, lambda i, c: (0,) * len(shape))

    block = pl.BlockSpec((step, channels, pixels), lambda i, c: (i, 0, 0))
    return pl.pallas_call(
        functools.partial(conv_kernel, steps),
        grid_spec=pltpu.PrefetchScalarGridSpec(
            num_scalar_prefetch=1,
            grid=(steps,),
            in_specs=[whole(own.shape)] * 2
            + [whole(own_time.shape)] * 2
            + [whole(features.shape)]
            + [block] * 3,
            out_specs=[block] + [whole(own.shape)] * 2 + [whole(own_time.shape)] * 2,
            scratch_shapes=[
                pltpu.VMEM((outs, depth), bf16),
                pltpu.VMEM((emb, outs), f32),
                pltpu.VMEM((outs, LANES), f32),
                pltpu.VMEM((outs, LANES), f32),
                pltpu.VMEM((depth, step * pixels), bf16),
                pltpu.VMEM((outs, depth), f32),
            ],
        ),
        out_shape=[
            jax.ShapeDtypeStruct(tiles.shape, bf16),
            jax.ShapeDtypeStruct(own.shape, bf16),
            jax.ShapeDtypeStruct(own.shape, bf16),
            jax.ShapeDtypeStruct(own_time.shape, bf16),
            jax.ShapeDtypeStruct(own_time.shape, bf16),
        ],
        compiler_params=pltpu.CompilerParams(vmem_limit_bytes=44 * 2**20),
        cost_estimate=pl.CostEstimate(
            flops=4 * number * pixels * depth * outs, bytes_accessed=8 * tiles.size, transcendentals=0
        ),
        name="conv_both",
    )(counts, own, other, own_time, other_time, features, normed, tiles, targets)


def swap(values, axis, mask):
    pairs = [(i, i ^ mask) for i in range(lax.axis_size(axis))]
    return lax.ppermute(values, axis, pairs)


def bits_of(axis):
    return (lax.axis_size(axis) - 1).bit_length()


def bit_groups(bits):
    return [(at, min(2, bits - at)) for at in range(0, bits, 2)]


def gather_partners(values, axis, low, bits):
    shape = values.shape
    values = values[None]
    for at, width in bit_groups(bits):
        parts = [values] + [swap(values, axis, m << (low + at)) for m in range(1, 1 << width)]
        values = jnp.concatenate(parts)
    return values.reshape((1 << bits,) + shape)


def add_up(parts):
    kept_as = parts[0].dtype
    parts = [part.astype(f32) for part in parts]
    while len(parts) > 1:
        parts = [sum(parts[n : n + 2]) for n in range(0, len(parts), 2)]
    return parts[0].astype(kept_as)


def sum_partners(values, axis, low, bits):
    for at, width in bit_groups(bits):
        parts = [values] + [swap(values, axis, m << (low + at)) for m in range(1, 1 << width)]
        values = add_up(parts)
    return values


def scatter_partners(values, axis, low, bits):
    shape = values.shape[1:]
    for at, width in bit_groups(bits):
        values = values.reshape((-1, 1 << width) + shape)
        parts = [values[:, 0]]
        parts += [swap(values[:, m], axis, m << (low + at)) for m in range(1, 1 << width)]
        values = add_up(parts)
    return values.reshape(shape)


def time_features(timesteps, emb):
    half_width = emb // 2
    frequency = jnp.exp(-math.log(10000.0) * jnp.arange(half_width, dtype=f32) / half_width)
    angles = frequency[:, None] * timesteps.astype(f32)[None, :]
    return jax.nn.silu(jnp.concatenate([jnp.cos(angles), jnp.sin(angles)])).astype(bf16)


def per_device(latents, target_noise, counts, timesteps, conv_master, temb_master):
    tiles = jnp.swapaxes(latents[0], 1, 2)
    targets = jnp.swapaxes(target_noise[0], 1, 2)
    number = tiles.shape[0]
    shards = lax.axis_size("fsdp")
    shard_bits, peer_bits = bits_of("fsdp"), bits_of("dp")
    rows, outs = conv_master.shape
    time_rows = temb_master.shape[0]
    part_bits = max(n for n in range(peer_bits + 1) if outs % (16 << n) == 0)
    parts = 1 << part_bits
    part = lax.axis_index("dp") & (parts - 1)
    plane_bits = shard_bits - 1

    master = conv_master.T.astype(bf16).reshape(parts, outs // parts, rows)
    mine = [lax.dynamic_index_in_dim(master, part ^ m, 0, keepdims=False) for m in range(parts)]
    time_master, first = lax.optimization_barrier((temb_master, mine[0]))
    time_master = time_master.astype(bf16)
    over_planes = gather_partners(first, "fsdp", 1, plane_bits)
    own_time = gather_partners(time_master, "fsdp", 1, plane_bits)
    over_planes, tiles_then = lax.optimization_barrier((over_planes, tiles))
    far = gather_partners(over_planes[1:], "dp", 0, part_bits)
    normed = group_norm(tiles_then)
    own = jnp.concatenate([jnp.stack(mine)[:, None], far], axis=1)
    own, own_time, normed, times = lax.optimization_barrier((own, own_time, normed, timesteps[0]))
    features = time_features(jnp.pad(times, (0, LANES - number)), time_rows * shards)
    other, other_time = swap(own, "fsdp", 1), swap(own_time, "fsdp", 1)

    predicted, keep, send, keep_time, send_time = conv_both(
        counts, own, other, own_time, other_time, features, normed, tiles, targets
    )

    grad = add_up([keep, swap(send, "fsdp", 1)])
    time_grad = add_up([keep_time, swap(send_time, "fsdp", 1)])
    grad, time_grad = lax.optimization_barrier((grad, time_grad))
    grad = scatter_partners(grad, "dp", 0, part_bits)
    for bit in range(part_bits, peer_bits):
        grad = sum_partners(grad, "dp", bit, 1)
    time_grad = scatter_partners(time_grad, "fsdp", 1, plane_bits)
    grad = scatter_partners(grad, "fsdp", 1, plane_bits)
    time_grad = sum_partners(time_grad, "dp", 0, peer_bits)
    grad = gather_partners(grad, "dp", 0, part_bits)
    grad = jnp.concatenate(
        [lax.dynamic_index_in_dim(grad, part ^ q, 0, keepdims=False) for q in range(parts)]
    )
    return (
        jnp.swapaxes(predicted, 1, 2)[None],
        grad.T.astype(f32),
        time_grad.astype(f32),
    )


def solution(mesh):
    placed = (
        P("fsdp", "dp", None, None),
        P("fsdp", "dp", None, None),
        P("fsdp", None),
        P("fsdp", "dp"),
        P("fsdp", None),
        P("fsdp", None),
    )
    return jax.shard_map(
        per_device,
        mesh=mesh,
        in_specs=placed,
        out_specs=(P("fsdp", "dp", None, None), P("fsdp", None), P("fsdp", None)),
        check_vma=False,
    )
```

```python
import functools
import math

import jax
import jax.numpy as jnp
import numpy as np
from jax import lax
from jax.experimental import pallas as pl
from jax.experimental.pallas import tpu as pltpu
from jax.sharding import PartitionSpec as P

GROUPS = 32
SIDE = 16
LANES = 128

bf16 = jnp.bfloat16
f32 = jnp.float32


def tiles_per_step(number):
    return max(size for size in range(1, 6) if number % size == 0)


def norm_kernel(group_width, same_ref, tiles_ref, out_ref):
    same_group = same_ref[...]
    number, channels, pixels = tiles_ref.shape
    scale = 1.0 / (group_width * pixels)
    lane = lax.broadcasted_iota(jnp.int32, (channels, LANES), 1)

    def group_means(values):
        row_sums = jnp.zeros((channels, LANES), f32)
        for t, value in enumerate(values):
            row_sums = jnp.where(lane == t, jnp.sum(value, axis=1, keepdims=True), row_sums)
        high = row_sums.astype(bf16)
        rest = row_sums - high.astype(f32)
        middle = rest.astype(bf16)
        low = (rest - middle.astype(f32)).astype(bf16)
        return scale * sum(
            jnp.dot(same_group, term, preferred_element_type=f32) for term in (high, middle, low)
        )

    mean = group_means([tiles_ref[t].astype(f32) for t in range(number)])
    centred = [tiles_ref[t].astype(f32) - mean[:, t : t + 1] for t in range(number)]
    spread = lax.rsqrt(group_means([value * value for value in centred]) + 1e-05)
    for t in range(number):
        half = (tiles_ref[t].astype(f32) - mean[:, t : t + 1]) * (0.5 * spread[:, t : t + 1])
        out_ref[t] = (half + half * jnp.tanh(half)).astype(bf16)


def group_norm(tiles):
    number, channels, pixels = tiles.shape
    step = tiles_per_step(number)
    group_width = channels // GROUPS
    group = np.arange(channels) // group_width
    same_group = jnp.asarray(group[:, None] == group[None, :], bf16)
    block = pl.BlockSpec((step, channels, pixels), lambda i: (i, 0, 0))
    return pl.pallas_call(
        functools.partial(norm_kernel, group_width),
        grid=(number // step,),
        in_specs=[pl.BlockSpec((channels, channels), lambda i: (0, 0)), block],
        out_specs=block,
        out_shape=jax.ShapeDtypeStruct(tiles.shape, bf16),
        compiler_params=pltpu.CompilerParams(vmem_limit_bytes=60 * 2**20),
        cost_estimate=pl.CostEstimate(
            flops=20 * tiles.size, bytes_accessed=4 * tiles.size, transcendentals=tiles.size
        ),
        name="group_norm",
    )(same_group, tiles)


def write_columns(values, columns_ref, at):
    channels, pixels = values.shape
    cell = lax.broadcasted_iota(jnp.int32, (channels, pixels), 1)
    column = cell % SIDE
    wide = values.astype(f32)
    for b in range(3):
        if b == 1:
            moved = wide
        else:
            moved = pltpu.roll(wide, (1 - b) % pixels, 1)
            moved = jnp.where(column == (0 if b == 0 else SIDE - 1), 0.0, moved)
        for a in range(3):
            if a == 1:
                shifted = moved
            else:
                shifted = pltpu.roll(moved, ((1 - a) * SIDE) % pixels, 1)
                outside = (cell < SIDE) if a == 0 else (cell >= pixels - SIDE)
                shifted = jnp.where(outside, 0.0, shifted)
            tap = 3 * a + b
            columns_ref[
                tap * channels : (tap + 1) * channels, at * pixels : (at + 1) * pixels
            ] = shifted.astype(values.dtype)


def conv_kernel(
    steps,
    counts_ref,
    own_ref,
    other_ref,
    own_time_ref,
    other_time_ref,
    features_ref,
    normed_ref,
    tiles_ref,
    target_ref,
    predicted_ref,
    keep_ref,
    send_ref,
    keep_time_ref,
    send_time_ref,
    weight,
    time_weight,
    bias,
    sums,
    columns,
    total,
):
    i = pl.program_id(0)
    parts, planes, part_rows, rows = own_ref.shape
    step, channels, pixels = normed_ref.shape
    shards = 2 * planes
    time_rows = own_time_ref.shape[1]
    my_shard, my_peer = lax.axis_index("fsdp"), lax.axis_index("dp")
    count = counts_ref[0, my_peer]
    core, plane, part = my_shard & 1, my_shard >> 1, my_peer & (parts - 1)
    outs = parts * part_rows
    lane = lax.broadcasted_iota(jnp.int32, (outs, LANES), 1)

    @pl.when(i == 0)
    def _():
        for f in range(shards):
            for q in range(parts):
                at = (q ^ part, (f // 2) ^ plane)
                block = jnp.where(core == f % 2, own_ref[at], other_ref[at])
                into = slice(q * part_rows, (q + 1) * part_rows)
                weight[into, f * rows : (f + 1) * rows] = block
            block = jnp.where(
                core == f % 2, own_time_ref[(f // 2) ^ plane], other_time_ref[(f // 2) ^ plane]
            )
            time_weight[f * time_rows : (f + 1) * time_rows, :] = block.astype(f32)
        bias[...] = lax.dot_general(
            time_weight[...].astype(bf16),
            features_ref[...],
            (((0,), (0,)), ((), ())),
            preferred_element_type=f32,
        )
        total[...] = jnp.zeros_like(total)
        sums[...] = jnp.zeros_like(sums)

    @pl.when(i * step < count)
    def _():
        for t in range(step):
            write_columns(normed_ref[t], columns, t)
        conv = jnp.dot(weight[...], columns[...], preferred_element_type=f32)
        errors = []
        error_sums = sums[...]
        for t in range(step):
            slot = i * step + t
            live = slot < count
            tile_bias = jnp.sum(jnp.where(lane == slot, bias[...], 0.0), axis=1, keepdims=True)
            pred32 = tiles_ref[t].astype(f32) + conv[:, t * pixels : (t + 1) * pixels] + tile_bias
            predicted_ref[t] = jnp.where(live, pred32, 0.0).astype(bf16)
            error = jnp.where(
                live, (pred32 - target_ref[t].astype(f32)) * (1.0 / pixels), 0.0
            ).astype(bf16)
            error_sum = jnp.sum(error.astype(f32), axis=1, keepdims=True)
            error_sums = jnp.where(lane == slot, error_sum, error_sums)
            errors.append(error)
        sums[...] = error_sums
        total[...] += lax.dot_general(
            jnp.concatenate(errors, axis=1),
            columns[...],
            (((1,), (1,)), ((), ())),
            preferred_element_type=f32,
        )

    @pl.when(i * step >= count)
    def _():
        predicted_ref[...] = jnp.zeros_like(predicted_ref)

    @pl.when(i == steps - 1)
    def _():
        high = sums[...].astype(bf16)
        low = (sums[...] - high.astype(f32)).astype(bf16)
        time_total = sum(
            lax.dot_general(
                features_ref[...], term, (((1,), (1,)), ((), ())), preferred_element_type=f32
            )
            for term in (high, low)
        )
        for c in range(2):
            for f in range(shards):
                into = keep_ref if f % 2 == c else send_ref
                time_into = keep_time_ref if f % 2 == c else send_time_ref

                @pl.when(core == c)
                def _():
                    at = (f // 2) ^ plane
                    for q in range(parts):
                        here = slice(q * part_rows, (q + 1) * part_rows)
                        into[q ^ part, at] = total[here, f * rows : (f + 1) * rows].astype(bf16)
                    time_into[at] = time_total[f * time_rows : (f + 1) * time_rows].astype(bf16)


def conv_both(counts, own, other, own_time, other_time, features, normed, tiles, targets):
    number, channels, pixels = normed.shape
    parts, planes, part_rows, rows = own.shape
    shards, outs = 2 * planes, parts * part_rows
    depth, emb = shards * rows, features.shape[0]
    step = tiles_per_step(number)
    steps = number // step

    def whole(shape):
        return pl.BlockSpec(shape, lambda i, c: (0,) * len(shape))

    block = pl.BlockSpec((step, channels, pixels), lambda i, c: (i, 0, 0))
    return pl.pallas_call(
        functools.partial(conv_kernel, steps),
        grid_spec=pltpu.PrefetchScalarGridSpec(
            num_scalar_prefetch=1,
            grid=(steps,),
            in_specs=[whole(own.shape)] * 2
            + [whole(own_time.shape)] * 2
            + [whole(features.shape)]
            + [block] * 3,
            out_specs=[block] + [whole(own.shape)] * 2 + [whole(own_time.shape)] * 2,
            scratch_shapes=[
                pltpu.VMEM((outs, depth), bf16),
                pltpu.VMEM((emb, outs), f32),
                pltpu.VMEM((outs, LANES), f32),
                pltpu.VMEM((outs, LANES), f32),
                pltpu.VMEM((depth, step * pixels), bf16),
                pltpu.VMEM((outs, depth), f32),
            ],
        ),
        out_shape=[
            jax.ShapeDtypeStruct(tiles.shape, bf16),
            jax.ShapeDtypeStruct(own.shape, bf16),
            jax.ShapeDtypeStruct(own.shape, bf16),
            jax.ShapeDtypeStruct(own_time.shape, bf16),
            jax.ShapeDtypeStruct(own_time.shape, bf16),
        ],
        compiler_params=pltpu.CompilerParams(vmem_limit_bytes=44 * 2**20),
        cost_estimate=pl.CostEstimate(
            flops=4 * number * pixels * depth * outs, bytes_accessed=8 * tiles.size, transcendentals=0
        ),
        name="conv_both",
    )(counts, own, other, own_time, other_time, features, normed, tiles, targets)


def swap(values, axis, mask):
    pairs = [(i, i ^ mask) for i in range(lax.axis_size(axis))]
    return lax.ppermute(values, axis, pairs)


def bits_of(axis):
    return (lax.axis_size(axis) - 1).bit_length()


def bit_groups(bits, most):
    return [(at, min(most, bits - at)) for at in range(0, bits, most)]


def gather_partners(values, axis, low, bits, most=2):
    shape = values.shape
    values = values[None]
    for at, width in bit_groups(bits, most):
        parts = [values] + [swap(values, axis, m << (low + at)) for m in range(1, 1 << width)]
        values = jnp.concatenate(parts)
    return values.reshape((1 << bits,) + shape)


def add_up(parts):
    kept_as = parts[0].dtype
    parts = [part.astype(f32) for part in parts]
    while len(parts) > 1:
        parts = [sum(parts[n : n + 2]) for n in range(0, len(parts), 2)]
    return parts[0].astype(kept_as)


def sum_partners(values, axis, low, bits, most=2):
    for at, width in bit_groups(bits, most):
        parts = [values] + [swap(values, axis, m << (low + at)) for m in range(1, 1 << width)]
        values = add_up(parts)
    return values


def scatter_partners(values, axis, low, bits, most=2):
    shape = values.shape[1:]
    for at, width in bit_groups(bits, most):
        values = values.reshape((-1, 1 << width) + shape)
        parts = [values[:, 0]]
        parts += [swap(values[:, m], axis, m << (low + at)) for m in range(1, 1 << width)]
        values = add_up(parts)
    return values.reshape(shape)


def time_features(timesteps, emb):
    half_width = emb // 2
    frequency = jnp.exp(-math.log(10000.0) * jnp.arange(half_width, dtype=f32) / half_width)
    angles = frequency[:, None] * timesteps.astype(f32)[None, :]
    return jax.nn.silu(jnp.concatenate([jnp.cos(angles), jnp.sin(angles)])).astype(bf16)


def per_device(latents, target_noise, counts, timesteps, conv_master, temb_master):
    tiles = jnp.swapaxes(latents[0], 1, 2)
    targets = jnp.swapaxes(target_noise[0], 1, 2)
    number = tiles.shape[0]
    shards = lax.axis_size("fsdp")
    shard_bits, peer_bits = bits_of("fsdp"), bits_of("dp")
    rows, outs = conv_master.shape
    time_rows = temb_master.shape[0]
    part_bits = max(n for n in range(peer_bits + 1) if outs % (16 << n) == 0)
    parts = 1 << part_bits
    part = lax.axis_index("dp") & (parts - 1)
    plane_bits = shard_bits - 1

    master = conv_master.T.astype(bf16).reshape(parts, outs // parts, rows)
    mine = [lax.dynamic_index_in_dim(master, part ^ m, 0, keepdims=False) for m in range(parts)]
    time_master, first = lax.optimization_barrier((temb_master, mine[0]))
    time_master = time_master.astype(bf16)
    over_planes = gather_partners(first, "fsdp", 1, plane_bits)
    own_time = gather_partners(time_master, "fsdp", 1, plane_bits, most=1)
    over_planes, tiles_then = lax.optimization_barrier((over_planes, tiles))
    far = gather_partners(over_planes[1:], "dp", 0, part_bits)
    normed = group_norm(tiles_then)
    own = jnp.concatenate([jnp.stack(mine)[:, None], far], axis=1)
    own, own_time, normed, times = lax.optimization_barrier((own, own_time, normed, timesteps[0]))
    features = time_features(jnp.pad(times, (0, LANES - number)), time_rows * shards)
    other, other_time = swap(own, "fsdp", 1), swap(own_time, "fsdp", 1)

    predicted, keep, send, keep_time, send_time = conv_both(
        counts, own, other, own_time, other_time, features, normed, tiles, targets
    )

    grad = add_up([keep, swap(send, "fsdp", 1)])
    grad, send_time = lax.optimization_barrier((grad, send_time))
    time_grad = add_up([keep_time, swap(send_time, "fsdp", 1)])
    grad = scatter_partners(grad, "dp", 0, part_bits)
    for bit in range(part_bits, peer_bits):
        grad = sum_partners(grad, "dp", bit, 1)
    time_grad = scatter_partners(time_grad, "fsdp", 1, plane_bits)
    grad, time_grad = lax.optimization_barrier((grad, time_grad))
    grad = scatter_partners(grad, "fsdp", 1, plane_bits)
    time_grad = sum_partners(time_grad, "dp", 0, peer_bits // 2, most=1)
    grad, time_grad = lax.optimization_barrier((grad, time_grad))
    grad = gather_partners(grad, "dp", 0, part_bits)
    time_grad = sum_partners(time_grad, "dp", peer_bits // 2, peer_bits - peer_bits // 2, most=1)
    grad = jnp.concatenate(
        [lax.dynamic_index_in_dim(grad, part ^ q, 0, keepdims=False) for q in range(parts)]
    )
    return (
        jnp.swapaxes(predicted, 1, 2)[None],
        grad.T.astype(f32),
        time_grad.astype(f32),
    )


def solution(mesh):
    placed = (
        P("fsdp", "dp", None, None),
        P("fsdp", "dp", None, None),
        P("fsdp", None),
        P("fsdp", "dp"),
        P("fsdp", None),
        P("fsdp", None),
    )
    return jax.shard_map(
        per_device,
        mesh=mesh,
        in_specs=placed,
        out_specs=(P("fsdp", "dp", None, None), P("fsdp", None), P("fsdp", None)),
        check_vma=False,
    )
```

```python
import functools
import math

import jax
import jax.numpy as jnp
import numpy as np
from jax import lax
from jax.experimental import pallas as pl
from jax.experimental.pallas import tpu as pltpu
from jax.sharding import PartitionSpec as P

GROUPS = 32
SIDE = 16
LANES = 128

bf16 = jnp.bfloat16
f32 = jnp.float32


def tiles_per_step(number):
    return max(size for size in range(1, 6) if number % size == 0)


def norm_kernel(group_width, same_ref, tiles_ref, out_ref):
    same_group = same_ref[...]
    number, channels, pixels = tiles_ref.shape
    scale = 1.0 / (group_width * pixels)
    lane = lax.broadcasted_iota(jnp.int32, (channels, LANES), 1)

    def group_means(values):
        row_sums = jnp.zeros((channels, LANES), f32)
        for t, value in enumerate(values):
            row_sums = jnp.where(lane == t, jnp.sum(value, axis=1, keepdims=True), row_sums)
        high = row_sums.astype(bf16)
        rest = row_sums - high.astype(f32)
        middle = rest.astype(bf16)
        low = (rest - middle.astype(f32)).astype(bf16)
        return scale * sum(
            jnp.dot(same_group, term, preferred_element_type=f32) for term in (high, middle, low)
        )

    mean = group_means([tiles_ref[t].astype(f32) for t in range(number)])
    centred = [tiles_ref[t].astype(f32) - mean[:, t : t + 1] for t in range(number)]
    spread = lax.rsqrt(group_means([value * value for value in centred]) + 1e-05)
    for t in range(number):
        half = (tiles_ref[t].astype(f32) - mean[:, t : t + 1]) * (0.5 * spread[:, t : t + 1])
        out_ref[t] = (half + half * jnp.tanh(half)).astype(bf16)


def group_norm(tiles):
    number, channels, pixels = tiles.shape
    step = tiles_per_step(number)
    group_width = channels // GROUPS
    group = np.arange(channels) // group_width
    same_group = jnp.asarray(group[:, None] == group[None, :], bf16)
    block = pl.BlockSpec((step, channels, pixels), lambda i: (i, 0, 0))
    return pl.pallas_call(
        functools.partial(norm_kernel, group_width),
        grid=(number // step,),
        in_specs=[pl.BlockSpec((channels, channels), lambda i: (0, 0)), block],
        out_specs=block,
        out_shape=jax.ShapeDtypeStruct(tiles.shape, bf16),
        compiler_params=pltpu.CompilerParams(vmem_limit_bytes=60 * 2**20),
        cost_estimate=pl.CostEstimate(
            flops=20 * tiles.size, bytes_accessed=4 * tiles.size, transcendentals=tiles.size
        ),
        name="group_norm",
    )(same_group, tiles)


def write_columns(values, columns_ref, at):
    channels, pixels = values.shape
    cell = lax.broadcasted_iota(jnp.int32, (channels, pixels), 1)
    column = cell % SIDE
    wide = values.astype(f32)
    for b in range(3):
        if b == 1:
            moved = wide
        else:
            moved = pltpu.roll(wide, (1 - b) % pixels, 1)
            moved = jnp.where(column == (0 if b == 0 else SIDE - 1), 0.0, moved)
        for a in range(3):
            if a == 1:
                shifted = moved
            else:
                shifted = pltpu.roll(moved, ((1 - a) * SIDE) % pixels, 1)
                outside = (cell < SIDE) if a == 0 else (cell >= pixels - SIDE)
                shifted = jnp.where(outside, 0.0, shifted)
            tap = 3 * a + b
            columns_ref[
                tap * channels : (tap + 1) * channels, at * pixels : (at + 1) * pixels
            ] = shifted.astype(values.dtype)


def conv_kernel(
    steps,
    counts_ref,
    own_ref,
    other_ref,
    own_time_ref,
    other_time_ref,
    features_ref,
    normed_ref,
    tiles_ref,
    target_ref,
    predicted_ref,
    keep_ref,
    send_ref,
    keep_time_ref,
    send_time_ref,
    weight,
    time_weight,
    bias,
    sums,
    columns,
    total,
):
    i = pl.program_id(0)
    parts, planes, part_rows, rows = own_ref.shape
    step, channels, pixels = normed_ref.shape
    shards = 2 * planes
    time_rows = own_time_ref.shape[1]
    my_shard, my_peer = lax.axis_index("fsdp"), lax.axis_index("dp")
    count = counts_ref[0, my_peer]
    core, plane, part = my_shard & 1, my_shard >> 1, my_peer & (parts - 1)
    outs = parts * part_rows
    lane = lax.broadcasted_iota(jnp.int32, (outs, LANES), 1)

    @pl.when(i == 0)
    def _():
        for f in range(shards):
            for q in range(parts):
                at = (q ^ part, (f // 2) ^ plane)
                block = jnp.where(core == f % 2, own_ref[at], other_ref[at])
                into = slice(q * part_rows, (q + 1) * part_rows)
                weight[into, f * rows : (f + 1) * rows] = block
            block = jnp.where(
                core == f % 2, own_time_ref[(f // 2) ^ plane], other_time_ref[(f // 2) ^ plane]
            )
            time_weight[f * time_rows : (f + 1) * time_rows, :] = block.astype(f32)
        bias[...] = lax.dot_general(
            time_weight[...].astype(bf16),
            features_ref[...],
            (((0,), (0,)), ((), ())),
            preferred_element_type=f32,
        )
        total[...] = jnp.zeros_like(total)
        sums[...] = jnp.zeros_like(sums)

    @pl.when(i * step < count)
    def _():
        for t in range(step):
            write_columns(normed_ref[t], columns, t)
        conv = jnp.dot(weight[...], columns[...], preferred_element_type=f32)
        errors = []
        error_sums = sums[...]
        for t in range(step):
            slot = i * step + t
            live = slot < count
            tile_bias = jnp.sum(jnp.where(lane == slot, bias[...], 0.0), axis=1, keepdims=True)
            pred32 = tiles_ref[t].astype(f32) + conv[:, t * pixels : (t + 1) * pixels] + tile_bias
            predicted_ref[t] = jnp.where(live, pred32, 0.0).astype(bf16)
            error = jnp.where(
                live, (pred32 - target_ref[t].astype(f32)) * (1.0 / pixels), 0.0
            ).astype(bf16)
            error_sum = jnp.sum(error.astype(f32), axis=1, keepdims=True)
            error_sums = jnp.where(lane == slot, error_sum, error_sums)
            errors.append(error)
        sums[...] = error_sums
        total[...] += lax.dot_general(
            jnp.concatenate(errors, axis=1),
            columns[...],
            (((1,), (1,)), ((), ())),
            preferred_element_type=f32,
        )

    @pl.when(i * step >= count)
    def _():
        predicted_ref[...] = jnp.zeros_like(predicted_ref)

    @pl.when(i == steps - 1)
    def _():
        high = sums[...].astype(bf16)
        low = (sums[...] - high.astype(f32)).astype(bf16)
        time_total = sum(
            lax.dot_general(
                features_ref[...], term, (((1,), (1,)), ((), ())), preferred_element_type=f32
            )
            for term in (high, low)
        )
        for c in range(2):
            for f in range(shards):
                into = keep_ref if f % 2 == c else send_ref
                time_into = keep_time_ref if f % 2 == c else send_time_ref

                @pl.when(core == c)
                def _():
                    at = (f // 2) ^ plane
                    for q in range(parts):
                        here = slice(q * part_rows, (q + 1) * part_rows)
                        into[q ^ part, at] = total[here, f * rows : (f + 1) * rows].astype(bf16)
                    time_into[at] = time_total[f * time_rows : (f + 1) * time_rows].astype(bf16)


def conv_both(counts, own, other, own_time, other_time, features, normed, tiles, targets):
    number, channels, pixels = normed.shape
    parts, planes, part_rows, rows = own.shape
    shards, outs = 2 * planes, parts * part_rows
    depth, emb = shards * rows, features.shape[0]
    step = tiles_per_step(number)
    steps = number // step

    def whole(shape):
        return pl.BlockSpec(shape, lambda i, c: (0,) * len(shape))

    block = pl.BlockSpec((step, channels, pixels), lambda i, c: (i, 0, 0))
    return pl.pallas_call(
        functools.partial(conv_kernel, steps),
        grid_spec=pltpu.PrefetchScalarGridSpec(
            num_scalar_prefetch=1,
            grid=(steps,),
            in_specs=[whole(own.shape)] * 2
            + [whole(own_time.shape)] * 2
            + [whole(features.shape)]
            + [block] * 3,
            out_specs=[block] + [whole(own.shape)] * 2 + [whole(own_time.shape)] * 2,
            scratch_shapes=[
                pltpu.VMEM((outs, depth), bf16),
                pltpu.VMEM((emb, outs), f32),
                pltpu.VMEM((outs, LANES), f32),
                pltpu.VMEM((outs, LANES), f32),
                pltpu.VMEM((depth, step * pixels), bf16),
                pltpu.VMEM((outs, depth), f32),
            ],
        ),
        out_shape=[
            jax.ShapeDtypeStruct(tiles.shape, bf16),
            jax.ShapeDtypeStruct(own.shape, bf16),
            jax.ShapeDtypeStruct(own.shape, bf16),
            jax.ShapeDtypeStruct(own_time.shape, bf16),
            jax.ShapeDtypeStruct(own_time.shape, bf16),
        ],
        compiler_params=pltpu.CompilerParams(vmem_limit_bytes=44 * 2**20),
        cost_estimate=pl.CostEstimate(
            flops=4 * number * pixels * depth * outs, bytes_accessed=8 * tiles.size, transcendentals=0
        ),
        name="conv_both",
    )(counts, own, other, own_time, other_time, features, normed, tiles, targets)


def swap(values, axis, mask):
    pairs = [(i, i ^ mask) for i in range(lax.axis_size(axis))]
    return lax.ppermute(values, axis, pairs)


def bits_of(axis):
    return (lax.axis_size(axis) - 1).bit_length()


def bit_groups(bits, most):
    return [(at, min(most, bits - at)) for at in range(0, bits, most)]


def gather_partners(values, axis, low, bits, most=2):
    shape = values.shape
    values = values[None]
    for at, width in reversed(bit_groups(bits, most)):
        parts = [values] + [swap(values, axis, m << (low + at)) for m in range(1, 1 << width)]
        values = jnp.stack(parts, axis=1).reshape((-1,) + shape)
    return values


def add_up(parts):
    kept_as = parts[0].dtype
    parts = [part.astype(f32) for part in parts]
    while len(parts) > 1:
        parts = [sum(parts[n : n + 2]) for n in range(0, len(parts), 2)]
    return parts[0].astype(kept_as)


def sum_partners(values, axis, low, bits, most=2):
    for at, width in bit_groups(bits, most):
        parts = [values] + [swap(values, axis, m << (low + at)) for m in range(1, 1 << width)]
        values = add_up(parts)
    return values


def scatter_partners(values, axis, low, bits, most=2):
    shape = values.shape[1:]
    for at, width in bit_groups(bits, most):
        values = values.reshape((-1, 1 << width) + shape)
        parts = [values[:, 0]]
        parts += [swap(values[:, m], axis, m << (low + at)) for m in range(1, 1 << width)]
        values = add_up(parts)
    return values.reshape(shape)


def time_features(timesteps, emb):
    half_width = emb // 2
    frequency = jnp.exp(-math.log(10000.0) * jnp.arange(half_width, dtype=f32) / half_width)
    angles = frequency[:, None] * timesteps.astype(f32)[None, :]
    return jax.nn.silu(jnp.concatenate([jnp.cos(angles), jnp.sin(angles)])).astype(bf16)


def per_device(latents, target_noise, counts, timesteps, conv_master, temb_master):
    tiles = jnp.swapaxes(latents[0], 1, 2)
    targets = jnp.swapaxes(target_noise[0], 1, 2)
    number = tiles.shape[0]
    shards = lax.axis_size("fsdp")
    shard_bits, peer_bits = bits_of("fsdp"), bits_of("dp")
    rows, outs = conv_master.shape
    time_rows = temb_master.shape[0]
    part_bits = max(n for n in range(peer_bits + 1) if outs % (16 << n) == 0)
    parts = 1 << part_bits
    part = lax.axis_index("dp") & (parts - 1)
    plane_bits = shard_bits - 1

    master = conv_master.T.astype(bf16).reshape(parts, outs // parts, rows)
    mine = [lax.dynamic_index_in_dim(master, part ^ m, 0, keepdims=False) for m in range(parts)]
    time_master, first = lax.optimization_barrier((temb_master, mine[0]))
    time_master = time_master.astype(bf16)
    over_planes = gather_partners(first, "fsdp", 1, plane_bits)
    near_bits = plane_bits // 2
    far_time = gather_partners(time_master, "fsdp", 1 + near_bits, plane_bits - near_bits, most=1)
    over_planes, far_time, tiles_then = lax.optimization_barrier((over_planes, far_time, tiles))
    far = gather_partners(over_planes[1:], "dp", 0, part_bits)
    own_time = gather_partners(far_time, "fsdp", 1, near_bits, most=1)
    own_time = own_time.swapaxes(0, 1).reshape((-1,) + time_master.shape)
    normed = group_norm(tiles_then)
    own = jnp.concatenate([jnp.stack(mine)[:, None], far], axis=1)
    own, own_time, normed, times = lax.optimization_barrier((own, own_time, normed, timesteps[0]))
    features = time_features(jnp.pad(times, (0, LANES - number)), time_rows * shards)
    other, other_time = swap(own, "fsdp", 1), swap(own_time, "fsdp", 1)

    predicted, keep, send, keep_time, send_time = conv_both(
        counts, own, other, own_time, other_time, features, normed, tiles, targets
    )

    grad = add_up([keep, swap(send, "fsdp", 1)])
    time_grad = add_up([keep_time, swap(send_time, "fsdp", 1)])
    grad, time_grad = lax.optimization_barrier((grad, time_grad))
    grad = scatter_partners(grad, "dp", 0, part_bits)
    for bit in range(part_bits, peer_bits):
        grad = sum_partners(grad, "dp", bit, 1)
    time_grad = scatter_partners(time_grad, "fsdp", 1, plane_bits)
    grad = scatter_partners(grad, "fsdp", 1, plane_bits)
    time_grad = sum_partners(time_grad, "dp", 0, peer_bits)
    grad = gather_partners(grad, "dp", 0, part_bits)
    grad = jnp.concatenate(
        [lax.dynamic_index_in_dim(grad, part ^ q, 0, keepdims=False) for q in range(parts)]
    )
    return (
        jnp.swapaxes(predicted, 1, 2)[None],
        grad.T.astype(f32),
        time_grad.astype(f32),
    )


def solution(mesh):
    placed = (
        P("fsdp", "dp", None, None),
        P("fsdp", "dp", None, None),
        P("fsdp", None),
        P("fsdp", "dp"),
        P("fsdp", None),
        P("fsdp", None),
    )
    return jax.shard_map(
        per_device,
        mesh=mesh,
        in_specs=placed,
        out_specs=(P("fsdp", "dp", None, None), P("fsdp", None), P("fsdp", None)),
        check_vma=False,
    )
```

```python
import functools
import math

import jax
import jax.numpy as jnp
import numpy as np
from jax import lax
from jax.experimental import pallas as pl
from jax.experimental.pallas import tpu as pltpu
from jax.sharding import PartitionSpec as P

GROUPS = 32
SIDE = 16
LANES = 128

bf16 = jnp.bfloat16
f32 = jnp.float32


def tiles_per_step(number):
    return max(size for size in range(1, 6) if number % size == 0)


def norm_kernel(group_width, same_ref, tiles_ref, *refs):
    out_ref = refs[-1]
    same_group = same_ref[...]
    number, channels, pixels = tiles_ref.shape
    scale = 1.0 / (group_width * pixels)
    lane = lax.broadcasted_iota(jnp.int32, (channels, LANES), 1)

    def group_means(values):
        row_sums = jnp.zeros((channels, LANES), f32)
        for t, value in enumerate(values):
            row_sums = jnp.where(lane == t, jnp.sum(value, axis=1, keepdims=True), row_sums)
        high = row_sums.astype(bf16)
        rest = row_sums - high.astype(f32)
        middle = rest.astype(bf16)
        low = (rest - middle.astype(f32)).astype(bf16)
        return scale * sum(
            jnp.dot(same_group, term, preferred_element_type=f32) for term in (high, middle, low)
        )

    mean = group_means([tiles_ref[t].astype(f32) for t in range(number)])
    centred = [tiles_ref[t].astype(f32) - mean[:, t : t + 1] for t in range(number)]
    spread = lax.rsqrt(group_means([value * value for value in centred]) + 1e-05)
    for t in range(number):
        half = (tiles_ref[t].astype(f32) - mean[:, t : t + 1]) * (0.5 * spread[:, t : t + 1])
        out_ref[t] = (half + half * jnp.tanh(half)).astype(bf16)


def group_norm(tiles, first, last, into=None):
    number, channels, pixels = tiles.shape
    step = tiles_per_step(number)
    group_width = channels // GROUPS
    group = np.arange(channels) // group_width
    same_group = jnp.asarray(group[:, None] == group[None, :], bf16)
    block = pl.BlockSpec((step, channels, pixels), lambda i: (i + first, 0, 0))
    size = (last - first) * step * channels * pixels
    operands, specs = [same_group, tiles], [pl.BlockSpec((channels, channels), lambda i: (0, 0)), block]
    if into is not None:
        operands, specs = operands + [into], specs + [pl.BlockSpec(memory_space=pl.ANY)]
    return pl.pallas_call(
        functools.partial(norm_kernel, group_width),
        grid=(last - first,),
        in_specs=specs,
        out_specs=block,
        out_shape=jax.ShapeDtypeStruct(tiles.shape, bf16),
        input_output_aliases={} if into is None else {2: 0},
        compiler_params=pltpu.CompilerParams(vmem_limit_bytes=60 * 2**20),
        cost_estimate=pl.CostEstimate(
            flops=20 * size, bytes_accessed=4 * size, transcendentals=size
        ),
        name="group_norm",
    )(*operands)


def write_columns(values, columns_ref, at):
    channels, pixels = values.shape
    cell = lax.broadcasted_iota(jnp.int32, (channels, pixels), 1)
    column = cell % SIDE
    wide = values.astype(f32)
    for b in range(3):
        if b == 1:
            moved = wide
        else:
            moved = pltpu.roll(wide, (1 - b) % pixels, 1)
            moved = jnp.where(column == (0 if b == 0 else SIDE - 1), 0.0, moved)
        for a in range(3):
            if a == 1:
                shifted = moved
            else:
                shifted = pltpu.roll(moved, ((1 - a) * SIDE) % pixels, 1)
                outside = (cell < SIDE) if a == 0 else (cell >= pixels - SIDE)
                shifted = jnp.where(outside, 0.0, shifted)
            tap = 3 * a + b
            columns_ref[
                tap * channels : (tap + 1) * channels, at * pixels : (at + 1) * pixels
            ] = shifted.astype(values.dtype)


def conv_kernel(
    steps,
    counts_ref,
    own_ref,
    other_ref,
    own_time_ref,
    other_time_ref,
    features_ref,
    normed_ref,
    tiles_ref,
    target_ref,
    predicted_ref,
    keep_ref,
    send_ref,
    keep_time_ref,
    send_time_ref,
    weight,
    time_weight,
    bias,
    sums,
    columns,
    total,
):
    i = pl.program_id(0)
    parts, planes, part_rows, rows = own_ref.shape
    step, channels, pixels = normed_ref.shape
    shards = 2 * planes
    time_rows = own_time_ref.shape[1]
    my_shard, my_peer = lax.axis_index("fsdp"), lax.axis_index("dp")
    count = counts_ref[0, my_peer]
    core, plane, part = my_shard & 1, my_shard >> 1, my_peer & (parts - 1)
    outs = parts * part_rows
    lane = lax.broadcasted_iota(jnp.int32, (outs, LANES), 1)

    @pl.when(i == 0)
    def _():
        for f in range(shards):
            for q in range(parts):
                at = (q ^ part, (f // 2) ^ plane)
                block = jnp.where(core == f % 2, own_ref[at], other_ref[at])
                into = slice(q * part_rows, (q + 1) * part_rows)
                weight[into, f * rows : (f + 1) * rows] = block
            block = jnp.where(
                core == f % 2, own_time_ref[(f // 2) ^ plane], other_time_ref[(f // 2) ^ plane]
            )
            time_weight[f * time_rows : (f + 1) * time_rows, :] = block.astype(f32)
        bias[...] = lax.dot_general(
            time_weight[...].astype(bf16),
            features_ref[...],
            (((0,), (0,)), ((), ())),
            preferred_element_type=f32,
        )
        total[...] = jnp.zeros_like(total)
        sums[...] = jnp.zeros_like(sums)

    @pl.when(i * step < count)
    def _():
        for t in range(step):
            write_columns(normed_ref[t], columns, t)
        conv = jnp.dot(weight[...], columns[...], preferred_element_type=f32)
        errors = []
        error_sums = sums[...]
        for t in range(step):
            slot = i * step + t
            live = slot < count
            tile_bias = jnp.sum(jnp.where(lane == slot, bias[...], 0.0), axis=1, keepdims=True)
            pred32 = tiles_ref[t].astype(f32) + conv[:, t * pixels : (t + 1) * pixels] + tile_bias
            predicted_ref[t] = jnp.where(live, pred32, 0.0).astype(bf16)
            error = jnp.where(
                live, (pred32 - target_ref[t].astype(f32)) * (1.0 / pixels), 0.0
            ).astype(bf16)
            error_sum = jnp.sum(error.astype(f32), axis=1, keepdims=True)
            error_sums = jnp.where(lane == slot, error_sum, error_sums)
            errors.append(error)
        sums[...] = error_sums
        total[...] += lax.dot_general(
            jnp.concatenate(errors, axis=1),
            columns[...],
            (((1,), (1,)), ((), ())),
            preferred_element_type=f32,
        )

    @pl.when(i * step >= count)
    def _():
        predicted_ref[...] = jnp.zeros_like(predicted_ref)

    @pl.when(i == steps - 1)
    def _():
        high = sums[...].astype(bf16)
        low = (sums[...] - high.astype(f32)).astype(bf16)
        time_total = sum(
            lax.dot_general(
                features_ref[...], term, (((1,), (1,)), ((), ())), preferred_element_type=f32
            )
            for term in (high, low)
        )
        for c in range(2):
            for f in range(shards):
                into = keep_ref if f % 2 == c else send_ref
                time_into = keep_time_ref if f % 2 == c else send_time_ref

                @pl.when(core == c)
                def _():
                    at = (f // 2) ^ plane
                    for q in range(parts):
                        here = slice(q * part_rows, (q + 1) * part_rows)
                        into[q ^ part, at] = total[here, f * rows : (f + 1) * rows].astype(bf16)
                    time_into[at] = time_total[f * time_rows : (f + 1) * time_rows].astype(bf16)


def conv_both(counts, own, other, own_time, other_time, features, normed, tiles, targets):
    number, channels, pixels = normed.shape
    parts, planes, part_rows, rows = own.shape
    shards, outs = 2 * planes, parts * part_rows
    depth, emb = shards * rows, features.shape[0]
    step = tiles_per_step(number)
    steps = number // step

    def whole(shape):
        return pl.BlockSpec(shape, lambda i, c: (0,) * len(shape))

    block = pl.BlockSpec((step, channels, pixels), lambda i, c: (i, 0, 0))
    return pl.pallas_call(
        functools.partial(conv_kernel, steps),
        grid_spec=pltpu.PrefetchScalarGridSpec(
            num_scalar_prefetch=1,
            grid=(steps,),
            in_specs=[whole(own.shape)] * 2
            + [whole(own_time.shape)] * 2
            + [whole(features.shape)]
            + [block] * 3,
            out_specs=[block] + [whole(own.shape)] * 2 + [whole(own_time.shape)] * 2,
            scratch_shapes=[
                pltpu.VMEM((outs, depth), bf16),
                pltpu.VMEM((emb, outs), f32),
                pltpu.VMEM((outs, LANES), f32),
                pltpu.VMEM((outs, LANES), f32),
                pltpu.VMEM((depth, step * pixels), bf16),
                pltpu.VMEM((outs, depth), f32),
            ],
        ),
        out_shape=[
            jax.ShapeDtypeStruct(tiles.shape, bf16),
            jax.ShapeDtypeStruct(own.shape, bf16),
            jax.ShapeDtypeStruct(own.shape, bf16),
            jax.ShapeDtypeStruct(own_time.shape, bf16),
            jax.ShapeDtypeStruct(own_time.shape, bf16),
        ],
        compiler_params=pltpu.CompilerParams(vmem_limit_bytes=44 * 2**20),
        cost_estimate=pl.CostEstimate(
            flops=4 * number * pixels * depth * outs, bytes_accessed=8 * tiles.size, transcendentals=0
        ),
        name="conv_both",
    )(counts, own, other, own_time, other_time, features, normed, tiles, targets)


def swap(values, axis, mask):
    pairs = [(i, i ^ mask) for i in range(lax.axis_size(axis))]
    return lax.ppermute(values, axis, pairs)


def bits_of(axis):
    return (lax.axis_size(axis) - 1).bit_length()


def bit_groups(bits, most):
    return [(at, min(most, bits - at)) for at in range(0, bits, most)]


def gather_partners(values, axis, low, bits, most=2):
    shape = values.shape
    values = values[None]
    for at, width in reversed(bit_groups(bits, most)):
        parts = [values] + [swap(values, axis, m << (low + at)) for m in range(1, 1 << width)]
        values = jnp.stack(parts, axis=1).reshape((-1,) + shape)
    return values


def add_up(parts):
    kept_as = parts[0].dtype
    parts = [part.astype(f32) for part in parts]
    while len(parts) > 1:
        parts = [sum(parts[n : n + 2]) for n in range(0, len(parts), 2)]
    return parts[0].astype(kept_as)


def sum_partners(values, axis, low, bits, most=2):
    for at, width in bit_groups(bits, most):
        parts = [values] + [swap(values, axis, m << (low + at)) for m in range(1, 1 << width)]
        values = add_up(parts)
    return values


def scatter_partners(values, axis, low, bits, most=2):
    shape = values.shape[1:]
    for at, width in bit_groups(bits, most):
        values = values.reshape((-1, 1 << width) + shape)
        parts = [values[:, 0]]
        parts += [swap(values[:, m], axis, m << (low + at)) for m in range(1, 1 << width)]
        values = add_up(parts)
    return values.reshape(shape)


def time_features(timesteps, emb):
    half_width = emb // 2
    frequency = jnp.exp(-math.log(10000.0) * jnp.arange(half_width, dtype=f32) / half_width)
    angles = frequency[:, None] * timesteps.astype(f32)[None, :]
    return jax.nn.silu(jnp.concatenate([jnp.cos(angles), jnp.sin(angles)])).astype(bf16)


def per_device(latents, target_noise, counts, timesteps, conv_master, temb_master):
    tiles = jnp.swapaxes(latents[0], 1, 2)
    targets = jnp.swapaxes(target_noise[0], 1, 2)
    number = tiles.shape[0]
    shards = lax.axis_size("fsdp")
    shard_bits, peer_bits = bits_of("fsdp"), bits_of("dp")
    rows, outs = conv_master.shape
    time_rows = temb_master.shape[0]
    part_bits = max(n for n in range(peer_bits + 1) if outs % (16 << n) == 0)
    parts = 1 << part_bits
    part = lax.axis_index("dp") & (parts - 1)
    plane_bits = shard_bits - 1

    master = conv_master.T.astype(bf16).reshape(parts, outs // parts, rows)
    mine = [lax.dynamic_index_in_dim(master, part ^ m, 0, keepdims=False) for m in range(parts)]
    time_master, first = lax.optimization_barrier((temb_master, mine[0]))
    time_master = time_master.astype(bf16)
    over_planes = gather_partners(first, "fsdp", 1, plane_bits)
    near_bits = plane_bits // 2
    far_time = gather_partners(time_master, "fsdp", 1 + near_bits, plane_bits - near_bits, most=1)
    steps = number // tiles_per_step(number)
    head = steps // 3
    tiles_then, first = lax.optimization_barrier((tiles, first))
    normed = group_norm(tiles_then, 0, head) if head else None
    over_planes, normed, tiles_then = lax.optimization_barrier((over_planes, normed, tiles))
    far_time, tiles_then = lax.optimization_barrier((far_time, tiles_then))
    far = gather_partners(over_planes[1:], "dp", 0, part_bits)
    own_time = gather_partners(far_time, "fsdp", 1, near_bits, most=1)
    own_time = own_time.swapaxes(0, 1).reshape((-1,) + time_master.shape)
    normed = group_norm(tiles_then, head, steps, normed)
    own = jnp.concatenate([jnp.stack(mine)[:, None], far], axis=1)
    own, own_time, normed, times = lax.optimization_barrier((own, own_time, normed, timesteps[0]))
    features = time_features(jnp.pad(times, (0, LANES - number)), time_rows * shards)
    other, other_time = swap(own, "fsdp", 1), swap(own_time, "fsdp", 1)

    predicted, keep, send, keep_time, send_time = conv_both(
        counts, own, other, own_time, other_time, features, normed, tiles, targets
    )

    grad = add_up([keep, swap(send, "fsdp", 1)])
    time_grad = add_up([keep_time, swap(send_time, "fsdp", 1)])
    grad, time_grad = lax.optimization_barrier((grad, time_grad))
    grad = scatter_partners(grad, "dp", 0, part_bits)
    for bit in range(part_bits, peer_bits):
        grad = sum_partners(grad, "dp", bit, 1)
    time_grad = scatter_partners(time_grad, "fsdp", 1, plane_bits)
    grad = scatter_partners(grad, "fsdp", 1, plane_bits)
    time_grad = sum_partners(time_grad, "dp", 0, peer_bits)
    grad = gather_partners(grad, "dp", 0, part_bits)
    grad = jnp.concatenate(
        [lax.dynamic_index_in_dim(grad, part ^ q, 0, keepdims=False) for q in range(parts)]
    )
    return (
        jnp.swapaxes(predicted, 1, 2)[None],
        grad.T.astype(f32),
        time_grad.astype(f32),
    )


def solution(mesh):
    placed = (
        P("fsdp", "dp", None, None),
        P("fsdp", "dp", None, None),
        P("fsdp", None),
        P("fsdp", "dp"),
        P("fsdp", None),
        P("fsdp", None),
    )
    return jax.shard_map(
        per_device,
        mesh=mesh,
        in_specs=placed,
        out_specs=(P("fsdp", "dp", None, None), P("fsdp", None), P("fsdp", None)),
        check_vma=False,
    )
```

```python
import functools
import math

import jax
import jax.numpy as jnp
import numpy as np
from jax import lax
from jax.experimental import pallas as pl
from jax.experimental.pallas import tpu as pltpu
from jax.sharding import PartitionSpec as P

GROUPS = 32
SIDE = 16
LANES = 128

bf16 = jnp.bfloat16
f32 = jnp.float32


def tiles_per_step(number):
    return max(size for size in range(1, 6) if number % size == 0)


def norm_kernel(group_width, same_ref, tiles_ref, *refs):
    out_ref = refs[-1]
    same_group = same_ref[...]
    number, channels, pixels = tiles_ref.shape
    scale = 1.0 / (group_width * pixels)
    lane = lax.broadcasted_iota(jnp.int32, (channels, LANES), 1)

    def group_means(values):
        row_sums = jnp.zeros((channels, LANES), f32)
        for t, value in enumerate(values):
            row_sums = jnp.where(lane == t, jnp.sum(value, axis=1, keepdims=True), row_sums)
        high = row_sums.astype(bf16)
        rest = row_sums - high.astype(f32)
        middle = rest.astype(bf16)
        low = (rest - middle.astype(f32)).astype(bf16)
        return scale * sum(
            jnp.dot(same_group, term, preferred_element_type=f32) for term in (high, middle, low)
        )

    mean = group_means([tiles_ref[t].astype(f32) for t in range(number)])
    centred = [tiles_ref[t].astype(f32) - mean[:, t : t + 1] for t in range(number)]
    spread = lax.rsqrt(group_means([value * value for value in centred]) + 1e-05)
    for t in range(number):
        half = (tiles_ref[t].astype(f32) - mean[:, t : t + 1]) * (0.5 * spread[:, t : t + 1])
        out_ref[t] = (half + half * jnp.tanh(half)).astype(bf16)


def group_norm(tiles, first, last, into=None):
    number, channels, pixels = tiles.shape
    step = tiles_per_step(number)
    group_width = channels // GROUPS
    group = np.arange(channels) // group_width
    same_group = jnp.asarray(group[:, None] == group[None, :], bf16)
    block = pl.BlockSpec((step, channels, pixels), lambda i: (i + first, 0, 0))
    size = (last - first) * step * channels * pixels
    operands, specs = [same_group, tiles], [pl.BlockSpec((channels, channels), lambda i: (0, 0)), block]
    if into is not None:
        operands, specs = operands + [into], specs + [pl.BlockSpec(memory_space=pl.ANY)]
    return pl.pallas_call(
        functools.partial(norm_kernel, group_width),
        grid=(last - first,),
        in_specs=specs,
        out_specs=block,
        out_shape=jax.ShapeDtypeStruct(tiles.shape, bf16),
        input_output_aliases={} if into is None else {2: 0},
        compiler_params=pltpu.CompilerParams(vmem_limit_bytes=60 * 2**20),
        cost_estimate=pl.CostEstimate(
            flops=20 * size, bytes_accessed=4 * size, transcendentals=size
        ),
        name="group_norm",
    )(*operands)


def write_columns(values, columns_ref, at):
    channels, pixels = values.shape
    cell = lax.broadcasted_iota(jnp.int32, (channels, pixels), 1)
    column = cell % SIDE
    wide = values.astype(f32)
    for b in range(3):
        if b == 1:
            moved = wide
        else:
            moved = pltpu.roll(wide, (1 - b) % pixels, 1)
            moved = jnp.where(column == (0 if b == 0 else SIDE - 1), 0.0, moved)
        for a in range(3):
            if a == 1:
                shifted = moved
            else:
                shifted = pltpu.roll(moved, ((1 - a) * SIDE) % pixels, 1)
                outside = (cell < SIDE) if a == 0 else (cell >= pixels - SIDE)
                shifted = jnp.where(outside, 0.0, shifted)
            tap = 3 * a + b
            columns_ref[
                tap * channels : (tap + 1) * channels, at * pixels : (at + 1) * pixels
            ] = shifted.astype(values.dtype)


def conv_kernel(
    steps,
    counts_ref,
    own_ref,
    other_ref,
    own_time_ref,
    other_time_ref,
    features_ref,
    normed_ref,
    tiles_ref,
    target_ref,
    predicted_ref,
    keep_ref,
    send_ref,
    keep_time_ref,
    send_time_ref,
    weight,
    time_weight,
    bias,
    sums,
    columns,
    total,
):
    i = pl.program_id(0)
    parts, planes, part_rows, rows = own_ref.shape
    step, channels, pixels = normed_ref.shape
    shards = 2 * planes
    time_rows = own_time_ref.shape[1]
    my_shard, my_peer = lax.axis_index("fsdp"), lax.axis_index("dp")
    count = counts_ref[0, my_peer]
    core, plane, part = my_shard & 1, my_shard >> 1, my_peer & (parts - 1)
    outs = parts * part_rows
    lane = lax.broadcasted_iota(jnp.int32, (outs, LANES), 1)

    @pl.when(i == 0)
    def _():
        for f in range(shards):
            for q in range(parts):
                at = (q ^ part, (f // 2) ^ plane)
                block = jnp.where(core == f % 2, own_ref[at], other_ref[at])
                into = slice(q * part_rows, (q + 1) * part_rows)
                weight[into, f * rows : (f + 1) * rows] = block
            block = jnp.where(
                core == f % 2, own_time_ref[(f // 2) ^ plane], other_time_ref[(f // 2) ^ plane]
            )
            time_weight[f * time_rows : (f + 1) * time_rows, :] = block.astype(f32)
        bias[...] = lax.dot_general(
            time_weight[...].astype(bf16),
            features_ref[...],
            (((0,), (0,)), ((), ())),
            preferred_element_type=f32,
        )
        total[...] = jnp.zeros_like(total)
        sums[...] = jnp.zeros_like(sums)

    @pl.when(i * step < count)
    def _():
        for t in range(step):
            write_columns(normed_ref[t], columns, t)
        conv = jnp.dot(weight[...], columns[...], preferred_element_type=f32)
        errors = []
        error_sums = sums[...]
        for t in range(step):
            slot = i * step + t
            live = slot < count
            tile_bias = jnp.sum(jnp.where(lane == slot, bias[...], 0.0), axis=1, keepdims=True)
            pred32 = tiles_ref[t].astype(f32) + conv[:, t * pixels : (t + 1) * pixels] + tile_bias
            predicted_ref[t] = jnp.where(live, pred32, 0.0).astype(bf16)
            error = jnp.where(
                live, (pred32 - target_ref[t].astype(f32)) * (1.0 / pixels), 0.0
            ).astype(bf16)
            error_sum = jnp.sum(error.astype(f32), axis=1, keepdims=True)
            error_sums = jnp.where(lane == slot, error_sum, error_sums)
            errors.append(error)
        sums[...] = error_sums
        total[...] += lax.dot_general(
            jnp.concatenate(errors, axis=1),
            columns[...],
            (((1,), (1,)), ((), ())),
            preferred_element_type=f32,
        )

    @pl.when(i * step >= count)
    def _():
        predicted_ref[...] = jnp.zeros_like(predicted_ref)

    @pl.when(i == steps - 1)
    def _():
        high = sums[...].astype(bf16)
        low = (sums[...] - high.astype(f32)).astype(bf16)
        time_total = sum(
            lax.dot_general(
                features_ref[...], term, (((1,), (1,)), ((), ())), preferred_element_type=f32
            )
            for term in (high, low)
        )
        for c in range(2):
            for f in range(shards):
                into = keep_ref if f % 2 == c else send_ref
                time_into = keep_time_ref if f % 2 == c else send_time_ref

                @pl.when(core == c)
                def _():
                    at = (f // 2) ^ plane
                    for q in range(parts):
                        here = slice(q * part_rows, (q + 1) * part_rows)
                        into[q ^ part, at] = total[here, f * rows : (f + 1) * rows].astype(bf16)
                    time_into[at] = time_total[f * time_rows : (f + 1) * time_rows].astype(bf16)


def conv_both(counts, own, other, own_time, other_time, features, normed, tiles, targets):
    number, channels, pixels = normed.shape
    parts, planes, part_rows, rows = own.shape
    shards, outs = 2 * planes, parts * part_rows
    depth, emb = shards * rows, features.shape[0]
    step = tiles_per_step(number)
    steps = number // step

    def whole(shape):
        return pl.BlockSpec(shape, lambda i, c: (0,) * len(shape))

    block = pl.BlockSpec((step, channels, pixels), lambda i, c: (i, 0, 0))
    return pl.pallas_call(
        functools.partial(conv_kernel, steps),
        grid_spec=pltpu.PrefetchScalarGridSpec(
            num_scalar_prefetch=1,
            grid=(steps,),
            in_specs=[whole(own.shape)] * 2
            + [whole(own_time.shape)] * 2
            + [whole(features.shape)]
            + [block] * 3,
            out_specs=[block] + [whole(own.shape)] * 2 + [whole(own_time.shape)] * 2,
            scratch_shapes=[
                pltpu.VMEM((outs, depth), bf16),
                pltpu.VMEM((emb, outs), f32),
                pltpu.VMEM((outs, LANES), f32),
                pltpu.VMEM((outs, LANES), f32),
                pltpu.VMEM((depth, step * pixels), bf16),
                pltpu.VMEM((outs, depth), f32),
            ],
        ),
        out_shape=[
            jax.ShapeDtypeStruct(tiles.shape, bf16),
            jax.ShapeDtypeStruct(own.shape, bf16),
            jax.ShapeDtypeStruct(own.shape, bf16),
            jax.ShapeDtypeStruct(own_time.shape, bf16),
            jax.ShapeDtypeStruct(own_time.shape, bf16),
        ],
        compiler_params=pltpu.CompilerParams(vmem_limit_bytes=44 * 2**20),
        cost_estimate=pl.CostEstimate(
            flops=4 * number * pixels * depth * outs, bytes_accessed=8 * tiles.size, transcendentals=0
        ),
        name="conv_both",
    )(counts, own, other, own_time, other_time, features, normed, tiles, targets)


def swap(values, axis, mask):
    pairs = [(i, i ^ mask) for i in range(lax.axis_size(axis))]
    return lax.ppermute(values, axis, pairs)


def bits_of(axis):
    return (lax.axis_size(axis) - 1).bit_length()


def bit_groups(bits, most):
    return [(at, min(most, bits - at)) for at in range(0, bits, most)]


def gather_partners(values, axis, low, bits, most=2):
    shape = values.shape
    values = values[None]
    for at, width in reversed(bit_groups(bits, most)):
        parts = [values] + [swap(values, axis, m << (low + at)) for m in range(1, 1 << width)]
        values = jnp.stack(parts, axis=1).reshape((-1,) + shape)
    return values


def add_up(parts):
    kept_as = parts[0].dtype
    parts = [part.astype(f32) for part in parts]
    while len(parts) > 1:
        parts = [sum(parts[n : n + 2]) for n in range(0, len(parts), 2)]
    return parts[0].astype(kept_as)


def sum_partners(values, axis, low, bits, most=2):
    for at, width in bit_groups(bits, most):
        parts = [values] + [swap(values, axis, m << (low + at)) for m in range(1, 1 << width)]
        values = add_up(parts)
    return values


def scatter_partners(values, axis, low, bits, most=2):
    shape = values.shape[1:]
    for at, width in bit_groups(bits, most):
        values = values.reshape((-1, 1 << width) + shape)
        parts = [values[:, 0]]
        parts += [swap(values[:, m], axis, m << (low + at)) for m in range(1, 1 << width)]
        values = add_up(parts)
    return values.reshape(shape)


def time_features(timesteps, emb):
    half_width = emb // 2
    frequency = jnp.exp(-math.log(10000.0) * jnp.arange(half_width, dtype=f32) / half_width)
    angles = frequency[:, None] * timesteps.astype(f32)[None, :]
    return jax.nn.silu(jnp.concatenate([jnp.cos(angles), jnp.sin(angles)])).astype(bf16)


def per_device(latents, target_noise, counts, timesteps, conv_master, temb_master):
    tiles = jnp.swapaxes(latents[0], 1, 2)
    targets = jnp.swapaxes(target_noise[0], 1, 2)
    number = tiles.shape[0]
    shards = lax.axis_size("fsdp")
    shard_bits, peer_bits = bits_of("fsdp"), bits_of("dp")
    rows, outs = conv_master.shape
    time_rows = temb_master.shape[0]
    part_bits = max(n for n in range(min(peer_bits, 2) + 1) if outs % (16 << n) == 0)
    parts = 1 << part_bits
    part = lax.axis_index("dp") & (parts - 1)
    plane_bits = shard_bits - 1

    part_rows = outs // parts
    first = lax.dynamic_slice(conv_master.T, (part * part_rows, 0), (part_rows, rows))
    first, conv_master, temb_master, tiles_then = lax.optimization_barrier(
        (first.astype(bf16), conv_master, temb_master, tiles)
    )
    over_planes = gather_partners(first, "fsdp", 1, plane_bits)
    time_master = temb_master.astype(bf16)
    near_bits = plane_bits // 2
    far_time = gather_partners(time_master, "fsdp", 1 + near_bits, plane_bits - near_bits, most=1)
    master = conv_master.T.astype(bf16).reshape(parts, part_rows, rows)
    mine = [lax.dynamic_index_in_dim(master, part ^ m, 0, keepdims=False) for m in range(parts)]
    mine = jnp.stack(mine)[:, None]
    steps = number // tiles_per_step(number)
    head = steps // 3
    normed = group_norm(tiles_then, 0, head) if head else None
    over_planes, mine, normed, tiles_then = lax.optimization_barrier(
        (over_planes, mine, normed, tiles_then)
    )
    far = [over_planes[None, 1:]]
    far += [swap(far[0], "dp", m) for m in range(1, parts)]
    far_time, tiles_then = lax.optimization_barrier((far_time, tiles_then))
    own_time = gather_partners(far_time, "fsdp", 1, near_bits, most=1)
    own_time = own_time.swapaxes(0, 1).reshape((-1,) + time_master.shape)
    normed = group_norm(tiles_then, head, steps, normed)
    near = jnp.concatenate([mine[:, 0], over_planes[1:]])
    normed, near = lax.optimization_barrier((normed, near))
    other_near = swap(near, "fsdp", 1)
    own_time, times = lax.optimization_barrier((own_time, timesteps[0]))
    other_far = [other_near[None, parts:]] + [swap(block, "fsdp", 1) for block in far[1:]]
    other_mine = other_near[:parts, None]
    features = time_features(jnp.pad(times, (0, LANES - number)), time_rows * shards)
    own = jnp.concatenate([mine, jnp.concatenate(far)], axis=1)
    other = jnp.concatenate([other_mine, jnp.concatenate(other_far)], axis=1)
    other_time = swap(own_time, "fsdp", 1)

    predicted, keep, send, keep_time, send_time = conv_both(
        counts, own, other, own_time, other_time, features, normed, tiles, targets
    )

    grad = add_up([keep, swap(send, "fsdp", 1)])
    time_grad = add_up([keep_time, swap(send_time, "fsdp", 1)])
    grad, time_grad = lax.optimization_barrier((grad, time_grad))
    grad = scatter_partners(grad, "dp", 0, part_bits)
    for bit in range(part_bits, peer_bits):
        grad = sum_partners(grad, "dp", bit, 1)
    time_grad = scatter_partners(time_grad, "fsdp", 1, plane_bits)
    grad = scatter_partners(grad, "fsdp", 1, plane_bits)
    time_grad = sum_partners(time_grad, "dp", 0, peer_bits)
    grad = gather_partners(grad, "dp", 0, part_bits)
    grad = jnp.concatenate(
        [lax.dynamic_index_in_dim(grad, part ^ q, 0, keepdims=False) for q in range(parts)]
    )
    return (
        jnp.swapaxes(predicted, 1, 2)[None],
        grad.T.astype(f32),
        time_grad.astype(f32),
    )


def solution(mesh):
    placed = (
        P("fsdp", "dp", None, None),
        P("fsdp", "dp", None, None),
        P("fsdp", None),
        P("fsdp", "dp"),
        P("fsdp", None),
        P("fsdp", None),
    )
    return jax.shard_map(
        per_device,
        mesh=mesh,
        in_specs=placed,
        out_specs=(P("fsdp", "dp", None, None), P("fsdp", None), P("fsdp", None)),
        check_vma=False,
    )
```

```python
import functools
import math

import jax
import jax.numpy as jnp
import numpy as np
from jax import lax
from jax.experimental import pallas as pl
from jax.experimental.pallas import tpu as pltpu
from jax.sharding import PartitionSpec as P

GROUPS = 32
SIDE = 16
LANES = 128

bf16 = jnp.bfloat16
f32 = jnp.float32


def tiles_per_step(number):
    return max(size for size in range(1, 6) if number % size == 0)


def norm_kernel(group_width, same_ref, tiles_ref, *refs):
    out_ref = refs[-1]
    same_group = same_ref[...]
    number, channels, pixels = tiles_ref.shape
    scale = 1.0 / (group_width * pixels)
    lane = lax.broadcasted_iota(jnp.int32, (channels, LANES), 1)

    def group_means(values):
        row_sums = jnp.zeros((channels, LANES), f32)
        for t, value in enumerate(values):
            row_sums = jnp.where(lane == t, jnp.sum(value, axis=1, keepdims=True), row_sums)
        high = row_sums.astype(bf16)
        rest = row_sums - high.astype(f32)
        middle = rest.astype(bf16)
        low = (rest - middle.astype(f32)).astype(bf16)
        return scale * sum(
            jnp.dot(same_group, term, preferred_element_type=f32) for term in (high, middle, low)
        )

    mean = group_means([tiles_ref[t].astype(f32) for t in range(number)])
    centred = [tiles_ref[t].astype(f32) - mean[:, t : t + 1] for t in range(number)]
    spread = lax.rsqrt(group_means([value * value for value in centred]) + 1e-05)
    for t in range(number):
        half = (tiles_ref[t].astype(f32) - mean[:, t : t + 1]) * (0.5 * spread[:, t : t + 1])
        out_ref[t] = (half + half * jnp.tanh(half)).astype(bf16)


def group_norm(tiles, first, last, into=None):
    number, channels, pixels = tiles.shape
    step = tiles_per_step(number)
    group_width = channels // GROUPS
    group = np.arange(channels) // group_width
    same_group = jnp.asarray(group[:, None] == group[None, :], bf16)
    block = pl.BlockSpec((step, channels, pixels), lambda i: (i + first, 0, 0))
    size = (last - first) * step * channels * pixels
    operands, specs = [same_group, tiles], [pl.BlockSpec((channels, channels), lambda i: (0, 0)), block]
    if into is not None:
        operands, specs = operands + [into], specs + [pl.BlockSpec(memory_space=pl.ANY)]
    return pl.pallas_call(
        functools.partial(norm_kernel, group_width),
        grid=(last - first,),
        in_specs=specs,
        out_specs=block,
        out_shape=jax.ShapeDtypeStruct(tiles.shape, bf16),
        input_output_aliases={} if into is None else {2: 0},
        compiler_params=pltpu.CompilerParams(vmem_limit_bytes=60 * 2**20),
        cost_estimate=pl.CostEstimate(
            flops=20 * size, bytes_accessed=4 * size, transcendentals=size
        ),
        name="group_norm",
    )(*operands)


def write_columns(values, columns_ref, at):
    channels, pixels = values.shape
    cell = lax.broadcasted_iota(jnp.int32, (channels, pixels), 1)
    column = cell % SIDE
    wide = values.astype(f32)
    for b in range(3):
        if b == 1:
            moved = wide
        else:
            moved = pltpu.roll(wide, (1 - b) % pixels, 1)
            moved = jnp.where(column == (0 if b == 0 else SIDE - 1), 0.0, moved)
        for a in range(3):
            if a == 1:
                shifted = moved
            else:
                shifted = pltpu.roll(moved, ((1 - a) * SIDE) % pixels, 1)
                outside = (cell < SIDE) if a == 0 else (cell >= pixels - SIDE)
                shifted = jnp.where(outside, 0.0, shifted)
            tap = 3 * a + b
            columns_ref[
                tap * channels : (tap + 1) * channels, at * pixels : (at + 1) * pixels
            ] = shifted.astype(values.dtype)


def conv_kernel(
    steps,
    counts_ref,
    own_ref,
    other_ref,
    own_time_ref,
    other_time_ref,
    features_ref,
    normed_ref,
    tiles_ref,
    target_ref,
    predicted_ref,
    keep_ref,
    send_ref,
    keep_time_ref,
    send_time_ref,
    weight,
    time_weight,
    bias,
    sums,
    columns,
    total,
):
    i = pl.program_id(0)
    parts, planes, part_rows, rows = own_ref.shape
    step, channels, pixels = normed_ref.shape
    shards = 2 * planes
    time_rows = own_time_ref.shape[1]
    my_shard, my_peer = lax.axis_index("fsdp"), lax.axis_index("dp")
    count = counts_ref[0, my_peer]
    core, plane, part = my_shard & 1, my_shard >> 1, my_peer & (parts - 1)
    outs = parts * part_rows
    lane = lax.broadcasted_iota(jnp.int32, (outs, LANES), 1)

    @pl.when(i == 0)
    def _():
        for f in range(shards):
            for q in range(parts):
                at = (q ^ part, (f // 2) ^ plane)
                block = jnp.where(core == f % 2, own_ref[at], other_ref[at])
                into = slice(q * part_rows, (q + 1) * part_rows)
                weight[into, f * rows : (f + 1) * rows] = block
            block = jnp.where(
                core == f % 2, own_time_ref[(f // 2) ^ plane], other_time_ref[(f // 2) ^ plane]
            )
            time_weight[f * time_rows : (f + 1) * time_rows, :] = block.astype(f32)
        bias[...] = lax.dot_general(
            time_weight[...].astype(bf16),
            features_ref[...],
            (((0,), (0,)), ((), ())),
            preferred_element_type=f32,
        )
        total[...] = jnp.zeros_like(total)
        sums[...] = jnp.zeros_like(sums)

    @pl.when(i * step < count)
    def _():
        for t in range(step):
            write_columns(normed_ref[t], columns, t)
        conv = jnp.dot(weight[...], columns[...], preferred_element_type=f32)
        errors = []
        error_sums = sums[...]
        for t in range(step):
            slot = i * step + t
            live = slot < count
            tile_bias = jnp.sum(jnp.where(lane == slot, bias[...], 0.0), axis=1, keepdims=True)
            pred32 = tiles_ref[t].astype(f32) + conv[:, t * pixels : (t + 1) * pixels] + tile_bias
            predicted_ref[t] = jnp.where(live, pred32, 0.0).astype(bf16)
            error = jnp.where(
                live, (pred32 - target_ref[t].astype(f32)) * (1.0 / pixels), 0.0
            ).astype(bf16)
            error_sum = jnp.sum(error.astype(f32), axis=1, keepdims=True)
            error_sums = jnp.where(lane == slot, error_sum, error_sums)
            errors.append(error)
        sums[...] = error_sums
        total[...] += lax.dot_general(
            jnp.concatenate(errors, axis=1),
            columns[...],
            (((1,), (1,)), ((), ())),
            preferred_element_type=f32,
        )

    @pl.when(i * step >= count)
    def _():
        predicted_ref[...] = jnp.zeros_like(predicted_ref)

    @pl.when(i == steps - 1)
    def _():
        high = sums[...].astype(bf16)
        low = (sums[...] - high.astype(f32)).astype(bf16)
        time_total = sum(
            lax.dot_general(
                features_ref[...], term, (((1,), (1,)), ((), ())), preferred_element_type=f32
            )
            for term in (high, low)
        )
        for c in range(2):
            for f in range(shards):
                into = keep_ref if f % 2 == c else send_ref
                time_into = keep_time_ref if f % 2 == c else send_time_ref

                @pl.when(core == c)
                def _():
                    at = (f // 2) ^ plane
                    for q in range(parts):
                        here = slice(q * part_rows, (q + 1) * part_rows)
                        into[q ^ part, at] = total[here, f * rows : (f + 1) * rows].astype(bf16)
                    time_into[at] = time_total[f * time_rows : (f + 1) * time_rows].astype(bf16)


def conv_both(counts, own, other, own_time, other_time, features, normed, tiles, targets):
    number, channels, pixels = normed.shape
    parts, planes, part_rows, rows = own.shape
    shards, outs = 2 * planes, parts * part_rows
    depth, emb = shards * rows, features.shape[0]
    step = tiles_per_step(number)
    steps = number // step

    def whole(shape):
        return pl.BlockSpec(shape, lambda i, c: (0,) * len(shape))

    block = pl.BlockSpec((step, channels, pixels), lambda i, c: (i, 0, 0))
    return pl.pallas_call(
        functools.partial(conv_kernel, steps),
        grid_spec=pltpu.PrefetchScalarGridSpec(
            num_scalar_prefetch=1,
            grid=(steps,),
            in_specs=[whole(own.shape)] * 2
            + [whole(own_time.shape)] * 2
            + [whole(features.shape)]
            + [block] * 3,
            out_specs=[block] + [whole(own.shape)] * 2 + [whole(own_time.shape)] * 2,
            scratch_shapes=[
                pltpu.VMEM((outs, depth), bf16),
                pltpu.VMEM((emb, outs), f32),
                pltpu.VMEM((outs, LANES), f32),
                pltpu.VMEM((outs, LANES), f32),
                pltpu.VMEM((depth, step * pixels), bf16),
                pltpu.VMEM((outs, depth), f32),
            ],
        ),
        out_shape=[
            jax.ShapeDtypeStruct(tiles.shape, bf16),
            jax.ShapeDtypeStruct(own.shape, bf16),
            jax.ShapeDtypeStruct(own.shape, bf16),
            jax.ShapeDtypeStruct(own_time.shape, bf16),
            jax.ShapeDtypeStruct(own_time.shape, bf16),
        ],
        compiler_params=pltpu.CompilerParams(vmem_limit_bytes=44 * 2**20),
        cost_estimate=pl.CostEstimate(
            flops=4 * number * pixels * depth * outs, bytes_accessed=8 * tiles.size, transcendentals=0
        ),
        name="conv_both",
    )(counts, own, other, own_time, other_time, features, normed, tiles, targets)


def swap(values, axis, mask):
    pairs = [(i, i ^ mask) for i in range(lax.axis_size(axis))]
    return lax.ppermute(values, axis, pairs)


def bits_of(axis):
    return (lax.axis_size(axis) - 1).bit_length()


def bit_groups(bits, most):
    return [(at, min(most, bits - at)) for at in range(0, bits, most)]


def gather_partners(values, axis, low, bits, most=2):
    shape = values.shape
    values = values[None]
    for at, width in reversed(bit_groups(bits, most)):
        parts = [values] + [swap(values, axis, m << (low + at)) for m in range(1, 1 << width)]
        values = jnp.stack(parts, axis=1).reshape((-1,) + shape)
    return values


def add_up(parts):
    kept_as = parts[0].dtype
    parts = [part.astype(f32) for part in parts]
    while len(parts) > 1:
        parts = [sum(parts[n : n + 2]) for n in range(0, len(parts), 2)]
    return parts[0].astype(kept_as)


def sum_partners(values, axis, low, bits, most=2):
    for at, width in bit_groups(bits, most):
        parts = [values] + [swap(values, axis, m << (low + at)) for m in range(1, 1 << width)]
        values = add_up(parts)
    return values


def scatter_partners(values, axis, low, bits, most=2):
    shape = values.shape[1:]
    for at, width in bit_groups(bits, most):
        values = values.reshape((-1, 1 << width) + shape)
        parts = [values[:, 0]]
        parts += [swap(values[:, m], axis, m << (low + at)) for m in range(1, 1 << width)]
        values = add_up(parts)
    return values.reshape(shape)


def time_features(timesteps, emb):
    half_width = emb // 2
    frequency = jnp.exp(-math.log(10000.0) * jnp.arange(half_width, dtype=f32) / half_width)
    angles = timesteps.astype(f32)[:, None] * frequency[None, :]
    waves = jnp.concatenate([jnp.cos(angles), jnp.sin(angles)], axis=1)
    features = jax.nn.silu(waves).astype(bf16)
    return jnp.pad(features, ((0, LANES - features.shape[0]), (0, 0))).T


def per_device(latents, target_noise, counts, timesteps, conv_master, temb_master):
    tiles = jnp.swapaxes(latents[0], 1, 2)
    targets = jnp.swapaxes(target_noise[0], 1, 2)
    number = tiles.shape[0]
    shards = lax.axis_size("fsdp")
    shard_bits, peer_bits = bits_of("fsdp"), bits_of("dp")
    rows, outs = conv_master.shape
    time_rows = temb_master.shape[0]
    part_bits = max(n for n in range(min(peer_bits, 2) + 1) if outs % (16 << n) == 0)
    parts = 1 << part_bits
    part = lax.axis_index("dp") & (parts - 1)
    plane_bits = shard_bits - 1

    part_rows = outs // parts
    master = conv_master.T.astype(bf16).reshape(parts, part_rows, rows)
    mine = [lax.dynamic_index_in_dim(master, part ^ m, 0, keepdims=False) for m in range(parts)]
    first, temb_master, tiles_then = lax.optimization_barrier((mine[0], temb_master, tiles))
    over_planes = gather_partners(first, "fsdp", 1, plane_bits)
    time_master = temb_master.astype(bf16)
    near_bits = plane_bits // 2
    far_time = gather_partners(time_master, "fsdp", 1 + near_bits, plane_bits - near_bits, most=1)
    mine = jnp.stack(mine)[:, None]
    steps = number // tiles_per_step(number)
    head = steps // 3
    normed = group_norm(tiles_then, 0, head) if head else None
    over_planes, mine, normed, tiles_then = lax.optimization_barrier(
        (over_planes, mine, normed, tiles_then)
    )
    far = [over_planes[None, 1:]]
    far += [swap(far[0], "dp", m) for m in range(1, parts)]
    far_time, tiles_then = lax.optimization_barrier((far_time, tiles_then))
    own_time = gather_partners(far_time, "fsdp", 1, near_bits, most=1)
    own_time = own_time.swapaxes(0, 1).reshape((-1,) + time_master.shape)
    normed = group_norm(tiles_then, head, steps, normed)
    near = jnp.concatenate([mine[:, 0], over_planes[1:]])
    normed, near = lax.optimization_barrier((normed, near))
    other_near = swap(near, "fsdp", 1)
    own_time, times = lax.optimization_barrier((own_time, timesteps[0]))
    other_far = [other_near[None, parts:]] + [swap(block, "fsdp", 1) for block in far[1:]]
    other_mine = other_near[:parts, None]
    features = time_features(times, time_rows * shards)
    own = jnp.concatenate([mine, jnp.concatenate(far)], axis=1)
    other = jnp.concatenate([other_mine, jnp.concatenate(other_far)], axis=1)
    other_time = swap(own_time, "fsdp", 1)

    predicted, keep, send, keep_time, send_time = conv_both(
        counts, own, other, own_time, other_time, features, normed, tiles, targets
    )

    grad = add_up([keep, swap(send, "fsdp", 1)])
    time_grad = add_up([keep_time, swap(send_time, "fsdp", 1)])
    grad, time_grad = lax.optimization_barrier((grad, time_grad))
    grad = scatter_partners(grad, "dp", 0, part_bits)
    for bit in range(part_bits, peer_bits):
        grad = sum_partners(grad, "dp", bit, 1)
    time_grad = scatter_partners(time_grad, "fsdp", 1, plane_bits)
    grad = scatter_partners(grad, "fsdp", 1, plane_bits)
    time_grad = sum_partners(time_grad, "dp", 0, peer_bits)
    grad = gather_partners(grad, "dp", 0, part_bits)
    grad = jnp.concatenate(
        [lax.dynamic_index_in_dim(grad, part ^ q, 0, keepdims=False) for q in range(parts)]
    )
    return (
        jnp.swapaxes(predicted, 1, 2)[None],
        grad.T.astype(f32),
        time_grad.astype(f32),
    )


def solution(mesh):
    placed = (
        P("fsdp", "dp", None, None),
        P("fsdp", "dp", None, None),
        P("fsdp", None),
        P("fsdp", "dp"),
        P("fsdp", None),
        P("fsdp", None),
    )
    return jax.shard_map(
        per_device,
        mesh=mesh,
        in_specs=placed,
        out_specs=(P("fsdp", "dp", None, None), P("fsdp", None), P("fsdp", None)),
        check_vma=False,
    )
```

```python
import functools
import math

import jax
import jax.numpy as jnp
import numpy as np
from jax import lax
from jax.experimental import pallas as pl
from jax.experimental.pallas import tpu as pltpu
from jax.sharding import PartitionSpec as P

GROUPS = 32
SIDE = 16
LANES = 128

bf16 = jnp.bfloat16
f32 = jnp.float32


def tiles_per_step(number):
    return max(size for size in range(1, 6) if number % size == 0)


def norm_kernel(group_width, same_ref, tiles_ref, *refs):
    out_ref = refs[-1]
    same_group = same_ref[...]
    number, channels, pixels = tiles_ref.shape
    scale = 1.0 / (group_width * pixels)
    lane = lax.broadcasted_iota(jnp.int32, (channels, LANES), 1)

    def group_means(values):
        row_sums = jnp.zeros((channels, LANES), f32)
        for t, value in enumerate(values):
            row_sums = jnp.where(lane == t, jnp.sum(value, axis=1, keepdims=True), row_sums)
        high = row_sums.astype(bf16)
        rest = row_sums - high.astype(f32)
        middle = rest.astype(bf16)
        low = (rest - middle.astype(f32)).astype(bf16)
        return scale * sum(
            jnp.dot(same_group, term, preferred_element_type=f32) for term in (high, middle, low)
        )

    mean = group_means([tiles_ref[t].astype(f32) for t in range(number)])
    centred = [tiles_ref[t].astype(f32) - mean[:, t : t + 1] for t in range(number)]
    spread = lax.rsqrt(group_means([value * value for value in centred]) + 1e-05)
    for t in range(number):
        half = (tiles_ref[t].astype(f32) - mean[:, t : t + 1]) * (0.5 * spread[:, t : t + 1])
        out_ref[t] = (half + half * jnp.tanh(half)).astype(bf16)


def group_norm(tiles, first, last, into=None):
    number, channels, pixels = tiles.shape
    step = tiles_per_step(number)
    group_width = channels // GROUPS
    group = np.arange(channels) // group_width
    same_group = jnp.asarray(group[:, None] == group[None, :], bf16)
    block = pl.BlockSpec((step, channels, pixels), lambda i: (i + first, 0, 0))
    size = (last - first) * step * channels * pixels
    operands, specs = [same_group, tiles], [pl.BlockSpec((channels, channels), lambda i: (0, 0)), block]
    if into is not None:
        operands, specs = operands + [into], specs + [pl.BlockSpec(memory_space=pl.ANY)]
    return pl.pallas_call(
        functools.partial(norm_kernel, group_width),
        grid=(last - first,),
        in_specs=specs,
        out_specs=block,
        out_shape=jax.ShapeDtypeStruct(tiles.shape, bf16),
        input_output_aliases={} if into is None else {2: 0},
        compiler_params=pltpu.CompilerParams(vmem_limit_bytes=60 * 2**20),
        cost_estimate=pl.CostEstimate(
            flops=20 * size, bytes_accessed=4 * size, transcendentals=size
        ),
        name="group_norm",
    )(*operands)


def write_columns(values, columns_ref, at):
    channels, pixels = values.shape
    cell = lax.broadcasted_iota(jnp.int32, (channels, pixels), 1)
    column = cell % SIDE
    wide = values.astype(f32)
    for b in range(3):
        if b == 1:
            moved = wide
        else:
            moved = pltpu.roll(wide, (1 - b) % pixels, 1)
            moved = jnp.where(column == (0 if b == 0 else SIDE - 1), 0.0, moved)
        for a in range(3):
            if a == 1:
                shifted = moved
            else:
                shifted = pltpu.roll(moved, ((1 - a) * SIDE) % pixels, 1)
                outside = (cell < SIDE) if a == 0 else (cell >= pixels - SIDE)
                shifted = jnp.where(outside, 0.0, shifted)
            tap = 3 * a + b
            columns_ref[
                tap * channels : (tap + 1) * channels, at * pixels : (at + 1) * pixels
            ] = shifted.astype(values.dtype)


def conv_kernel(
    steps,
    counts_ref,
    own_ref,
    other_ref,
    own_time_ref,
    other_time_ref,
    features_ref,
    normed_ref,
    tiles_ref,
    target_ref,
    predicted_ref,
    keep_ref,
    send_ref,
    keep_time_ref,
    send_time_ref,
    weight,
    time_weight,
    bias,
    sums,
    columns,
    total,
):
    i = pl.program_id(0)
    parts, planes, part_rows, rows = own_ref.shape
    step, channels, pixels = normed_ref.shape
    shards = 2 * planes
    time_rows = own_time_ref.shape[1]
    my_shard, my_peer = lax.axis_index("fsdp"), lax.axis_index("dp")
    count = counts_ref[0, my_peer]
    core, plane, part = my_shard & 1, my_shard >> 1, my_peer & (parts - 1)
    outs = parts * part_rows
    lane = lax.broadcasted_iota(jnp.int32, (outs, LANES), 1)

    @pl.when(i == 0)
    def _():
        for f in range(shards):
            for q in range(parts):
                at = (q ^ part, (f // 2) ^ plane)
                block = jnp.where(core == f % 2, own_ref[at], other_ref[at])
                into = slice(q * part_rows, (q + 1) * part_rows)
                weight[into, f * rows : (f + 1) * rows] = block
            block = jnp.where(
                core == f % 2, own_time_ref[(f // 2) ^ plane], other_time_ref[(f // 2) ^ plane]
            )
            time_weight[f * time_rows : (f + 1) * time_rows, :] = block.astype(f32)
        bias[...] = lax.dot_general(
            time_weight[...].astype(bf16),
            features_ref[...],
            (((0,), (0,)), ((), ())),
            preferred_element_type=f32,
        )
        total[...] = jnp.zeros_like(total)
        sums[...] = jnp.zeros_like(sums)

    @pl.when(i * step < count)
    def _():
        for t in range(step):
            write_columns(normed_ref[t], columns, t)
        conv = jnp.dot(weight[...], columns[...], preferred_element_type=f32)
        errors = []
        error_sums = sums[...]
        for t in range(step):
            slot = i * step + t
            live = slot < count
            tile_bias = jnp.sum(jnp.where(lane == slot, bias[...], 0.0), axis=1, keepdims=True)
            pred32 = tiles_ref[t].astype(f32) + conv[:, t * pixels : (t + 1) * pixels] + tile_bias
            predicted_ref[t] = jnp.where(live, pred32, 0.0).astype(bf16)
            error = jnp.where(
                live, (pred32 - target_ref[t].astype(f32)) * (1.0 / pixels), 0.0
            ).astype(bf16)
            error_sum = jnp.sum(error.astype(f32), axis=1, keepdims=True)
            error_sums = jnp.where(lane == slot, error_sum, error_sums)
            errors.append(error)
        sums[...] = error_sums
        total[...] += lax.dot_general(
            jnp.concatenate(errors, axis=1),
            columns[...],
            (((1,), (1,)), ((), ())),
            preferred_element_type=f32,
        )

    @pl.when(i * step >= count)
    def _():
        predicted_ref[...] = jnp.zeros_like(predicted_ref)

    @pl.when(i == steps - 1)
    def _():
        high = sums[...].astype(bf16)
        low = (sums[...] - high.astype(f32)).astype(bf16)
        time_total = sum(
            lax.dot_general(
                features_ref[...], term, (((1,), (1,)), ((), ())), preferred_element_type=f32
            )
            for term in (high, low)
        )
        for c in range(2):
            for f in range(shards):
                into = keep_ref if f % 2 == c else send_ref
                time_into = keep_time_ref if f % 2 == c else send_time_ref

                @pl.when(core == c)
                def _():
                    at = (f // 2) ^ plane
                    for q in range(parts):
                        here = slice(q * part_rows, (q + 1) * part_rows)
                        into[q ^ part, at] = total[here, f * rows : (f + 1) * rows].astype(bf16)
                    time_into[at] = time_total[f * time_rows : (f + 1) * time_rows].astype(bf16)


def conv_both(counts, own, other, own_time, other_time, features, normed, tiles, targets):
    number, channels, pixels = normed.shape
    parts, planes, part_rows, rows = own.shape
    shards, outs = 2 * planes, parts * part_rows
    depth, emb = shards * rows, features.shape[0]
    step = tiles_per_step(number)
    steps = number // step

    resident = pl.BlockSpec(memory_space=pltpu.VMEM)
    block = pl.BlockSpec((step, channels, pixels), lambda i, c: (i, 0, 0))
    return pl.pallas_call(
        functools.partial(conv_kernel, steps),
        grid_spec=pltpu.PrefetchScalarGridSpec(
            num_scalar_prefetch=1,
            grid=(steps,),
            in_specs=[resident] * 5 + [block] * 3,
            out_specs=[block] + [resident] * 4,
            scratch_shapes=[
                pltpu.VMEM((outs, depth), bf16),
                pltpu.VMEM((emb, outs), f32),
                pltpu.VMEM((outs, LANES), f32),
                pltpu.VMEM((outs, LANES), f32),
                pltpu.VMEM((depth, step * pixels), bf16),
                pltpu.VMEM((outs, depth), f32),
            ],
        ),
        out_shape=[
            jax.ShapeDtypeStruct(tiles.shape, bf16),
            jax.ShapeDtypeStruct(own.shape, bf16),
            jax.ShapeDtypeStruct(own.shape, bf16),
            jax.ShapeDtypeStruct(own_time.shape, bf16),
            jax.ShapeDtypeStruct(own_time.shape, bf16),
        ],
        compiler_params=pltpu.CompilerParams(vmem_limit_bytes=32 * 2**20),
        cost_estimate=pl.CostEstimate(
            flops=4 * number * pixels * depth * outs, bytes_accessed=8 * tiles.size, transcendentals=0
        ),
        name="conv_both",
    )(counts, own, other, own_time, other_time, features, normed, tiles, targets)


def swap(values, axis, mask):
    pairs = [(i, i ^ mask) for i in range(lax.axis_size(axis))]
    return lax.ppermute(values, axis, pairs)


def bits_of(axis):
    return (lax.axis_size(axis) - 1).bit_length()


def bit_groups(bits, most):
    return [(at, min(most, bits - at)) for at in range(0, bits, most)]


def gather_partners(values, axis, low, bits, most=2):
    shape = values.shape
    values = values[None]
    for at, width in reversed(bit_groups(bits, most)):
        parts = [values] + [swap(values, axis, m << (low + at)) for m in range(1, 1 << width)]
        values = jnp.stack(parts, axis=1).reshape((-1,) + shape)
    return values


def add_up(parts):
    kept_as = parts[0].dtype
    parts = [part.astype(f32) for part in parts]
    while len(parts) > 1:
        parts = [sum(parts[n : n + 2]) for n in range(0, len(parts), 2)]
    return parts[0].astype(kept_as)


def sum_partners(values, axis, low, bits, most=2):
    for at, width in bit_groups(bits, most):
        parts = [values] + [swap(values, axis, m << (low + at)) for m in range(1, 1 << width)]
        values = add_up(parts)
    return values


def scatter_partners(values, axis, low, bits, most=2):
    shape = values.shape[1:]
    for at, width in bit_groups(bits, most):
        values = values.reshape((-1, 1 << width) + shape)
        parts = [values[:, 0]]
        parts += [swap(values[:, m], axis, m << (low + at)) for m in range(1, 1 << width)]
        values = add_up(parts)
    return values.reshape(shape)


def time_features(timesteps, emb):
    half_width = emb // 2
    frequency = jnp.exp(-math.log(10000.0) * jnp.arange(half_width, dtype=f32) / half_width)
    timesteps = jnp.pad(timesteps, (0, LANES - timesteps.shape[0]))
    angles = frequency[:, None] * timesteps.astype(f32)[None, :]
    return jax.nn.silu(jnp.concatenate([jnp.cos(angles), jnp.sin(angles)])).astype(bf16)


def per_device(latents, target_noise, counts, timesteps, conv_master, temb_master):
    tiles = jnp.swapaxes(latents[0], 1, 2)
    targets = jnp.swapaxes(target_noise[0], 1, 2)
    number = tiles.shape[0]
    shards = lax.axis_size("fsdp")
    shard_bits, peer_bits = bits_of("fsdp"), bits_of("dp")
    rows, outs = conv_master.shape
    time_rows = temb_master.shape[0]
    part_bits = max(n for n in range(min(peer_bits, 2) + 1) if outs % (16 << n) == 0)
    parts = 1 << part_bits
    part = lax.axis_index("dp") & (parts - 1)
    plane_bits = shard_bits - 1

    part_rows = outs // parts
    master = conv_master.T.astype(bf16).reshape(parts, part_rows, rows)
    mine = [lax.dynamic_index_in_dim(master, part ^ m, 0, keepdims=False) for m in range(parts)]
    first, temb_master, tiles_then = lax.optimization_barrier((mine[0], temb_master, tiles))
    over_planes = gather_partners(first, "fsdp", 1, plane_bits)
    time_master = temb_master.astype(bf16)
    near_bits = plane_bits // 2
    far_time = gather_partners(time_master, "fsdp", 1 + near_bits, plane_bits - near_bits, most=1)
    mine = jnp.stack(mine)[:, None]
    steps = number // tiles_per_step(number)
    head = steps // 3
    normed = group_norm(tiles_then, 0, head) if head else None
    over_planes, mine, normed, tiles_then = lax.optimization_barrier(
        (over_planes, mine, normed, tiles_then)
    )
    far = [over_planes[None, 1:]]
    far += [swap(far[0], "dp", m) for m in range(1, parts)]
    far_time, tiles_then = lax.optimization_barrier((far_time, tiles_then))
    own_time = gather_partners(far_time, "fsdp", 1, near_bits, most=1)
    own_time = own_time.swapaxes(0, 1).reshape((-1,) + time_master.shape)
    normed = group_norm(tiles_then, head, steps, normed)
    near = jnp.concatenate([mine[:, 0], over_planes[1:]])
    normed, near = lax.optimization_barrier((normed, near))
    other_near = swap(near, "fsdp", 1)
    own_time, times = lax.optimization_barrier((own_time, timesteps[0]))
    other_far = [other_near[None, parts:]] + [swap(block, "fsdp", 1) for block in far[1:]]
    other_mine = other_near[:parts, None]
    features = time_features(times, time_rows * shards)
    own = jnp.concatenate([mine, jnp.concatenate(far)], axis=1)
    other = jnp.concatenate([other_mine, jnp.concatenate(other_far)], axis=1)
    other_time = swap(own_time, "fsdp", 1)

    predicted, keep, send, keep_time, send_time = conv_both(
        counts, own, other, own_time, other_time, features, normed, tiles, targets
    )

    grad = add_up([keep, swap(send, "fsdp", 1)])
    time_grad = add_up([keep_time, swap(send_time, "fsdp", 1)])
    grad, time_grad = lax.optimization_barrier((grad, time_grad))
    grad = scatter_partners(grad, "dp", 0, part_bits)
    for bit in range(part_bits, peer_bits):
        grad = sum_partners(grad, "dp", bit, 1)
    time_grad = scatter_partners(time_grad, "fsdp", 1, plane_bits)
    grad = scatter_partners(grad, "fsdp", 1, plane_bits)
    time_grad = sum_partners(time_grad, "dp", 0, peer_bits)
    grad = gather_partners(grad, "dp", 0, part_bits)
    grad = jnp.concatenate(
        [lax.dynamic_index_in_dim(grad, part ^ q, 0, keepdims=False) for q in range(parts)]
    )
    return (
        jnp.swapaxes(predicted, 1, 2)[None],
        grad.T.astype(f32),
        time_grad.astype(f32),
    )


def solution(mesh):
    placed = (
        P("fsdp", "dp", None, None),
        P("fsdp", "dp", None, None),
        P("fsdp", None),
        P("fsdp", "dp"),
        P("fsdp", None),
        P("fsdp", None),
    )
    return jax.shard_map(
        per_device,
        mesh=mesh,
        in_specs=placed,
        out_specs=(P("fsdp", "dp", None, None), P("fsdp", None), P("fsdp", None)),
        check_vma=False,
    )
```

```python
import functools
import math

import jax
import jax.numpy as jnp
import numpy as np
from jax import lax
from jax.experimental import pallas as pl
from jax.experimental.pallas import tpu as pltpu
from jax.sharding import PartitionSpec as P

GROUPS = 32
SIDE = 16
LANES = 128

bf16 = jnp.bfloat16
f32 = jnp.float32


def tiles_per_step(number):
    return max(size for size in range(1, 6) if number % size == 0)


def norm_kernel(group_width, same_ref, tiles_ref, *refs):
    out_ref = refs[-1]
    same_group = same_ref[...]
    number, channels, pixels = tiles_ref.shape
    scale = 1.0 / (group_width * pixels)
    lane = lax.broadcasted_iota(jnp.int32, (channels, LANES), 1)

    def group_means(values):
        row_sums = jnp.zeros((channels, LANES), f32)
        for t, value in enumerate(values):
            row_sums = jnp.where(lane == t, jnp.sum(value, axis=1, keepdims=True), row_sums)
        high = row_sums.astype(bf16)
        rest = row_sums - high.astype(f32)
        middle = rest.astype(bf16)
        low = (rest - middle.astype(f32)).astype(bf16)
        return scale * sum(
            jnp.dot(same_group, term, preferred_element_type=f32) for term in (high, middle, low)
        )

    mean = group_means([tiles_ref[t].astype(f32) for t in range(number)])
    centred = [tiles_ref[t].astype(f32) - mean[:, t : t + 1] for t in range(number)]
    spread = lax.rsqrt(group_means([value * value for value in centred]) + 1e-05)
    for t in range(number):
        half = (tiles_ref[t].astype(f32) - mean[:, t : t + 1]) * (0.5 * spread[:, t : t + 1])
        out_ref[t] = (half + half * jnp.tanh(half)).astype(bf16)


def group_norm(tiles, first, last, into=None):
    number, channels, pixels = tiles.shape
    step = tiles_per_step(number)
    group_width = channels // GROUPS
    group = np.arange(channels) // group_width
    same_group = jnp.asarray(group[:, None] == group[None, :], bf16)
    block = pl.BlockSpec((step, channels, pixels), lambda i: (i + first, 0, 0))
    size = (last - first) * step * channels * pixels
    operands, specs = [same_group, tiles], [pl.BlockSpec((channels, channels), lambda i: (0, 0)), block]
    if into is not None:
        operands, specs = operands + [into], specs + [pl.BlockSpec(memory_space=pl.ANY)]
    return pl.pallas_call(
        functools.partial(norm_kernel, group_width),
        grid=(last - first,),
        in_specs=specs,
        out_specs=block,
        out_shape=jax.ShapeDtypeStruct(tiles.shape, bf16),
        input_output_aliases={} if into is None else {2: 0},
        compiler_params=pltpu.CompilerParams(vmem_limit_bytes=60 * 2**20),
        cost_estimate=pl.CostEstimate(
            flops=20 * size, bytes_accessed=4 * size, transcendentals=size
        ),
        name="group_norm",
    )(*operands)


def write_columns(values, columns_ref, at):
    channels, pixels = values.shape
    cell = lax.broadcasted_iota(jnp.int32, (channels, pixels), 1)
    column = cell % SIDE
    wide = values.astype(f32)
    for b in range(3):
        if b == 1:
            moved = wide
        else:
            moved = pltpu.roll(wide, (1 - b) % pixels, 1)
            moved = jnp.where(column == (0 if b == 0 else SIDE - 1), 0.0, moved)
        for a in range(3):
            if a == 1:
                shifted = moved
            else:
                shifted = pltpu.roll(moved, ((1 - a) * SIDE) % pixels, 1)
                outside = (cell < SIDE) if a == 0 else (cell >= pixels - SIDE)
                shifted = jnp.where(outside, 0.0, shifted)
            tap = 3 * a + b
            columns_ref[
                tap * channels : (tap + 1) * channels, at * pixels : (at + 1) * pixels
            ] = shifted.astype(values.dtype)


def conv_kernel(
    steps,
    counts_ref,
    own_ref,
    other_ref,
    own_time_ref,
    other_time_ref,
    features_ref,
    normed_ref,
    tiles_ref,
    target_ref,
    predicted_ref,
    keep_time_ref,
    send_time_ref,
    *refs,
):
    keep_refs, send_refs = refs[: len(refs) // 2 - 3], refs[len(refs) // 2 - 3 : -6]
    weight, time_weight, bias, sums, columns, total = refs[-6:]
    i = pl.program_id(0)
    parts, planes, part_rows, rows = own_ref.shape
    step, channels, pixels = normed_ref.shape
    shards = 2 * planes
    time_rows = own_time_ref.shape[1]
    my_shard, my_peer = lax.axis_index("fsdp"), lax.axis_index("dp")
    count = counts_ref[0, my_peer]
    core, plane, part = my_shard & 1, my_shard >> 1, my_peer & (parts - 1)
    outs = parts * part_rows
    lane = lax.broadcasted_iota(jnp.int32, (outs, LANES), 1)

    @pl.when(i == 0)
    def _():
        for f in range(shards):
            for q in range(parts):
                at = (q ^ part, (f // 2) ^ plane)
                block = jnp.where(core == f % 2, own_ref[at], other_ref[at])
                into = slice(q * part_rows, (q + 1) * part_rows)
                weight[into, f * rows : (f + 1) * rows] = block
            block = jnp.where(
                core == f % 2, own_time_ref[(f // 2) ^ plane], other_time_ref[(f // 2) ^ plane]
            )
            time_weight[f * time_rows : (f + 1) * time_rows, :] = block.astype(f32)
        bias[...] = lax.dot_general(
            time_weight[...].astype(bf16),
            features_ref[...],
            (((0,), (0,)), ((), ())),
            preferred_element_type=f32,
        )
        total[...] = jnp.zeros_like(total)
        sums[...] = jnp.zeros_like(sums)

    @pl.when(i * step < count)
    def _():
        for t in range(step):
            write_columns(normed_ref[t], columns, t)
        conv = jnp.dot(weight[...], columns[...], preferred_element_type=f32)
        errors = []
        error_sums = sums[...]
        for t in range(step):
            slot = i * step + t
            live = slot < count
            tile_bias = jnp.sum(jnp.where(lane == slot, bias[...], 0.0), axis=1, keepdims=True)
            pred32 = tiles_ref[t].astype(f32) + conv[:, t * pixels : (t + 1) * pixels] + tile_bias
            predicted_ref[t] = jnp.where(live, pred32, 0.0).astype(bf16)
            error = jnp.where(
                live, (pred32 - target_ref[t].astype(f32)) * (1.0 / pixels), 0.0
            ).astype(bf16)
            error_sum = jnp.sum(error.astype(f32), axis=1, keepdims=True)
            error_sums = jnp.where(lane == slot, error_sum, error_sums)
            errors.append(error)
        sums[...] = error_sums
        total[...] += lax.dot_general(
            jnp.concatenate(errors, axis=1),
            columns[...],
            (((1,), (1,)), ((), ())),
            preferred_element_type=f32,
        )

    @pl.when(i * step >= count)
    def _():
        predicted_ref[...] = jnp.zeros_like(predicted_ref)

    @pl.when(i == steps - 1)
    def _():
        high = sums[...].astype(bf16)
        low = (sums[...] - high.astype(f32)).astype(bf16)
        time_total = sum(
            lax.dot_general(
                features_ref[...], term, (((1,), (1,)), ((), ())), preferred_element_type=f32
            )
            for term in (high, low)
        )
        for c in range(2):
            for f in range(shards):
                time_into = keep_time_ref if f % 2 == c else send_time_ref

                @pl.when(core == c)
                def _():
                    at = (f // 2) ^ plane
                    for k in range(parts):
                        into = (keep_refs if f % 2 == c else send_refs)[k]
                        here = pl.ds(pl.multiple_of((k ^ part) * part_rows, part_rows), part_rows)
                        into[at] = total[here, f * rows : (f + 1) * rows].astype(bf16)
                    time_into[at] = time_total[f * time_rows : (f + 1) * time_rows].astype(bf16)


def conv_both(counts, own, other, own_time, other_time, features, normed, tiles, targets):
    number, channels, pixels = normed.shape
    parts, planes, part_rows, rows = own.shape
    shards, outs = 2 * planes, parts * part_rows
    depth, emb = shards * rows, features.shape[0]
    step = tiles_per_step(number)
    steps = number // step

    resident = pl.BlockSpec(memory_space=pltpu.VMEM)
    block = pl.BlockSpec((step, channels, pixels), lambda i, c: (i, 0, 0))
    return pl.pallas_call(
        functools.partial(conv_kernel, steps),
        grid_spec=pltpu.PrefetchScalarGridSpec(
            num_scalar_prefetch=1,
            grid=(steps,),
            in_specs=[resident] * 5 + [block] * 3,
            out_specs=[block] + [resident] * (2 + 2 * parts),
            scratch_shapes=[
                pltpu.VMEM((outs, depth), bf16),
                pltpu.VMEM((emb, outs), f32),
                pltpu.VMEM((outs, LANES), f32),
                pltpu.VMEM((outs, LANES), f32),
                pltpu.VMEM((depth, step * pixels), bf16),
                pltpu.VMEM((outs, depth), f32),
            ],
        ),
        out_shape=[
            jax.ShapeDtypeStruct(tiles.shape, bf16),
            jax.ShapeDtypeStruct(own_time.shape, bf16),
            jax.ShapeDtypeStruct(own_time.shape, bf16),
        ]
        + [jax.ShapeDtypeStruct(own.shape[1:], bf16)] * (2 * parts),
        compiler_params=pltpu.CompilerParams(vmem_limit_bytes=32 * 2**20),
        cost_estimate=pl.CostEstimate(
            flops=4 * number * pixels * depth * outs, bytes_accessed=8 * tiles.size, transcendentals=0
        ),
        name="conv_both",
    )(counts, own, other, own_time, other_time, features, normed, tiles, targets)


def swap(values, axis, mask):
    pairs = [(i, i ^ mask) for i in range(lax.axis_size(axis))]
    return lax.ppermute(values, axis, pairs)


def bits_of(axis):
    return (lax.axis_size(axis) - 1).bit_length()


def bit_groups(bits, most):
    return [(at, min(most, bits - at)) for at in range(0, bits, most)]


def gather_partners(values, axis, low, bits, most=2):
    shape = values.shape
    values = values[None]
    for at, width in reversed(bit_groups(bits, most)):
        parts = [values] + [swap(values, axis, m << (low + at)) for m in range(1, 1 << width)]
        values = jnp.stack(parts, axis=1).reshape((-1,) + shape)
    return values


def add_up(parts):
    kept_as = parts[0].dtype
    parts = [part.astype(f32) for part in parts]
    while len(parts) > 1:
        parts = [sum(parts[n : n + 2]) for n in range(0, len(parts), 2)]
    return parts[0].astype(kept_as)


def sum_partners(values, axis, low, bits, most=2):
    for at, width in bit_groups(bits, most):
        parts = [values] + [swap(values, axis, m << (low + at)) for m in range(1, 1 << width)]
        values = add_up(parts)
    return values


def scatter_partners(values, axis, low, bits, most=2):
    shape = values.shape[1:]
    for at, width in bit_groups(bits, most):
        values = values.reshape((-1, 1 << width) + shape)
        parts = [values[:, 0]]
        parts += [swap(values[:, m], axis, m << (low + at)) for m in range(1, 1 << width)]
        values = add_up(parts)
    return values.reshape(shape)


def time_features(timesteps, emb):
    half_width = emb // 2
    frequency = jnp.exp(-math.log(10000.0) * jnp.arange(half_width, dtype=f32) / half_width)
    timesteps = jnp.pad(timesteps, (0, LANES - timesteps.shape[0]))
    angles = frequency[:, None] * timesteps.astype(f32)[None, :]
    return jax.nn.silu(jnp.concatenate([jnp.cos(angles), jnp.sin(angles)])).astype(bf16)


def per_device(latents, target_noise, counts, timesteps, conv_master, temb_master):
    tiles = jnp.swapaxes(latents[0], 1, 2)
    targets = jnp.swapaxes(target_noise[0], 1, 2)
    number = tiles.shape[0]
    shards = lax.axis_size("fsdp")
    shard_bits, peer_bits = bits_of("fsdp"), bits_of("dp")
    rows, outs = conv_master.shape
    time_rows = temb_master.shape[0]
    part_bits = max(n for n in range(min(peer_bits, 2) + 1) if outs % (16 << n) == 0)
    parts = 1 << part_bits
    part = lax.axis_index("dp") & (parts - 1)
    plane_bits = shard_bits - 1

    part_rows = outs // parts
    master = conv_master.T.astype(bf16).reshape(parts, part_rows, rows)
    mine = [lax.dynamic_index_in_dim(master, part ^ m, 0, keepdims=False) for m in range(parts)]
    first, temb_master, tiles_then = lax.optimization_barrier((mine[0], temb_master, tiles))
    over_planes = gather_partners(first, "fsdp", 1, plane_bits)
    time_master = temb_master.astype(bf16)
    near_bits = plane_bits // 2
    far_time = gather_partners(time_master, "fsdp", 1 + near_bits, plane_bits - near_bits, most=1)
    mine = jnp.stack(mine)[:, None]
    steps = number // tiles_per_step(number)
    head = steps // 3
    normed = group_norm(tiles_then, 0, head) if head else None
    over_planes, mine, normed, tiles_then = lax.optimization_barrier(
        (over_planes, mine, normed, tiles_then)
    )
    far = [over_planes[None, 1:]]
    far += [swap(far[0], "dp", m) for m in range(1, parts)]
    far_time, tiles_then = lax.optimization_barrier((far_time, tiles_then))
    own_time = gather_partners(far_time, "fsdp", 1, near_bits, most=1)
    own_time = own_time.swapaxes(0, 1).reshape((-1,) + time_master.shape)
    normed = group_norm(tiles_then, head, steps, normed)
    near = jnp.concatenate([mine[:, 0], over_planes[1:]])
    normed, near = lax.optimization_barrier((normed, near))
    other_near = swap(near, "fsdp", 1)
    own_time, times = lax.optimization_barrier((own_time, timesteps[0]))
    other_far = [other_near[None, parts:]] + [swap(block, "fsdp", 1) for block in far[1:]]
    other_mine = other_near[:parts, None]
    features = time_features(times, time_rows * shards)
    own = jnp.concatenate([mine, jnp.concatenate(far)], axis=1)
    other = jnp.concatenate([other_mine, jnp.concatenate(other_far)], axis=1)
    other_time = swap(own_time, "fsdp", 1)

    predicted, keep_time, send_time, *blocks = conv_both(
        counts, own, other, own_time, other_time, features, normed, tiles, targets
    )

    keep, send = blocks[:parts], blocks[parts:]
    blocks = [swap(send[k], "fsdp", 1) for k in [*range(1, parts), 0]]
    blocks = [add_up([keep[k], blocks[k - 1]]) for k in range(parts)]
    time_grad = add_up([keep_time, swap(send_time, "fsdp", 1)])
    blocks[-1], time_grad = lax.optimization_barrier((blocks[-1], time_grad))
    grad = add_up(blocks[:1] + [swap(blocks[k], "dp", k) for k in range(1, parts)])
    for bit in range(part_bits, peer_bits):
        grad = sum_partners(grad, "dp", bit, 1)
    time_grad = scatter_partners(time_grad, "fsdp", 1, plane_bits)
    grad = scatter_partners(grad, "fsdp", 1, plane_bits)
    time_grad = sum_partners(time_grad, "dp", 0, peer_bits)
    grad = gather_partners(grad, "dp", 0, part_bits)
    grad = jnp.concatenate(
        [lax.dynamic_index_in_dim(grad, part ^ q, 0, keepdims=False) for q in range(parts)]
    )
    return (
        jnp.swapaxes(predicted, 1, 2)[None],
        grad.T.astype(f32),
        time_grad.astype(f32),
    )


def solution(mesh):
    placed = (
        P("fsdp", "dp", None, None),
        P("fsdp", "dp", None, None),
        P("fsdp", None),
        P("fsdp", "dp"),
        P("fsdp", None),
        P("fsdp", None),
    )
    return jax.shard_map(
        per_device,
        mesh=mesh,
        in_specs=placed,
        out_specs=(P("fsdp", "dp", None, None), P("fsdp", None), P("fsdp", None)),
        check_vma=False,
    )
```

```python
import functools
import math

import jax
import jax.numpy as jnp
import numpy as np
from jax import lax
from jax.experimental import pallas as pl
from jax.experimental.pallas import tpu as pltpu
from jax.sharding import PartitionSpec as P

GROUPS = 32
SIDE = 16
LANES = 128

bf16 = jnp.bfloat16
f32 = jnp.float32


def tiles_per_step(number):
    return max(size for size in range(1, 6) if number % size == 0)


def norm_kernel(group_width, same_ref, tiles_ref, *refs):
    out_ref = refs[-1]
    same_group = same_ref[...]
    number, channels, pixels = tiles_ref.shape
    scale = 1.0 / (group_width * pixels)
    lane = lax.broadcasted_iota(jnp.int32, (channels, LANES), 1)

    def group_means(values):
        row_sums = jnp.zeros((channels, LANES), f32)
        for t, value in enumerate(values):
            row_sums = jnp.where(lane == t, jnp.sum(value, axis=1, keepdims=True), row_sums)
        high = row_sums.astype(bf16)
        rest = row_sums - high.astype(f32)
        middle = rest.astype(bf16)
        low = (rest - middle.astype(f32)).astype(bf16)
        return scale * sum(
            jnp.dot(same_group, term, preferred_element_type=f32) for term in (high, middle, low)
        )

    mean = group_means([tiles_ref[t].astype(f32) for t in range(number)])
    centred = [tiles_ref[t].astype(f32) - mean[:, t : t + 1] for t in range(number)]
    spread = lax.rsqrt(group_means([value * value for value in centred]) + 1e-05)
    for t in range(number):
        half = (tiles_ref[t].astype(f32) - mean[:, t : t + 1]) * (0.5 * spread[:, t : t + 1])
        out_ref[t] = (half + half * jnp.tanh(half)).astype(bf16)


def group_norm(tiles, first, last, into=None):
    number, channels, pixels = tiles.shape
    step = tiles_per_step(number)
    group_width = channels // GROUPS
    group = np.arange(channels) // group_width
    same_group = jnp.asarray(group[:, None] == group[None, :], bf16)
    block = pl.BlockSpec((step, channels, pixels), lambda i: (i + first, 0, 0))
    size = (last - first) * step * channels * pixels
    operands, specs = [same_group, tiles], [pl.BlockSpec((channels, channels), lambda i: (0, 0)), block]
    if into is not None:
        operands, specs = operands + [into], specs + [pl.BlockSpec(memory_space=pl.ANY)]
    return pl.pallas_call(
        functools.partial(norm_kernel, group_width),
        grid=(last - first,),
        in_specs=specs,
        out_specs=block,
        out_shape=jax.ShapeDtypeStruct(tiles.shape, bf16),
        input_output_aliases={} if into is None else {2: 0},
        compiler_params=pltpu.CompilerParams(vmem_limit_bytes=24 * 2**20),
        cost_estimate=pl.CostEstimate(
            flops=20 * size, bytes_accessed=4 * size, transcendentals=size
        ),
        name="group_norm",
    )(*operands)


def write_columns(values, columns_ref, at):
    channels, pixels = values.shape
    cell = lax.broadcasted_iota(jnp.int32, (channels, pixels), 1)
    column = cell % SIDE
    wide = values.astype(f32)
    for b in range(3):
        if b == 1:
            moved = wide
        else:
            moved = pltpu.roll(wide, (1 - b) % pixels, 1)
            moved = jnp.where(column == (0 if b == 0 else SIDE - 1), 0.0, moved)
        for a in range(3):
            if a == 1:
                shifted = moved
            else:
                shifted = pltpu.roll(moved, ((1 - a) * SIDE) % pixels, 1)
                outside = (cell < SIDE) if a == 0 else (cell >= pixels - SIDE)
                shifted = jnp.where(outside, 0.0, shifted)
            tap = 3 * a + b
            columns_ref[
                tap * channels : (tap + 1) * channels, at * pixels : (at + 1) * pixels
            ] = shifted.astype(values.dtype)


def conv_kernel(
    steps,
    counts_ref,
    own_ref,
    other_ref,
    own_time_ref,
    other_time_ref,
    features_ref,
    normed_ref,
    tiles_ref,
    target_ref,
    predicted_ref,
    keep_time_ref,
    send_time_ref,
    *refs,
):
    keep_refs, send_refs = refs[: len(refs) // 2 - 3], refs[len(refs) // 2 - 3 : -6]
    weight, time_weight, bias, sums, columns, total = refs[-6:]
    i = pl.program_id(0)
    parts, planes, part_rows, rows = own_ref.shape
    step, channels, pixels = normed_ref.shape
    shards = 2 * planes
    time_rows = own_time_ref.shape[1]
    my_shard, my_peer = lax.axis_index("fsdp"), lax.axis_index("dp")
    count = counts_ref[0, my_peer]
    core, plane, part = my_shard & 1, my_shard >> 1, my_peer & (parts - 1)
    outs = parts * part_rows
    lane = lax.broadcasted_iota(jnp.int32, (outs, LANES), 1)

    @pl.when(i == 0)
    def _():
        for f in range(shards):
            for q in range(parts):
                at = (q ^ part, (f // 2) ^ plane)
                block = jnp.where(core == f % 2, own_ref[at], other_ref[at])
                into = slice(q * part_rows, (q + 1) * part_rows)
                weight[into, f * rows : (f + 1) * rows] = block
            block = jnp.where(
                core == f % 2, own_time_ref[(f // 2) ^ plane], other_time_ref[(f // 2) ^ plane]
            )
            time_weight[f * time_rows : (f + 1) * time_rows, :] = block.astype(f32)
        bias[...] = lax.dot_general(
            time_weight[...].astype(bf16),
            features_ref[...],
            (((0,), (0,)), ((), ())),
            preferred_element_type=f32,
        )
        total[...] = jnp.zeros_like(total)
        sums[...] = jnp.zeros_like(sums)

    @pl.when(i * step < count)
    def _():
        for t in range(step):
            write_columns(normed_ref[t], columns, t)
        conv = jnp.dot(weight[...], columns[...], preferred_element_type=f32)
        errors = []
        error_sums = sums[...]
        for t in range(step):
            slot = i * step + t
            live = slot < count
            tile_bias = jnp.sum(jnp.where(lane == slot, bias[...], 0.0), axis=1, keepdims=True)
            pred32 = tiles_ref[t].astype(f32) + conv[:, t * pixels : (t + 1) * pixels] + tile_bias
            predicted_ref[t] = jnp.where(live, pred32, 0.0).astype(bf16)
            error = jnp.where(
                live, (pred32 - target_ref[t].astype(f32)) * (1.0 / pixels), 0.0
            ).astype(bf16)
            error_sum = jnp.sum(error.astype(f32), axis=1, keepdims=True)
            error_sums = jnp.where(lane == slot, error_sum, error_sums)
            errors.append(error)
        sums[...] = error_sums
        total[...] += lax.dot_general(
            jnp.concatenate(errors, axis=1),
            columns[...],
            (((1,), (1,)), ((), ())),
            preferred_element_type=f32,
        )

    @pl.when(i * step >= count)
    def _():
        predicted_ref[...] = jnp.zeros_like(predicted_ref)

    @pl.when(i == steps - 1)
    def _():
        high = sums[...].astype(bf16)
        low = (sums[...] - high.astype(f32)).astype(bf16)
        time_total = sum(
            lax.dot_general(
                features_ref[...], term, (((1,), (1,)), ((), ())), preferred_element_type=f32
            )
            for term in (high, low)
        )
        for c in range(2):
            for f in range(shards):
                time_into = keep_time_ref if f % 2 == c else send_time_ref

                @pl.when(core == c)
                def _():
                    at = (f // 2) ^ plane
                    for k in range(parts):
                        into = (keep_refs if f % 2 == c else send_refs)[k]
                        here = pl.ds(pl.multiple_of((k ^ part) * part_rows, part_rows), part_rows)
                        into[at] = total[here, f * rows : (f + 1) * rows].astype(bf16)
                    time_into[at] = time_total[f * time_rows : (f + 1) * time_rows].astype(bf16)


def conv_both(counts, own, other, own_time, other_time, features, normed, tiles, targets):
    number, channels, pixels = normed.shape
    parts, planes, part_rows, rows = own.shape
    shards, outs = 2 * planes, parts * part_rows
    depth, emb = shards * rows, features.shape[0]
    step = tiles_per_step(number)
    steps = number // step

    resident = pl.BlockSpec(memory_space=pltpu.VMEM)
    block = pl.BlockSpec((step, channels, pixels), lambda i, c: (i, 0, 0))
    return pl.pallas_call(
        functools.partial(conv_kernel, steps),
        grid_spec=pltpu.PrefetchScalarGridSpec(
            num_scalar_prefetch=1,
            grid=(steps,),
            in_specs=[resident] * 5 + [block] * 3,
            out_specs=[block] + [resident] * (2 + 2 * parts),
            scratch_shapes=[
                pltpu.VMEM((outs, depth), bf16),
                pltpu.VMEM((emb, outs), f32),
                pltpu.VMEM((outs, LANES), f32),
                pltpu.VMEM((outs, LANES), f32),
                pltpu.VMEM((depth, step * pixels), bf16),
                pltpu.VMEM((outs, depth), f32),
            ],
        ),
        out_shape=[
            jax.ShapeDtypeStruct(tiles.shape, bf16),
            jax.ShapeDtypeStruct(own_time.shape, bf16),
            jax.ShapeDtypeStruct(own_time.shape, bf16),
        ]
        + [jax.ShapeDtypeStruct(own.shape[1:], bf16)] * (2 * parts),
        compiler_params=pltpu.CompilerParams(vmem_limit_bytes=32 * 2**20),
        cost_estimate=pl.CostEstimate(
            flops=4 * number * pixels * depth * outs, bytes_accessed=8 * tiles.size, transcendentals=0
        ),
        name="conv_both",
    )(counts, own, other, own_time, other_time, features, normed, tiles, targets)


def swap(values, axis, mask):
    pairs = [(i, i ^ mask) for i in range(lax.axis_size(axis))]
    return lax.ppermute(values, axis, pairs)


def bits_of(axis):
    return (lax.axis_size(axis) - 1).bit_length()


def bit_groups(bits, most):
    return [(at, min(most, bits - at)) for at in range(0, bits, most)]


def gather_partners(values, axis, low, bits, most=2):
    shape = values.shape
    values = values[None]
    for at, width in reversed(bit_groups(bits, most)):
        parts = [values] + [swap(values, axis, m << (low + at)) for m in range(1, 1 << width)]
        values = jnp.stack(parts, axis=1).reshape((-1,) + shape)
    return values


def add_up(parts):
    kept_as = parts[0].dtype
    parts = [part.astype(f32) for part in parts]
    while len(parts) > 1:
        parts = [sum(parts[n : n + 2]) for n in range(0, len(parts), 2)]
    return parts[0].astype(kept_as)


def sum_partners(values, axis, low, bits, most=2):
    for at, width in bit_groups(bits, most):
        parts = [values] + [swap(values, axis, m << (low + at)) for m in range(1, 1 << width)]
        values = add_up(parts)
    return values


def scatter_partners(values, axis, low, bits, most=2):
    shape = values.shape[1:]
    for at, width in bit_groups(bits, most):
        values = values.reshape((-1, 1 << width) + shape)
        parts = [values[:, 0]]
        parts += [swap(values[:, m], axis, m << (low + at)) for m in range(1, 1 << width)]
        values = add_up(parts)
    return values.reshape(shape)


def time_features(timesteps, emb):
    half_width = emb // 2
    frequency = jnp.exp(-math.log(10000.0) * jnp.arange(half_width, dtype=f32) / half_width)
    timesteps = jnp.pad(timesteps, (0, LANES - timesteps.shape[0]))
    angles = frequency[:, None] * timesteps.astype(f32)[None, :]
    return jax.nn.silu(jnp.concatenate([jnp.cos(angles), jnp.sin(angles)])).astype(bf16)


def per_device(latents, target_noise, counts, timesteps, conv_master, temb_master):
    tiles = jnp.swapaxes(latents[0], 1, 2)
    targets = jnp.swapaxes(target_noise[0], 1, 2)
    number = tiles.shape[0]
    shards = lax.axis_size("fsdp")
    shard_bits, peer_bits = bits_of("fsdp"), bits_of("dp")
    rows, outs = conv_master.shape
    time_rows = temb_master.shape[0]
    part_bits = max(n for n in range(min(peer_bits, 2) + 1) if outs % (16 << n) == 0)
    parts = 1 << part_bits
    part = lax.axis_index("dp") & (parts - 1)
    plane_bits = shard_bits - 1

    part_rows = outs // parts
    master = conv_master.T.astype(bf16).reshape(parts, part_rows, rows)
    mine = [lax.dynamic_index_in_dim(master, part ^ m, 0, keepdims=False) for m in range(parts)]
    first, temb_master, tiles_then = lax.optimization_barrier((mine[0], temb_master, tiles))
    over_planes = gather_partners(first, "fsdp", 1, plane_bits)
    time_master = temb_master.astype(bf16)
    near_bits = plane_bits // 2
    far_time = gather_partners(time_master, "fsdp", 1 + near_bits, plane_bits - near_bits, most=1)
    mine = jnp.stack(mine)[:, None]
    steps = number // tiles_per_step(number)
    head = steps // 3
    normed = group_norm(tiles_then, 0, head) if head else None
    over_planes, mine, normed, tiles_then = lax.optimization_barrier(
        (over_planes, mine, normed, tiles_then)
    )
    far = [over_planes[None, 1:]]
    far += [swap(far[0], "dp", m) for m in range(1, parts)]
    far_time, tiles_then = lax.optimization_barrier((far_time, tiles_then))
    own_time = gather_partners(far_time, "fsdp", 1, near_bits, most=1)
    own_time = own_time.swapaxes(0, 1).reshape((-1,) + time_master.shape)
    normed = group_norm(tiles_then, head, steps, normed)
    near = jnp.concatenate([mine[:, 0], over_planes[1:]])
    normed, near = lax.optimization_barrier((normed, near))
    other_near = swap(near, "fsdp", 1)
    own_time, times = lax.optimization_barrier((own_time, timesteps[0]))
    other_far = [other_near[None, parts:]] + [swap(block, "fsdp", 1) for block in far[1:]]
    other_mine = other_near[:parts, None]
    features = time_features(times, time_rows * shards)
    own = jnp.concatenate([mine, jnp.concatenate(far)], axis=1)
    other = jnp.concatenate([other_mine, jnp.concatenate(other_far)], axis=1)
    other_time = swap(own_time, "fsdp", 1)

    predicted, keep_time, send_time, *blocks = conv_both(
        counts, own, other, own_time, other_time, features, normed, tiles, targets
    )

    keep, send = blocks[:parts], blocks[parts:]
    blocks = [swap(send[k], "fsdp", 1) for k in [*range(1, parts), 0]]
    blocks = [add_up([keep[k], blocks[k - 1]]) for k in range(parts)]
    time_grad = add_up([keep_time, swap(send_time, "fsdp", 1)])
    blocks[-1], time_grad = lax.optimization_barrier((blocks[-1], time_grad))
    grad = add_up(blocks[:1] + [swap(blocks[k], "dp", k) for k in range(1, parts)])
    for bit in range(part_bits, peer_bits):
        grad = sum_partners(grad, "dp", bit, 1)
    time_grad = scatter_partners(time_grad, "fsdp", 1, plane_bits)
    grad = scatter_partners(grad, "fsdp", 1, plane_bits)
    time_grad = sum_partners(time_grad, "dp", 0, peer_bits)
    grad = gather_partners(grad, "dp", 0, part_bits)
    grad = jnp.concatenate(
        [lax.dynamic_index_in_dim(grad, part ^ q, 0, keepdims=False) for q in range(parts)]
    )
    return (
        jnp.swapaxes(predicted, 1, 2)[None],
        grad.T.astype(f32),
        time_grad.astype(f32),
    )


def solution(mesh):
    placed = (
        P("fsdp", "dp", None, None),
        P("fsdp", "dp", None, None),
        P("fsdp", None),
        P("fsdp", "dp"),
        P("fsdp", None),
        P("fsdp", None),
    )
    return jax.shard_map(
        per_device,
        mesh=mesh,
        in_specs=placed,
        out_specs=(P("fsdp", "dp", None, None), P("fsdp", None), P("fsdp", None)),
        check_vma=False,
    )
```

```python
import functools
import math

import jax
import jax.numpy as jnp
from jax import lax
from jax.experimental import pallas as pl
from jax.experimental.pallas import tpu as pltpu
from jax.sharding import PartitionSpec as P

GROUPS = 32
SIDE = 16
LANES = 128

bf16 = jnp.bfloat16
f32 = jnp.float32


def tiles_per_step(number):
    return max(size for size in range(1, 6) if number % size == 0)


def norm_kernel(group_width, tiles_ref, *refs):
    out_ref = refs[-1]
    number, channels, pixels = tiles_ref.shape

    def group_of(shape, axis):
        channel = lax.broadcasted_iota(jnp.int32, shape, axis).astype(f32)
        return jnp.floor((channel + 0.5) * (1.0 / group_width))

    same_group = (group_of((channels, channels), 0) == group_of((channels, channels), 1)).astype(bf16)
    scale = 1.0 / (group_width * pixels)
    lane = lax.broadcasted_iota(jnp.int32, (channels, LANES), 1)

    def group_means(values):
        row_sums = jnp.zeros((channels, LANES), f32)
        for t, value in enumerate(values):
            row_sums = jnp.where(lane == t, jnp.sum(value, axis=1, keepdims=True), row_sums)
        high = row_sums.astype(bf16)
        rest = row_sums - high.astype(f32)
        middle = rest.astype(bf16)
        low = (rest - middle.astype(f32)).astype(bf16)
        return scale * sum(
            jnp.dot(same_group, term, preferred_element_type=f32) for term in (high, middle, low)
        )

    mean = group_means([tiles_ref[t].astype(f32) for t in range(number)])
    centred = [tiles_ref[t].astype(f32) - mean[:, t : t + 1] for t in range(number)]
    spread = lax.rsqrt(group_means([value * value for value in centred]) + 1e-05)
    for t in range(number):
        half = (tiles_ref[t].astype(f32) - mean[:, t : t + 1]) * (0.5 * spread[:, t : t + 1])
        out_ref[t] = (half + half * jnp.tanh(half)).astype(bf16)


def group_norm(tiles, first, last, into=None):
    number, channels, pixels = tiles.shape
    step = tiles_per_step(number)
    group_width = channels // GROUPS
    block = pl.BlockSpec((step, channels, pixels), lambda i: (i + first, 0, 0))
    size = (last - first) * step * channels * pixels
    operands, specs = [tiles], [block]
    if into is not None:
        operands, specs = operands + [into], specs + [pl.BlockSpec(memory_space=pl.ANY)]
    return pl.pallas_call(
        functools.partial(norm_kernel, group_width),
        grid=(last - first,),
        in_specs=specs,
        out_specs=block,
        out_shape=jax.ShapeDtypeStruct(tiles.shape, bf16),
        input_output_aliases={} if into is None else {1: 0},
        compiler_params=pltpu.CompilerParams(vmem_limit_bytes=24 * 2**20),
        cost_estimate=pl.CostEstimate(
            flops=20 * size, bytes_accessed=4 * size, transcendentals=size
        ),
        name="group_norm",
    )(*operands)


def write_columns(values, columns_ref, at):
    channels, pixels = values.shape
    cell = lax.broadcasted_iota(jnp.int32, (channels, pixels), 1)
    column = cell % SIDE
    wide = values.astype(f32)
    for b in range(3):
        if b == 1:
            moved = wide
        else:
            moved = pltpu.roll(wide, (1 - b) % pixels, 1)
            moved = jnp.where(column == (0 if b == 0 else SIDE - 1), 0.0, moved)
        for a in range(3):
            if a == 1:
                shifted = moved
            else:
                shifted = pltpu.roll(moved, ((1 - a) * SIDE) % pixels, 1)
                outside = (cell < SIDE) if a == 0 else (cell >= pixels - SIDE)
                shifted = jnp.where(outside, 0.0, shifted)
            tap = 3 * a + b
            columns_ref[
                tap * channels : (tap + 1) * channels, at * pixels : (at + 1) * pixels
            ] = shifted.astype(values.dtype)


def conv_kernel(
    steps,
    counts_ref,
    own_ref,
    other_ref,
    own_time_ref,
    other_time_ref,
    features_ref,
    normed_ref,
    tiles_ref,
    target_ref,
    predicted_ref,
    keep_time_ref,
    send_time_ref,
    *refs,
):
    keep_refs, send_refs = refs[: len(refs) // 2 - 3], refs[len(refs) // 2 - 3 : -6]
    weight, time_weight, bias, sums, columns, total = refs[-6:]
    i = pl.program_id(0)
    parts, planes, part_rows, rows = own_ref.shape
    step, channels, pixels = normed_ref.shape
    shards = 2 * planes
    time_rows = own_time_ref.shape[1]
    my_shard, my_peer = lax.axis_index("fsdp"), lax.axis_index("dp")
    count = counts_ref[0, my_peer]
    core, plane, part = my_shard & 1, my_shard >> 1, my_peer & (parts - 1)
    outs = parts * part_rows
    lane = lax.broadcasted_iota(jnp.int32, (outs, LANES), 1)

    @pl.when(i == 0)
    def _():
        for f in range(shards):
            for q in range(parts):
                at = (q ^ part, (f // 2) ^ plane)
                block = jnp.where(core == f % 2, own_ref[at], other_ref[at])
                into = slice(q * part_rows, (q + 1) * part_rows)
                weight[into, f * rows : (f + 1) * rows] = block
            block = jnp.where(
                core == f % 2, own_time_ref[(f // 2) ^ plane], other_time_ref[(f // 2) ^ plane]
            )
            time_weight[f * time_rows : (f + 1) * time_rows, :] = block.astype(f32)
        bias[...] = lax.dot_general(
            time_weight[...].astype(bf16),
            features_ref[...],
            (((0,), (0,)), ((), ())),
            preferred_element_type=f32,
        )
        total[...] = jnp.zeros_like(total)
        sums[...] = jnp.zeros_like(sums)

    @pl.when(i * step < count)
    def _():
        for t in range(step):
            write_columns(normed_ref[t], columns, t)
        conv = jnp.dot(weight[...], columns[...], preferred_element_type=f32)
        errors = []
        error_sums = sums[...]
        for t in range(step):
            slot = i * step + t
            live = slot < count
            tile_bias = jnp.sum(jnp.where(lane == slot, bias[...], 0.0), axis=1, keepdims=True)
            pred32 = tiles_ref[t].astype(f32) + conv[:, t * pixels : (t + 1) * pixels] + tile_bias
            predicted_ref[t] = jnp.where(live, pred32, 0.0).astype(bf16)
            error = jnp.where(
                live, (pred32 - target_ref[t].astype(f32)) * (1.0 / pixels), 0.0
            ).astype(bf16)
            error_sum = jnp.sum(error.astype(f32), axis=1, keepdims=True)
            error_sums = jnp.where(lane == slot, error_sum, error_sums)
            errors.append(error)
        sums[...] = error_sums
        total[...] += lax.dot_general(
            jnp.concatenate(errors, axis=1),
            columns[...],
            (((1,), (1,)), ((), ())),
            preferred_element_type=f32,
        )

    @pl.when(i * step >= count)
    def _():
        predicted_ref[...] = jnp.zeros_like(predicted_ref)

    @pl.when(i == steps - 1)
    def _():
        high = sums[...].astype(bf16)
        low = (sums[...] - high.astype(f32)).astype(bf16)
        time_total = sum(
            lax.dot_general(
                features_ref[...], term, (((1,), (1,)), ((), ())), preferred_element_type=f32
            )
            for term in (high, low)
        )
        for c in range(2):
            for f in range(shards):
                time_into = keep_time_ref if f % 2 == c else send_time_ref

                @pl.when(core == c)
                def _():
                    at = (f // 2) ^ plane
                    for k in range(parts):
                        into = (keep_refs if f % 2 == c else send_refs)[k]
                        here = pl.ds(pl.multiple_of((k ^ part) * part_rows, part_rows), part_rows)
                        into[at] = total[here, f * rows : (f + 1) * rows].astype(bf16)
                    time_into[at] = time_total[f * time_rows : (f + 1) * time_rows].astype(bf16)


def conv_both(counts, own, other, own_time, other_time, features, normed, tiles, targets):
    number, channels, pixels = normed.shape
    parts, planes, part_rows, rows = own.shape
    shards, outs = 2 * planes, parts * part_rows
    depth, emb = shards * rows, features.shape[0]
    step = tiles_per_step(number)
    steps = number // step

    resident = pl.BlockSpec(memory_space=pltpu.VMEM)
    block = pl.BlockSpec((step, channels, pixels), lambda i, c: (i, 0, 0))
    return pl.pallas_call(
        functools.partial(conv_kernel, steps),
        grid_spec=pltpu.PrefetchScalarGridSpec(
            num_scalar_prefetch=1,
            grid=(steps,),
            in_specs=[resident] * 5 + [block] * 3,
            out_specs=[block] + [resident] * (2 + 2 * parts),
            scratch_shapes=[
                pltpu.VMEM((outs, depth), bf16),
                pltpu.VMEM((emb, outs), f32),
                pltpu.VMEM((outs, LANES), f32),
                pltpu.VMEM((outs, LANES), f32),
                pltpu.VMEM((depth, step * pixels), bf16),
                pltpu.VMEM((outs, depth), f32),
            ],
        ),
        out_shape=[
            jax.ShapeDtypeStruct(tiles.shape, bf16),
            jax.ShapeDtypeStruct(own_time.shape, bf16),
            jax.ShapeDtypeStruct(own_time.shape, bf16),
        ]
        + [jax.ShapeDtypeStruct(own.shape[1:], bf16)] * (2 * parts),
        compiler_params=pltpu.CompilerParams(vmem_limit_bytes=32 * 2**20),
        cost_estimate=pl.CostEstimate(
            flops=4 * number * pixels * depth * outs, bytes_accessed=8 * tiles.size, transcendentals=0
        ),
        name="conv_both",
    )(counts, own, other, own_time, other_time, features, normed, tiles, targets)


def swap(values, axis, mask):
    pairs = [(i, i ^ mask) for i in range(lax.axis_size(axis))]
    return lax.ppermute(values, axis, pairs)


def bits_of(axis):
    return (lax.axis_size(axis) - 1).bit_length()


def bit_groups(bits, most):
    return [(at, min(most, bits - at)) for at in range(0, bits, most)]


def gather_partners(values, axis, low, bits, most=2):
    shape = values.shape
    values = values[None]
    for at, width in reversed(bit_groups(bits, most)):
        parts = [values] + [swap(values, axis, m << (low + at)) for m in range(1, 1 << width)]
        values = jnp.stack(parts, axis=1).reshape((-1,) + shape)
    return values


def add_up(parts):
    kept_as = parts[0].dtype
    parts = [part.astype(f32) for part in parts]
    while len(parts) > 1:
        parts = [sum(parts[n : n + 2]) for n in range(0, len(parts), 2)]
    return parts[0].astype(kept_as)


def sum_partners(values, axis, low, bits, most=2):
    for at, width in bit_groups(bits, most):
        parts = [values] + [swap(values, axis, m << (low + at)) for m in range(1, 1 << width)]
        values = add_up(parts)
    return values


def scatter_partners(values, axis, low, bits, most=2):
    shape = values.shape[1:]
    for at, width in bit_groups(bits, most):
        values = values.reshape((-1, 1 << width) + shape)
        parts = [values[:, 0]]
        parts += [swap(values[:, m], axis, m << (low + at)) for m in range(1, 1 << width)]
        values = add_up(parts)
    return values.reshape(shape)


def time_features(timesteps, emb):
    half_width = emb // 2
    frequency = jnp.exp(-math.log(10000.0) * jnp.arange(half_width, dtype=f32) / half_width)
    timesteps = jnp.pad(timesteps, (0, LANES - timesteps.shape[0]))
    angles = frequency[:, None] * timesteps.astype(f32)[None, :]
    return jax.nn.silu(jnp.concatenate([jnp.cos(angles), jnp.sin(angles)])).astype(bf16)


def per_device(latents, target_noise, counts, timesteps, conv_master, temb_master):
    tiles = jnp.swapaxes(latents[0], 1, 2)
    targets = jnp.swapaxes(target_noise[0], 1, 2)
    number = tiles.shape[0]
    shards = lax.axis_size("fsdp")
    shard_bits, peer_bits = bits_of("fsdp"), bits_of("dp")
    rows, outs = conv_master.shape
    time_rows = temb_master.shape[0]
    part_bits = max(n for n in range(min(peer_bits, 2) + 1) if outs % (16 << n) == 0)
    parts = 1 << part_bits
    part = lax.axis_index("dp") & (parts - 1)
    plane_bits = shard_bits - 1

    part_rows = outs // parts
    master = conv_master.T.astype(bf16).reshape(parts, part_rows, rows)
    mine = [lax.dynamic_index_in_dim(master, part ^ m, 0, keepdims=False) for m in range(parts)]
    first, temb_master, tiles_then = lax.optimization_barrier((mine[0], temb_master, tiles))
    over_planes = gather_partners(first, "fsdp", 1, plane_bits)
    time_master = temb_master.astype(bf16)
    near_bits = plane_bits // 2
    far_time = gather_partners(time_master, "fsdp", 1 + near_bits, plane_bits - near_bits, most=1)
    mine = jnp.stack(mine)[:, None]
    steps = number // tiles_per_step(number)
    head = steps // 3
    normed = group_norm(tiles_then, 0, head) if head else None
    over_planes, mine, normed, tiles_then = lax.optimization_barrier(
        (over_planes, mine, normed, tiles_then)
    )
    far = [over_planes[None, 1:]]
    far += [swap(far[0], "dp", m) for m in range(1, parts)]
    far_time, tiles_then = lax.optimization_barrier((far_time, tiles_then))
    own_time = gather_partners(far_time, "fsdp", 1, near_bits, most=1)
    own_time = own_time.swapaxes(0, 1).reshape((-1,) + time_master.shape)
    normed = group_norm(tiles_then, head, steps, normed)
    near = jnp.concatenate([mine[:, 0], over_planes[1:]])
    normed, near = lax.optimization_barrier((normed, near))
    other_near = swap(near, "fsdp", 1)
    own_time, times = lax.optimization_barrier((own_time, timesteps[0]))
    other_far = [other_near[None, parts:]] + [swap(block, "fsdp", 1) for block in far[1:]]
    other_mine = other_near[:parts, None]
    features = time_features(times, time_rows * shards)
    own = jnp.concatenate([mine, jnp.concatenate(far)], axis=1)
    other = jnp.concatenate([other_mine, jnp.concatenate(other_far)], axis=1)
    other_time = swap(own_time, "fsdp", 1)

    predicted, keep_time, send_time, *blocks = conv_both(
        counts, own, other, own_time, other_time, features, normed, tiles, targets
    )

    keep, send = blocks[:parts], blocks[parts:]
    blocks = [swap(send[k], "fsdp", 1) for k in [*range(1, parts), 0]]
    blocks = [add_up([keep[k], blocks[k - 1]]) for k in range(parts)]
    time_grad = add_up([keep_time, swap(send_time, "fsdp", 1)])
    blocks[-1], time_grad = lax.optimization_barrier((blocks[-1], time_grad))
    grad = add_up(blocks[:1] + [swap(blocks[k], "dp", k) for k in range(1, parts)])
    for bit in range(part_bits, peer_bits):
        grad = sum_partners(grad, "dp", bit, 1)
    time_grad = scatter_partners(time_grad, "fsdp", 1, plane_bits)
    grad = scatter_partners(grad, "fsdp", 1, plane_bits)
    time_grad = sum_partners(time_grad, "dp", 0, peer_bits)
    grad = gather_partners(grad, "dp", 0, part_bits)
    grad = jnp.concatenate(
        [lax.dynamic_index_in_dim(grad, part ^ q, 0, keepdims=False) for q in range(parts)]
    )
    return (
        jnp.swapaxes(predicted, 1, 2)[None],
        grad.T.astype(f32),
        time_grad.astype(f32),
    )


def solution(mesh):
    placed = (
        P("fsdp", "dp", None, None),
        P("fsdp", "dp", None, None),
        P("fsdp", None),
        P("fsdp", "dp"),
        P("fsdp", None),
        P("fsdp", None),
    )
    return jax.shard_map(
        per_device,
        mesh=mesh,
        in_specs=placed,
        out_specs=(P("fsdp", "dp", None, None), P("fsdp", None), P("fsdp", None)),
        check_vma=False,
    )
```
